32 devices in a mesh: groups: 2 (over y), pool: 4 (over z), heads: 2 (over x), sub: 2 (over core).
Axes of the slice: x: 2, y: 2, z: 4, core: 2. Of those that a mesh axis runs over, the one named last changes fastest.
Arguments:
- queries: bfloat16 [16, 128, 8192], P(('groups', 'pool'), None, ('heads', 'sub')), parts along dimension 0, may hold values from -6 to 6
- latent_store: bfloat16 [32768, 512], P(('groups', 'pool')), parts along dimension 0, may hold values from -6 to 6
- kv_up: bfloat16 [512, 8, 2, 128], P(None, ('heads', 'sub')), may hold values from -0.25 to 0.25
- q_gain: float32 [128], replicated, may hold values from 0.1 to 1.9
- k_gain: float32 [128], replicated, may hold values from 0.1 to 1.9
- out_weight: bfloat16 [8192, 8192], P(('heads', 'sub'), 'pool'), may hold values from -0.5 to 0.5
- place_holder: int32 [16, 8], P('groups'), parts along dimension 0, may hold values from 0 to 3, as said below
- place_block: int32 [16, 8], P('groups'), parts along dimension 0, may hold values from 0 to 31, as said below
- image_count: int32 [16], P('groups'), parts along dimension 0, may hold values from 1 to 1024, 5120 in all
- serving_request: int32 [16], P('groups'), parts along dimension 0, may hold values from 0 to 7, as said below
Outputs:
- update: bfloat16 [2048, 8192], P(('groups', 'pool', 'heads', 'sub')), parts along dimension 0
The draws below stay inside these ranges and needn't reach their ends.
There are 2 independent parts, one for each index of `groups`. The reference program is written for one: setup_inputs(seed, part) draws one part's arguments, and reference() takes and returns one part's arrays. A program takes and returns all parts, laid end to end along the dimension named above; an argument that names none is the same for every part. Nothing has to cross between parts.
Inputs may be any that keep to these rules, and one draw needn't show every extreme that they name: `place_holder`: the 16 blocks of the requests of the 2 slots at one pool index lie on one holder at most 8 times, and some holder takes exactly 8 of them; one holder of each part stores exactly 32 blocks. `place_block`: no two blocks on one holder share a block slot. `serving_request`: each request is served in exactly one slot; slot k stands at pool index k // 2. The first image_count[r] image token slots of request r are live; the others are left out of its softmax.
All inputs are finite; a program needn't handle non-finite values.
Results may differ from the reference program's by a relative error of at most 0.0072.
Values may be sent and summed in bfloat16 or wider, within the bound.
No kernel may reach another device: no remote copies, remote signals or barrier semaphores. Data moves between devices by JAX's collectives and lax.ppermute only.
A program may use at most 128 MiB of HBM per device.

```python
import math
import jax
import jax.numpy as jnp
import numpy as np
from jax import lax

D = 8192
H = 64
KVH = 8
HD = 128
RANK = 512
TEXT = 128
REQ_DEV = 2
NB = 8
BLK = 128
IMG_MAX = 1024
REQUESTS = 8
CAP = 8
STORE_DEV = 32
N_POOL = 4


def placement_tables(key):
    items = REQ_DEV * NB
    entries = N_POOL * items
    keys = jax.random.split(key, 5)
    hottest = jax.random.randint(keys[0], (), 0, N_POOL)
    other_keys = jax.random.split(keys[1], N_POOL)
    others = jax.vmap(lambda one: jax.random.permutation(one, N_POOL - 1))(other_keys)
    others = others + (others >= hottest).astype(jnp.int32)
    order_index = jnp.arange(items, dtype=jnp.int32)
    cycled = jnp.maximum(order_index - CAP, 0) % (N_POOL - 1)
    assigned = jnp.where(order_index[None, :] < CAP, hottest, others[:, cycled])
    shuffle_keys = jax.random.split(keys[2], N_POOL)
    shuffles = jax.vmap(lambda one: jax.random.permutation(one, items))(shuffle_keys)
    inverse = jnp.argsort(shuffles, axis=1)
    holder_item = jnp.take_along_axis(assigned, inverse, axis=1).reshape(entries)
    tiebreak = jax.random.permutation(keys[3], entries)
    ordering = jnp.argsort(holder_item * entries + tiebreak)
    position = jnp.argsort(ordering).astype(jnp.int32)
    per_holder = jnp.sum((holder_item[:, None] == jnp.arange(N_POOL)[None, :]).astype(jnp.int32), axis=0)
    first_slot = jnp.cumsum(per_holder) - per_holder
    block_item = position - first_slot[holder_item]
    serving = jax.random.permutation(keys[4], REQUESTS).astype(jnp.int32)
    slot_of_request = jnp.argsort(serving)
    holder_request = holder_item.reshape(REQUESTS, NB)[slot_of_request]
    block_request = block_item.reshape(REQUESTS, NB)[slot_of_request]
    return (holder_request.astype(jnp.int32), block_request.astype(jnp.int32), serving)


def draw_place_holder(key, part):
    return placement_tables(key)[0]


def draw_place_block(key, part):
    return placement_tables(key)[1]


def draw_serving_request(key, part):
    return placement_tables(key)[2]


def level_of(stream_key, dims, cuts, smallest, top_value):
    loudness = 1.0
    for dim, shards_of in cuts:
        steps = jax.random.uniform(jax.random.fold_in(jax.random.fold_in(stream_key, 6), dim), (shards_of,), jnp.float32, smallest / len(cuts), top_value / len(cuts))
        loudness = loudness * jnp.repeat(jnp.exp(steps), dims[dim] // shards_of).reshape((-1,) + (1,) * (len(dims) - 1 - dim))
    return loudness


def profile(count, total, reach, slope):
    loads = [(1 << 20) // math.isqrt(standing ** slope) + 1 for standing in range(2, count + 1)]
    rest, given = total - reach - (count - 1), [1] * (count - 1)
    while rest > 0:
        candidates = [i for i in range(count - 1) if given[i] < reach]
        mass, budget = sum([loads[i] for i in candidates]), rest
        for i in candidates:
            extra = min(reach - given[i], max(1, budget * loads[i] // mass), rest)
            given[i] = given[i] + extra
            rest = rest - extra
    return np.array([reach] + given)


def ragged_sizes(own_key, number_of, total, most, slope):
    if number_of == 2:
        one = jax.random.randint(own_key, (), max(1, total - most), min(most, total - 1) + 1)
        return jnp.stack([one, total - one])
    tallies = jnp.asarray(profile(number_of, total, most, slope), jnp.int32)
    twos = (number_of - 1) // 2
    giver, receiver = tallies[1:1 + 2 * twos:2], tallies[2:2 + 2 * twos:2]
    margin = jnp.minimum(giver - 1, most - receiver)
    moved = jax.random.randint(jax.random.fold_in(own_key, 1), (twos,), 0, 1 << 20) % (margin + 1)
    tallies = tallies.at[1:1 + 2 * twos:2].set(giver - moved).at[2:2 + 2 * twos:2].set(receiver + moved)
    return tallies[jax.random.permutation(jax.random.fold_in(own_key, 2), number_of)]


def scatter_about(stream_key, dims, width, limit, cuts=(), kind=jnp.bfloat16):
    level = level_of(stream_key, dims, cuts, -0.22, 0.18) if cuts else 1.0
    values = jax.random.normal(stream_key, dims, jnp.float32) * width * level
    return jnp.minimum(jnp.maximum(values, -limit), limit).astype(kind)


def setup_inputs(seed: int = 0, part: int = 0) -> dict:
    key_of = jax.random.split(jax.random.key(seed), 11)
    own_keys = jax.random.split(jax.random.fold_in(key_of[10], part), 11)
    queries = scatter_about(own_keys[0], (REQUESTS, TEXT, H * HD), 1.0, 6.0, ((0, 4), (2, 4)))
    latent_store = scatter_about(own_keys[1], (N_POOL * STORE_DEV * BLK, RANK), 1.0, 6.0, ((0, 4),))
    kv_up = scatter_about(key_of[2], (RANK, KVH, 2, HD), RANK ** -0.5, 0.25, ((1, 4),))
    q_gain = jnp.clip(1.0 + 0.18 * jax.random.normal(key_of[3], (HD,), jnp.float32), 0.1, 1.9)
    k_gain = jnp.clip(1.0 + 0.18 * jax.random.normal(key_of[4], (HD,), jnp.float32), 0.1, 1.9)
    out_weight = scatter_about(key_of[5], (H * HD, D), HD ** -0.5, 0.5, ((0, 4), (1, 4)))
    place_holder = draw_place_holder(jax.random.fold_in(jax.random.fold_in(key_of[10], part), 71), part)
    place_block = draw_place_block(jax.random.fold_in(jax.random.fold_in(key_of[10], part), 71), part)
    image_count = ragged_sizes(own_keys[8], REQUESTS, REQUESTS * IMG_MAX * 5 // 8, IMG_MAX, 2).astype(jnp.int32)
    serving_request = draw_serving_request(jax.random.fold_in(jax.random.fold_in(key_of[10], part), 71), part)
    return {"queries": queries, "latent_store": latent_store, "kv_up": kv_up, "q_gain": q_gain, "k_gain": k_gain, "out_weight": out_weight, "place_holder": place_holder, "place_block": place_block, "image_count": image_count, "serving_request": serving_request}


def rms_scale(values, gain):
    return values * lax.rsqrt(lax.optimization_barrier(jnp.mean(values * values, axis=-1, keepdims=True)) + 1e-05) * gain

def reference(queries, latent_store, kv_up, q_gain, k_gain, out_weight, place_holder, place_block, image_count, serving_request):
    per_group = H // KVH
    softmax_scale = 1.0 / math.sqrt(HD)
    up_matrix = kv_up.reshape(RANK, KVH * 2 * HD)
    offsets = jnp.arange(BLK, dtype=jnp.int32)
    positions = jnp.arange(NB * BLK, dtype=jnp.int32)

    def one_slot(inputs):
        query_rows, request = inputs
        holders = place_holder[request].astype(jnp.int32)
        blocks = place_block[request].astype(jnp.int32)
        starts = (holders * STORE_DEV + blocks) * BLK
        indices = (starts[:, None] + offsets[None, :]).reshape(-1).astype(jnp.int32)
        latents = latent_store[indices]
        projected = jnp.dot(latents, up_matrix, preferred_element_type=jnp.float32).reshape(NB * BLK, KVH, 2, HD)
        keys = rms_scale(projected[:, :, 0], k_gain).astype(jnp.bfloat16)
        values = projected[:, :, 1].astype(jnp.bfloat16)
        shaped = query_rows.astype(jnp.float32).reshape(TEXT, KVH, per_group, HD)
        normed = rms_scale(shaped, q_gain).astype(jnp.bfloat16)
        scores = jnp.einsum('tgqd,sgd->gqts', normed.astype(jnp.float32), keys.astype(jnp.float32)) * softmax_scale
        live = positions < image_count[request]
        expo = jnp.where(live, jnp.exp(scores), jnp.zeros((), scores.dtype))
        probs = (expo / lax.optimization_barrier(jnp.sum(expo, axis=-1, keepdims=True))).astype(jnp.bfloat16)
        attended = jnp.einsum('gqts,sgd->tgqd', probs.astype(jnp.float32), values.astype(jnp.float32))
        return attended.astype(jnp.bfloat16).reshape(TEXT, H * HD)
    attended = lax.map(one_slot, (queries, serving_request))
    flat = attended.reshape(REQUESTS * TEXT, H * HD)
    return jnp.dot(flat, out_weight, preferred_element_type=jnp.float32).astype(jnp.bfloat16)
```

```python
import math

import jax
import jax.numpy as jnp
from jax import lax
from jax.sharding import PartitionSpec as P

BLK = 128
CHUNKS = 2


def rms_scale(values, gain):
    return values * lax.rsqrt(jnp.mean(values * values, axis=-1, keepdims=True) + 1e-05) * gain


def pair_rank(holders):
    count = holders.shape[1]
    same = holders[:, :, None] == holders[:, None, :]
    earlier = jnp.arange(count)[None, :] < jnp.arange(count)[:, None]
    return jnp.sum((same & earlier[None]).astype(jnp.int32), axis=2)


def shift(values, axis, step):
    size = lax.axis_size(axis)
    return lax.ppermute(values, axis, [(i, (i + step) % size) for i in range(size)])


def exchange_sum(pieces, axis):
    size = lax.axis_size(axis)
    index = lax.axis_index(axis)
    total = lax.dynamic_index_in_dim(pieces, index, 0, keepdims=False)
    for step in range(1, size):
        away = lax.dynamic_index_in_dim(pieces, (index + step) % size, 0, keepdims=False)
        total = total + shift(away.astype(jnp.bfloat16), axis, step).astype(jnp.float32)
    return total


def fetch_latents(latent_store, place_holder, place_block, serving_request, items):
    pool_size = lax.axis_size("pool")
    pool_index = lax.axis_index("pool")
    share_count = lax.axis_size(("heads", "sub"))
    share = lax.axis_index(("heads", "sub"))
    capacity = 2 * ((items + pool_size - 1) // pool_size)
    total_requests = serving_request.shape[0]
    request_ids = jnp.arange(total_requests, dtype=jnp.int32)
    selector = (serving_request[:, None] == request_ids[None, :]).astype(jnp.int32)
    holders = jnp.dot(selector, place_holder).reshape(pool_size, items)
    blocks = jnp.dot(selector, place_block).reshape(pool_size, items)
    ranks = pair_rank(holders)
    slot_ids = jnp.arange(capacity, dtype=jnp.int32)
    matched = (holders[:, None, :] == pool_index) & (ranks[:, None, :] == slot_ids[None, :, None])
    send_block = jnp.sum(jnp.where(matched, blocks[:, None, :], 0), axis=2)
    rows = BLK // share_count
    rank_width = latent_store.shape[1]
    store = latent_store.reshape(-1, rows, rank_width)
    outgoing = jnp.take(store, send_block.reshape(-1) * share_count + share, axis=0)
    incoming = lax.all_to_all(
        outgoing.reshape(pool_size, capacity * rows, rank_width),
        "pool",
        split_axis=0,
        concat_axis=0,
        tiled=True,
    )
    my_holders = lax.dynamic_index_in_dim(holders, pool_index, 0, keepdims=False)
    my_ranks = lax.dynamic_index_in_dim(ranks, pool_index, 0, keepdims=False)
    chosen = jnp.take(
        incoming.reshape(pool_size * capacity, rows, rank_width),
        my_holders * capacity + my_ranks,
        axis=0,
    )
    return selector, chosen


def per_device(
    queries,
    latent_store,
    kv_up,
    q_gain,
    k_gain,
    out_weight,
    place_holder,
    place_block,
    image_count,
    serving_request,
):
    pool_size = lax.axis_size("pool")
    pool_index = lax.axis_index("pool")
    heads_size = lax.axis_size("heads")
    sub_size = lax.axis_size("sub")
    share_count = heads_size * sub_size
    requests_here, text_rows, query_width = queries.shape
    blocks_each = place_holder.shape[1]
    items = requests_here * blocks_each
    heads_here, head_width = kv_up.shape[1], kv_up.shape[3]
    per_group = query_width // (heads_here * head_width)
    selector, chosen = fetch_latents(
        latent_store, place_holder, place_block, serving_request, items
    )
    rank_width = chosen.shape[2]
    share_rows = chosen.shape[1]
    image_slots = blocks_each * BLK
    latents = lax.all_gather(
        chosen.reshape(requests_here, blocks_each * share_rows, rank_width),
        ("heads", "sub"),
        axis=1,
        tiled=True,
    )
    projected = jnp.einsum("rsk,kgcd->rsgcd", latents, kv_up, preferred_element_type=jnp.float32)
    keys = rms_scale(projected[:, :, :, 0], k_gain).astype(jnp.bfloat16)
    values = projected[:, :, :, 1].astype(jnp.bfloat16)
    slots = jnp.arange(image_slots, dtype=jnp.int32)
    share_of, within = slots // (blocks_each * share_rows), slots % (blocks_each * share_rows)
    positions = (within // share_rows) * BLK + share_of * share_rows + within % share_rows
    count_here = lax.dynamic_slice_in_dim(
        jnp.dot(selector, image_count), pool_index * requests_here, requests_here
    )
    live = positions[None, :] < count_here[:, None]
    softmax_scale = 1.0 / math.sqrt(head_width)
    segment = requests_here * text_rows // share_count
    part_rows = segment // CHUNKS
    shaped = queries.reshape(
        requests_here,
        share_count // requests_here,
        CHUNKS,
        part_rows,
        heads_here,
        per_group,
        head_width,
    )
    outputs = []
    for chunk in range(CHUNKS):
        part = shaped[:, :, chunk].reshape(requests_here, -1, heads_here, per_group, head_width)
        normed = rms_scale(part.astype(jnp.float32), q_gain).astype(jnp.bfloat16)
        scores = (
            jnp.einsum("rtgqd,rsgd->rgqts", normed, keys, preferred_element_type=jnp.float32)
            * softmax_scale
        )
        expo = jnp.where(live[:, None, None, None, :], jnp.exp(scores), jnp.zeros((), jnp.float32))
        probs = (expo / jnp.sum(expo, axis=-1, keepdims=True)).astype(jnp.bfloat16)
        attended = jnp.einsum(
            "rgqts,rsgd->rtgqd", probs, values, preferred_element_type=jnp.float32
        )
        attended = attended.astype(jnp.bfloat16).reshape(share_count * part_rows, query_width)
        rows = lax.all_gather(attended, "pool", axis=0, tiled=True)
        partial = jnp.dot(rows, out_weight, preferred_element_type=jnp.float32)
        columns = partial.shape[1]
        partial = partial.reshape(pool_size, heads_size, sub_size, part_rows, columns)
        by_sub = exchange_sum(jnp.moveaxis(partial, 2, 0), "sub")
        by_heads = exchange_sum(jnp.moveaxis(by_sub, 1, 0), "heads")
        mine = by_heads.astype(jnp.bfloat16)
        arrived = lax.all_to_all(mine, "pool", split_axis=0, concat_axis=0, tiled=True)
        outputs.append(jnp.moveaxis(arrived, 0, 1).reshape(part_rows, pool_size * columns))
    return jnp.concatenate(outputs, axis=0)


def solution(mesh):
    in_specs = (
        P(("groups", "pool"), None, ("heads", "sub")),
        P(("groups", "pool"), None),
        P(None, ("heads", "sub"), None, None),
        P(),
        P(),
        P(("heads", "sub"), "pool"),
        P("groups", None),
        P("groups", None),
        P("groups"),
        P("groups"),
    )
    out_specs = P(("groups", "pool", "heads", "sub"), None)
    return jax.shard_map(
        per_device, mesh=mesh, in_specs=in_specs, out_specs=out_specs, check_vma=False
    )
```

```python
import math

import jax
import jax.numpy as jnp
from jax import lax
from jax.sharding import PartitionSpec as P

BLK = 128
CHUNKS = 2


def rms_scale(values, gain):
    return values * lax.rsqrt(jnp.mean(values * values, axis=-1, keepdims=True) + 1e-05) * gain


def pair_rank(holders):
    count = holders.shape[1]
    same = holders[:, :, None] == holders[:, None, :]
    earlier = jnp.arange(count)[None, :] < jnp.arange(count)[:, None]
    return jnp.sum((same & earlier[None]).astype(jnp.int32), axis=2)


def swap(values, axis, flip):
    return lax.ppermute(values, axis, [(i, i ^ flip) for i in range(lax.axis_size(axis))])


def spread_over_pool(block):
    index = lax.axis_index("pool")
    at_end = (index == 0) | (index == 3)
    across = swap(block, "pool", 3)
    beside = swap(block, "pool", 1)
    passed = jnp.where(at_end, block, across)
    second = lax.ppermute(passed, "pool", [(0, 2), (3, 1), (1, 0), (2, 3)])
    return [block, beside, second, across]


def reduce_shares(partial):
    axes = ("heads", "sub")
    share = lax.axis_index(axes)
    total = lax.dynamic_index_in_dim(partial, share, 0, keepdims=False)
    for flip in range(1, lax.axis_size(axes)):
        away = lax.dynamic_index_in_dim(partial, share ^ flip, 0, keepdims=False)
        total = total + swap(away.astype(jnp.bfloat16), axes, flip).astype(jnp.float32)
    return total.astype(jnp.bfloat16)


def fetch_latents(latent_store, place_holder, place_block, serving_request, items):
    pool_size = lax.axis_size("pool")
    pool_index = lax.axis_index("pool")
    share_count = lax.axis_size(("heads", "sub"))
    share = lax.axis_index(("heads", "sub"))
    capacity = 2 * ((items + pool_size - 1) // pool_size)
    total_requests = serving_request.shape[0]
    request_ids = jnp.arange(total_requests, dtype=jnp.int32)
    selector = (serving_request[:, None] == request_ids[None, :]).astype(jnp.int32)
    holders = jnp.dot(selector, place_holder).reshape(pool_size, items)
    blocks = jnp.dot(selector, place_block).reshape(pool_size, items)
    ranks = pair_rank(holders)
    slot_ids = jnp.arange(capacity, dtype=jnp.int32)
    matched = (holders[:, None, :] == pool_index) & (ranks[:, None, :] == slot_ids[None, :, None])
    send_block = jnp.sum(jnp.where(matched, blocks[:, None, :], 0), axis=2)
    rows = BLK // share_count
    store = latent_store.reshape(-1, rows, latent_store.shape[1])
    pieces = []
    for flip in range(pool_size):
        wanted = lax.dynamic_index_in_dim(send_block, pool_index ^ flip, 0, keepdims=False)
        piece = store.at[wanted * share_count + share].get(mode="promise_in_bounds")
        pieces.append(piece if flip == 0 else swap(piece, "pool", flip))
    my_holders = lax.dynamic_index_in_dim(holders, pool_index, 0, keepdims=False)
    my_ranks = lax.dynamic_index_in_dim(ranks, pool_index, 0, keepdims=False)
    chosen = jnp.concatenate(pieces, axis=0).at[(my_holders ^ pool_index) * capacity + my_ranks]
    return selector, chosen.get(mode="promise_in_bounds")


def per_device(
    queries,
    latent_store,
    kv_up,
    q_gain,
    k_gain,
    out_weight,
    place_holder,
    place_block,
    image_count,
    serving_request,
):
    pool_size = lax.axis_size("pool")
    pool_index = lax.axis_index("pool")
    heads_size = lax.axis_size("heads")
    sub_size = lax.axis_size("sub")
    share_count = heads_size * sub_size
    share = lax.axis_index(("heads", "sub"))
    requests_here, text_rows, query_width = queries.shape
    blocks_each = place_holder.shape[1]
    items = requests_here * blocks_each
    heads_here, head_width = kv_up.shape[1], kv_up.shape[3]
    per_group = query_width // (heads_here * head_width)
    selector, chosen = fetch_latents(
        latent_store, place_holder, place_block, serving_request, items
    )
    rank_width = chosen.shape[2]
    share_rows = chosen.shape[1]
    image_slots = blocks_each * BLK
    chosen = chosen.reshape(requests_here, blocks_each * share_rows, rank_width)
    over_heads = [chosen] + [swap(chosen, "heads", flip) for flip in range(1, heads_size)]
    quarters = []
    for part in over_heads:
        quarters += [part] + [swap(part, "sub", flip) for flip in range(1, sub_size)]
    latents = jnp.concatenate(quarters, axis=1)
    projected = jnp.einsum("rsk,kgcd->rsgcd", latents, kv_up, preferred_element_type=jnp.float32)
    keys = rms_scale(projected[:, :, :, 0], k_gain).astype(jnp.bfloat16)
    values = projected[:, :, :, 1].astype(jnp.bfloat16)
    slots = jnp.arange(image_slots, dtype=jnp.int32)
    share_of, within = slots // (blocks_each * share_rows), slots % (blocks_each * share_rows)
    positions = (
        (within // share_rows) * BLK + (share_of ^ share) * share_rows + within % share_rows
    )
    count_here = lax.dynamic_slice_in_dim(
        jnp.dot(selector, image_count), pool_index * requests_here, requests_here
    )
    live = positions[None, :] < count_here[:, None]
    softmax_scale = 1.0 / math.sqrt(head_width)
    part_rows = requests_here * text_rows // share_count // CHUNKS
    columns = out_weight.shape[1]
    shaped = queries.reshape(
        requests_here,
        share_count // requests_here,
        CHUNKS,
        part_rows,
        heads_here,
        per_group,
        head_width,
    )
    output = jnp.zeros((CHUNKS * part_rows, pool_size * columns), jnp.bfloat16)
    for chunk in range(CHUNKS):
        part = shaped[:, :, chunk].reshape(requests_here, -1, heads_here, per_group, head_width)
        normed = rms_scale(part.astype(jnp.float32), q_gain).astype(jnp.bfloat16)
        scores = (
            jnp.einsum("rtgqd,rsgd->rgqts", normed, keys, preferred_element_type=jnp.float32)
            * softmax_scale
        )
        expo = jnp.where(live[:, None, None, None, :], jnp.exp(scores), jnp.zeros((), jnp.float32))
        probs = (expo / jnp.sum(expo, axis=-1, keepdims=True)).astype(jnp.bfloat16)
        attended = jnp.einsum(
            "rgqts,rsgd->rtgqd", probs, values, preferred_element_type=jnp.float32
        )
        attended = attended.astype(jnp.bfloat16).reshape(share_count * part_rows, query_width)
        if pool_size != 4:
            rows = lax.all_gather(attended, "pool", axis=0, tiled=True)
            partial = jnp.dot(rows, out_weight, preferred_element_type=jnp.float32)
            partial = partial.reshape(pool_size, share_count, part_rows, columns)
            mine = reduce_shares(jnp.moveaxis(partial, 1, 0))
            back = lax.all_to_all(mine, "pool", split_axis=0, concat_axis=0, tiled=True)
            back = jnp.moveaxis(back, 0, 1).reshape(part_rows, pool_size * columns)
            output = lax.dynamic_update_slice(output, back, (chunk * part_rows, 0))
            continue
        for flip, rows in enumerate(spread_over_pool(attended)):
            partial = jnp.dot(rows, out_weight, preferred_element_type=jnp.float32)
            mine = reduce_shares(partial.reshape(share_count, part_rows, columns))
            back = mine if flip == 0 else swap(mine, "pool", flip)
            output = lax.dynamic_update_slice(
                output, back, (chunk * part_rows, (pool_index ^ flip) * columns)
            )
    return output


def solution(mesh):
    in_specs = (
        P(("groups", "pool"), None, ("heads", "sub")),
        P(("groups", "pool"), None),
        P(None, ("heads", "sub"), None, None),
        P(),
        P(),
        P(("heads", "sub"), "pool"),
        P("groups", None),
        P("groups", None),
        P("groups"),
        P("groups"),
    )
    out_specs = P(("groups", "pool", "heads", "sub"), None)
    return jax.shard_map(
        per_device, mesh=mesh, in_specs=in_specs, out_specs=out_specs, check_vma=False
    )
```

```python
import math

import jax
import jax.numpy as jnp
from jax import lax
from jax.sharding import PartitionSpec as P

BLK = 128
CHUNKS = 2


def rms_scale(values, gain):
    return values * lax.rsqrt(jnp.mean(values * values, axis=-1, keepdims=True) + 1e-05) * gain


def pair_rank(holders):
    count = holders.shape[1]
    same = holders[:, :, None] == holders[:, None, :]
    earlier = jnp.arange(count)[None, :] < jnp.arange(count)[:, None]
    return jnp.sum((same & earlier[None]).astype(jnp.int32), axis=2)


def swap(values, axis, flip):
    return lax.ppermute(values, axis, [(i, i ^ flip) for i in range(lax.axis_size(axis))])


def second_hop(block, across):
    index = lax.axis_index("pool")
    at_end = (index == 0) | (index == 3)
    passed = jnp.where(at_end, block, across)
    return lax.ppermute(passed, "pool", [(0, 2), (3, 1), (1, 0), (2, 3)])


def exchange_sum(pieces, axis):
    index = lax.axis_index(axis)
    total = lax.dynamic_index_in_dim(pieces, index, 0, keepdims=False)
    for flip in range(1, lax.axis_size(axis)):
        away = lax.dynamic_index_in_dim(pieces, index ^ flip, 0, keepdims=False)
        total = total + swap(away.astype(jnp.bfloat16), axis, flip).astype(jnp.float32)
    return total


def project_out(blocks, out_weight, part_rows):
    heads_size, sub_size = lax.axis_size("heads"), lax.axis_size("sub")
    rows = jnp.concatenate(blocks, axis=0)
    partial = jnp.dot(rows, out_weight, preferred_element_type=jnp.float32)
    partial = partial.reshape(len(blocks), heads_size, sub_size, part_rows, -1)
    by_sub = exchange_sum(jnp.moveaxis(partial, 2, 0), "sub")
    by_heads = exchange_sum(jnp.moveaxis(by_sub, 1, 0), "heads").astype(jnp.bfloat16)
    return [by_heads[i] for i in range(len(blocks))]


def fetch_latents(latent_store, place_holder, place_block, serving_request, items):
    pool_size = lax.axis_size("pool")
    pool_index = lax.axis_index("pool")
    share_count = lax.axis_size(("heads", "sub"))
    share = lax.axis_index(("heads", "sub"))
    capacity = 2 * ((items + pool_size - 1) // pool_size)
    total_requests = serving_request.shape[0]
    request_ids = jnp.arange(total_requests, dtype=jnp.int32)
    selector = (serving_request[:, None] == request_ids[None, :]).astype(jnp.int32)
    holders = jnp.dot(selector, place_holder).reshape(pool_size, items)
    blocks = jnp.dot(selector, place_block).reshape(pool_size, items)
    ranks = pair_rank(holders)
    slot_ids = jnp.arange(capacity, dtype=jnp.int32)
    matched = (holders[:, None, :] == pool_index) & (ranks[:, None, :] == slot_ids[None, :, None])
    send_block = jnp.sum(jnp.where(matched, blocks[:, None, :], 0), axis=2)
    rows = BLK // share_count
    store = latent_store.reshape(-1, rows, latent_store.shape[1])
    partners = jnp.arange(pool_size, dtype=jnp.int32) ^ pool_index
    wanted = send_block.at[partners].get(mode="promise_in_bounds").reshape(-1)
    outgoing = store.at[wanted * share_count + share].get(mode="promise_in_bounds")
    outgoing = outgoing.reshape(pool_size, capacity, rows, -1)
    pieces = [outgoing[0]] + [swap(outgoing[flip], "pool", flip) for flip in range(1, pool_size)]
    my_holders = lax.dynamic_index_in_dim(holders, pool_index, 0, keepdims=False)
    my_ranks = lax.dynamic_index_in_dim(ranks, pool_index, 0, keepdims=False)
    chosen = jnp.concatenate(pieces, axis=0).at[(my_holders ^ pool_index) * capacity + my_ranks]
    return selector, chosen.get(mode="promise_in_bounds")


def per_device(
    queries,
    latent_store,
    kv_up,
    q_gain,
    k_gain,
    out_weight,
    place_holder,
    place_block,
    image_count,
    serving_request,
):
    pool_size = lax.axis_size("pool")
    pool_index = lax.axis_index("pool")
    heads_size = lax.axis_size("heads")
    sub_size = lax.axis_size("sub")
    share_count = heads_size * sub_size
    share = lax.axis_index(("heads", "sub"))
    requests_here, text_rows, query_width = queries.shape
    blocks_each = place_holder.shape[1]
    items = requests_here * blocks_each
    heads_here, head_width = kv_up.shape[1], kv_up.shape[3]
    per_group = query_width // (heads_here * head_width)
    selector, chosen = fetch_latents(
        latent_store, place_holder, place_block, serving_request, items
    )
    rank_width = chosen.shape[2]
    share_rows = chosen.shape[1]
    image_slots = blocks_each * BLK
    chosen = chosen.reshape(requests_here, blocks_each * share_rows, rank_width)
    over_heads = [chosen] + [swap(chosen, "heads", flip) for flip in range(1, heads_size)]
    quarters = []
    for part in over_heads:
        quarters += [part] + [swap(part, "sub", flip) for flip in range(1, sub_size)]
    latents = jnp.concatenate(quarters, axis=1)
    projected = jnp.einsum("rsk,kgcd->rsgcd", latents, kv_up, preferred_element_type=jnp.float32)
    keys = rms_scale(projected[:, :, :, 0], k_gain).astype(jnp.bfloat16)
    values = projected[:, :, :, 1].astype(jnp.bfloat16)
    slots = jnp.arange(image_slots, dtype=jnp.int32)
    share_of, within = slots // (blocks_each * share_rows), slots % (blocks_each * share_rows)
    positions = (
        (within // share_rows) * BLK + (share_of ^ share) * share_rows + within % share_rows
    )
    count_here = lax.dynamic_slice_in_dim(
        jnp.dot(selector, image_count), pool_index * requests_here, requests_here
    )
    live = positions[None, :] < count_here[:, None]
    softmax_scale = 1.0 / math.sqrt(head_width)
    part_rows = requests_here * text_rows // share_count // CHUNKS
    columns = out_weight.shape[1]
    shaped = queries.reshape(
        requests_here,
        share_count // requests_here,
        CHUNKS,
        part_rows,
        heads_here,
        per_group,
        head_width,
    )

    def attend(chunk):
        part = shaped[:, :, chunk].reshape(requests_here, -1, heads_here, per_group, head_width)
        normed = rms_scale(part.astype(jnp.float32), q_gain).astype(jnp.bfloat16)
        scores = (
            jnp.einsum("rtgqd,rsgd->rgqts", normed, keys, preferred_element_type=jnp.float32)
            * softmax_scale
        )
        expo = jnp.where(live[:, None, None, None, :], jnp.exp(scores), jnp.zeros((), jnp.float32))
        probs = (expo / jnp.sum(expo, axis=-1, keepdims=True)).astype(jnp.bfloat16)
        attended = jnp.einsum(
            "rgqts,rsgd->rtgqd", probs, values, preferred_element_type=jnp.float32
        )
        return attended.astype(jnp.bfloat16).reshape(share_count * part_rows, query_width)

    if pool_size != 4:
        outputs = []
        for chunk in range(CHUNKS):
            rows = lax.all_gather(attend(chunk), "pool", axis=0)
            blocks = [rows[i] for i in range(pool_size)]
            mine = jnp.stack(project_out(blocks, out_weight, part_rows))
            back = lax.all_to_all(mine, "pool", split_axis=0, concat_axis=0, tiled=True)
            outputs.append(jnp.moveaxis(back, 0, 1).reshape(part_rows, pool_size * columns))
        return jnp.concatenate(outputs, axis=0)

    tie = lax.optimization_barrier
    first = attend(0)
    across0, beside0 = swap(first, "pool", 3), swap(first, "pool", 1)
    last = attend(1)
    (own0,) = project_out([first], out_weight, part_rows)
    across0, beside0, last, own0, first = tie((across0, beside0, last, own0, first))
    second0 = second_hop(first, across0)
    across1, beside1 = swap(last, "pool", 3), swap(last, "pool", 1)
    mine = project_out([across0, beside0, last], out_weight, part_rows)
    second0, across1, beside1, last, mine = tie((second0, across1, beside1, last, mine))
    out_across0, out_beside0, own1 = mine
    second1 = second_hop(last, across1)
    back_across0, back_beside0 = swap(out_across0, "pool", 3), swap(out_beside0, "pool", 1)
    mine = project_out([across1, beside1, second0], out_weight, part_rows)
    second1, back_across0, back_beside0, mine = tie((second1, back_across0, back_beside0, mine))
    out_across1, out_beside1, out_second0 = mine
    back_second0, back_across1 = swap(out_second0, "pool", 2), swap(out_across1, "pool", 3)
    back_beside1 = swap(out_beside1, "pool", 1)
    mine = project_out([second1], out_weight, part_rows)
    back_second0, back_across1, back_beside1, mine = tie(
        (back_second0, back_across1, back_beside1, mine)
    )
    back_second1 = swap(mine[0], "pool", 2)
    output = jnp.zeros((CHUNKS * part_rows, pool_size * columns), jnp.bfloat16)
    backs = [
        [own0, back_beside0, back_second0, back_across0],
        [own1, back_beside1, back_second1, back_across1],
    ]
    for chunk in range(CHUNKS):
        for flip in (0, 1, 3, 2):
            output = lax.dynamic_update_slice(
                output, backs[chunk][flip], (chunk * part_rows, (pool_index ^ flip) * columns)
            )
    return output


def solution(mesh):
    in_specs = (
        P(("groups", "pool"), None, ("heads", "sub")),
        P(("groups", "pool"), None),
        P(None, ("heads", "sub"), None, None),
        P(),
        P(),
        P(("heads", "sub"), "pool"),
        P("groups", None),
        P("groups", None),
        P("groups"),
        P("groups"),
    )
    out_specs = P(("groups", "pool", "heads", "sub"), None)
    return jax.shard_map(
        per_device, mesh=mesh, in_specs=in_specs, out_specs=out_specs, check_vma=False
    )
```

```python
import math

import jax
import jax.numpy as jnp
from jax import lax
from jax.sharding import PartitionSpec as P

BLK = 128
CHUNKS = 2


def rms_scale(values, gain):
    return values * lax.rsqrt(jnp.mean(values * values, axis=-1, keepdims=True) + 1e-05) * gain


def pair_rank(holders):
    count = holders.shape[1]
    same = holders[:, :, None] == holders[:, None, :]
    earlier = jnp.arange(count)[None, :] < jnp.arange(count)[:, None]
    return jnp.sum((same & earlier[None]).astype(jnp.int32), axis=2)


def swap(values, axis, flip):
    return lax.ppermute(values, axis, [(i, i ^ flip) for i in range(lax.axis_size(axis))])


def second_hop(block, across):
    index = lax.axis_index("pool")
    at_end = (index == 0) | (index == 3)
    passed = jnp.where(at_end, block, across)
    return lax.ppermute(passed, "pool", [(0, 2), (3, 1), (1, 0), (2, 3)])


def exchange_sum(pieces, axis):
    index = lax.axis_index(axis)
    total = lax.dynamic_index_in_dim(pieces, index, 0, keepdims=False).astype(jnp.float32)
    for flip in range(1, lax.axis_size(axis)):
        away = lax.dynamic_index_in_dim(pieces, index ^ flip, 0, keepdims=False)
        total = total + swap(away.astype(jnp.bfloat16), axis, flip).astype(jnp.float32)
    return total


def project_out(blocks, out_weight):
    rows = jnp.concatenate(blocks, axis=0)
    partial = jnp.dot(rows, out_weight, preferred_element_type=jnp.float32)
    return partial.astype(jnp.bfloat16)


def sum_direct(partial, count):
    axes = ("heads", "sub")
    pieces = partial.reshape(count, lax.axis_size(axes), -1, partial.shape[1])
    total = exchange_sum(jnp.moveaxis(pieces, 1, 0), axes).astype(jnp.bfloat16)
    return [total[i] for i in range(count)]


def sum_in_turn(partial, count):
    heads_size, sub_size = lax.axis_size("heads"), lax.axis_size("sub")
    pieces = partial.reshape(count, heads_size, sub_size, -1, partial.shape[1])
    by_sub = exchange_sum(jnp.moveaxis(pieces, 2, 0), "sub")
    total = exchange_sum(jnp.moveaxis(by_sub, 1, 0), "heads").astype(jnp.bfloat16)
    return [total[i] for i in range(count)]


def fetch_latents(latent_store, place_holder, place_block, serving_request, items):
    pool_size = lax.axis_size("pool")
    pool_index = lax.axis_index("pool")
    share_count = lax.axis_size(("heads", "sub"))
    share = lax.axis_index(("heads", "sub"))
    capacity = 2 * ((items + pool_size - 1) // pool_size)
    total_requests = serving_request.shape[0]
    request_ids = jnp.arange(total_requests, dtype=jnp.int32)
    selector = (serving_request[:, None] == request_ids[None, :]).astype(jnp.int32)
    holders = jnp.dot(selector, place_holder).reshape(pool_size, items)
    blocks = jnp.dot(selector, place_block).reshape(pool_size, items)
    ranks = pair_rank(holders)
    slot_ids = jnp.arange(capacity, dtype=jnp.int32)
    matched = (holders[:, None, :] == pool_index) & (ranks[:, None, :] == slot_ids[None, :, None])
    send_block = jnp.sum(jnp.where(matched, blocks[:, None, :], 0), axis=2)
    rows = BLK // share_count
    store = latent_store.reshape(-1, rows, latent_store.shape[1])
    partners = jnp.arange(pool_size, dtype=jnp.int32) ^ pool_index
    wanted = send_block.at[partners].get(mode="promise_in_bounds").reshape(-1)
    outgoing = store.at[wanted * share_count + share].get(mode="promise_in_bounds")
    outgoing = outgoing.reshape(pool_size, capacity, rows, -1)
    pieces = [outgoing[0]] + [swap(outgoing[flip], "pool", flip) for flip in range(1, pool_size)]
    my_holders = lax.dynamic_index_in_dim(holders, pool_index, 0, keepdims=False)
    my_ranks = lax.dynamic_index_in_dim(ranks, pool_index, 0, keepdims=False)
    chosen = jnp.concatenate(pieces, axis=0).at[(my_holders ^ pool_index) * capacity + my_ranks]
    return selector, chosen.get(mode="promise_in_bounds")


def per_device(
    queries,
    latent_store,
    kv_up,
    q_gain,
    k_gain,
    out_weight,
    place_holder,
    place_block,
    image_count,
    serving_request,
):
    pool_size = lax.axis_size("pool")
    pool_index = lax.axis_index("pool")
    heads_size = lax.axis_size("heads")
    sub_size = lax.axis_size("sub")
    share_count = heads_size * sub_size
    share = lax.axis_index(("heads", "sub"))
    requests_here, text_rows, query_width = queries.shape
    blocks_each = place_holder.shape[1]
    items = requests_here * blocks_each
    heads_here, head_width = kv_up.shape[1], kv_up.shape[3]
    per_group = query_width // (heads_here * head_width)
    selector, chosen = fetch_latents(
        latent_store, place_holder, place_block, serving_request, items
    )
    rank_width = chosen.shape[2]
    share_rows = chosen.shape[1]
    image_slots = blocks_each * BLK
    chosen = chosen.reshape(requests_here, blocks_each * share_rows, rank_width)
    over_heads = [chosen] + [swap(chosen, "heads", flip) for flip in range(1, heads_size)]
    quarters = []
    for part in over_heads:
        quarters += [part] + [swap(part, "sub", flip) for flip in range(1, sub_size)]
    latents = jnp.concatenate(quarters, axis=1)
    projected = jnp.einsum("rsk,kgcd->rsgcd", latents, kv_up, preferred_element_type=jnp.float32)
    keys = rms_scale(projected[:, :, :, 0], k_gain).astype(jnp.bfloat16)
    values = projected[:, :, :, 1].astype(jnp.bfloat16)
    slots = jnp.arange(image_slots, dtype=jnp.int32)
    share_of, within = slots // (blocks_each * share_rows), slots % (blocks_each * share_rows)
    positions = (
        (within // share_rows) * BLK + (share_of ^ share) * share_rows + within % share_rows
    )
    count_here = lax.dynamic_slice_in_dim(
        jnp.dot(selector, image_count), pool_index * requests_here, requests_here
    )
    live = positions[None, :] < count_here[:, None]
    softmax_scale = 1.0 / math.sqrt(head_width)
    part_rows = requests_here * text_rows // share_count // CHUNKS
    columns = out_weight.shape[1]
    shaped = queries.reshape(
        requests_here,
        share_count // requests_here,
        CHUNKS,
        part_rows,
        heads_here,
        per_group,
        head_width,
    )

    def attend(chunk):
        part = shaped[:, :, chunk].reshape(requests_here, -1, heads_here, per_group, head_width)
        normed = rms_scale(part.astype(jnp.float32), q_gain).astype(jnp.bfloat16)
        scores = (
            jnp.einsum("rtgqd,rsgd->rgqts", normed, keys, preferred_element_type=jnp.float32)
            * softmax_scale
        )
        expo = jnp.where(live[:, None, None, None, :], jnp.exp(scores), jnp.zeros((), jnp.float32))
        probs = (expo / jnp.sum(expo, axis=-1, keepdims=True)).astype(jnp.bfloat16)
        attended = jnp.einsum(
            "rgqts,rsgd->rtgqd", probs, values, preferred_element_type=jnp.float32
        )
        return attended.astype(jnp.bfloat16).reshape(share_count * part_rows, query_width)

    if pool_size != 4:
        outputs = []
        for chunk in range(CHUNKS):
            rows = lax.all_gather(attend(chunk), "pool", axis=0)
            blocks = [rows[i] for i in range(pool_size)]
            mine = jnp.stack(sum_in_turn(project_out(blocks, out_weight), pool_size))
            back = lax.all_to_all(mine, "pool", split_axis=0, concat_axis=0, tiled=True)
            outputs.append(jnp.moveaxis(back, 0, 1).reshape(part_rows, pool_size * columns))
        return jnp.concatenate(outputs, axis=0)

    tie = lax.optimization_barrier
    first = attend(0)
    across0, beside0 = swap(first, "pool", 3), swap(first, "pool", 1)
    last = attend(1)
    first, last, across0, beside0 = tie((first, last, across0, beside0))
    second0 = second_hop(first, across0)
    partial = project_out([first, beside0, across0, last], out_weight)
    second0, partial, last = tie((second0, partial, last))
    across1, beside1 = swap(last, "pool", 3), swap(last, "pool", 1)
    mine = sum_direct(partial, 4)
    across1, beside1, mine, last = tie((across1, beside1, mine, last))
    own0, out_beside0, out_across0, own1 = mine
    second1 = second_hop(last, across1)
    partial = project_out([beside1, across1, second0], out_weight)
    second1, partial = tie((second1, partial))
    back_across0, back_beside0 = swap(out_across0, "pool", 3), swap(out_beside0, "pool", 1)
    mine = sum_in_turn(partial, 3)
    partial = project_out([second1], out_weight)
    back_across0, back_beside0, mine, partial = tie((back_across0, back_beside0, mine, partial))
    out_beside1, out_across1, out_second0 = mine
    back_across1, back_second0 = swap(out_across1, "pool", 3), swap(out_second0, "pool", 2)
    back_beside1 = swap(out_beside1, "pool", 1)
    mine = sum_in_turn(partial, 1)
    back_across1, back_second0, back_beside1, mine = tie(
        (back_across1, back_second0, back_beside1, mine)
    )
    back_second1 = swap(mine[0], "pool", 2)
    output = jnp.zeros((CHUNKS * part_rows, pool_size * columns), jnp.bfloat16)
    backs = [
        [own0, back_beside0, back_second0, back_across0],
        [own1, back_beside1, back_second1, back_across1],
    ]
    for chunk in range(CHUNKS):
        for flip in (0, 1, 3, 2):
            output = lax.dynamic_update_slice(
                output, backs[chunk][flip], (chunk * part_rows, (pool_index ^ flip) * columns)
            )
    return output


def solution(mesh):
    in_specs = (
        P(("groups", "pool"), None, ("heads", "sub")),
        P(("groups", "pool"), None),
        P(None, ("heads", "sub"), None, None),
        P(),
        P(),
        P(("heads", "sub"), "pool"),
        P("groups", None),
        P("groups", None),
        P("groups"),
        P("groups"),
    )
    out_specs = P(("groups", "pool", "heads", "sub"), None)
    return jax.shard_map(
        per_device, mesh=mesh, in_specs=in_specs, out_specs=out_specs, check_vma=False
    )
```

```python
import functools
import math

import jax
import jax.numpy as jnp
from jax import lax
from jax.experimental import pallas as pl
from jax.experimental.pallas import tpu as pltpu
from jax.sharding import PartitionSpec as P

BLK = 128


def rms_scale(values, gain):
    return values * lax.rsqrt(jnp.mean(values * values, axis=-1, keepdims=True) + 1e-05) * gain


def pair_rank(holders):
    count = holders.shape[1]
    same = holders[:, :, None] == holders[:, None, :]
    earlier = jnp.arange(count)[None, :] < jnp.arange(count)[:, None]
    return jnp.sum((same & earlier[None]).astype(jnp.int32), axis=2)


def swap(values, axis, flip):
    return lax.ppermute(values, axis, [(i, i ^ flip) for i in range(lax.axis_size(axis))])


def second_hop(block, across):
    index = lax.axis_index("pool")
    at_end = (index == 0) | (index == 3)
    passed = jnp.where(at_end, block, across)
    return lax.ppermute(passed, "pool", [(0, 2), (3, 1), (1, 0), (2, 3)])


def exchange_sum(pieces, axis):
    index = lax.axis_index(axis)
    total = lax.dynamic_index_in_dim(pieces, index, 0, keepdims=False).astype(jnp.float32)
    for flip in range(1, lax.axis_size(axis)):
        away = lax.dynamic_index_in_dim(pieces, index ^ flip, 0, keepdims=False)
        total = total + swap(away.astype(jnp.bfloat16), axis, flip).astype(jnp.float32)
    return total


def project_out(blocks, out_weight):
    rows = jnp.concatenate(blocks, axis=0)
    partial = jnp.dot(rows, out_weight, preferred_element_type=jnp.float32)
    return partial.astype(jnp.bfloat16)


def sum_in_turn(partial, count):
    heads_size, sub_size = lax.axis_size("heads"), lax.axis_size("sub")
    pieces = partial.reshape(count, heads_size, sub_size, -1, partial.shape[1])
    by_sub = exchange_sum(jnp.moveaxis(pieces, 2, 0), "sub")
    total = exchange_sum(jnp.moveaxis(by_sub, 1, 0), "heads").astype(jnp.bfloat16)
    return [total[i] for i in range(count)]


def fetch_latents(latent_store, place_holder, place_block, serving_request, items):
    pool_size = lax.axis_size("pool")
    pool_index = lax.axis_index("pool")
    share_count = lax.axis_size(("heads", "sub"))
    share = lax.axis_index(("heads", "sub"))
    capacity = 2 * ((items + pool_size - 1) // pool_size)
    total_requests = serving_request.shape[0]
    request_ids = jnp.arange(total_requests, dtype=jnp.int32)
    selector = (serving_request[:, None] == request_ids[None, :]).astype(jnp.int32)
    holders = jnp.dot(selector, place_holder).reshape(pool_size, items)
    blocks = jnp.dot(selector, place_block).reshape(pool_size, items)
    ranks = pair_rank(holders)
    slot_ids = jnp.arange(capacity, dtype=jnp.int32)
    matched = (holders[:, None, :] == pool_index) & (ranks[:, None, :] == slot_ids[None, :, None])
    send_block = jnp.sum(jnp.where(matched, blocks[:, None, :], 0), axis=2)
    rows = BLK // share_count
    store = latent_store.reshape(-1, rows, latent_store.shape[1])
    partners = jnp.arange(pool_size, dtype=jnp.int32) ^ pool_index
    wanted = send_block.at[partners].get(mode="promise_in_bounds").reshape(-1)
    outgoing = store.at[wanted * share_count + share].get(mode="promise_in_bounds")
    outgoing = outgoing.reshape(pool_size, capacity, rows, -1)
    pieces = [outgoing[0]] + [swap(outgoing[flip], "pool", flip) for flip in range(1, pool_size)]
    my_holders = lax.dynamic_index_in_dim(holders, pool_index, 0, keepdims=False)
    my_ranks = lax.dynamic_index_in_dim(ranks, pool_index, 0, keepdims=False)
    chosen = jnp.concatenate(pieces, axis=0).at[(my_holders ^ pool_index) * capacity + my_ranks]
    return selector, chosen.get(mode="promise_in_bounds")


def attend_kernel(share_count, scalars, queries, *refs):
    parts, (kv_up, q_gain, k_gain, out, keys, values) = refs[:share_count], refs[share_count:]
    head_width = q_gain.shape[1]
    per_group = queries.shape[2] // head_width
    part_slots = parts[0].shape[1]
    share_rows = BLK // share_count
    count, share = scalars[0], scalars[1]
    for flip in range(share_count):
        rows = pl.ds(flip * part_slots, part_slots)
        projected = jnp.dot(parts[flip][0], kv_up[...], preferred_element_type=jnp.float32)
        key = rms_scale(projected[:, :head_width], k_gain[...])
        keys[rows, :] = key.astype(jnp.bfloat16)
        slot = lax.broadcasted_iota(jnp.int32, (part_slots, head_width), 0)
        position = (slot // share_rows) * BLK + (share ^ flip) * share_rows + slot % share_rows
        live = jnp.where(position < count, 1.0, 0.0)
        values[rows, :head_width] = (projected[:, head_width:] * live).astype(jnp.bfloat16)
        values[rows, head_width:] = live.astype(jnp.bfloat16)
    scale = math.log2(math.e) / math.sqrt(head_width)
    together = 2 if per_group % 2 == 0 else 1
    text = queries.shape[1]
    for first in range(0, per_group, together):
        normed = []
        for head in range(first, first + together):
            query = queries[0, :, head * head_width : (head + 1) * head_width]
            normed.append(rms_scale(query.astype(jnp.float32), q_gain[...]).astype(jnp.bfloat16))
        scores = lax.dot_general(
            jnp.concatenate(normed, axis=0),
            keys[...],
            (((1,), (1,)), ((), ())),
            preferred_element_type=jnp.float32,
        )
        expo = jnp.exp2(scores * scale).astype(jnp.bfloat16)
        total = jnp.dot(expo, values[...], preferred_element_type=jnp.float32)
        result = (total[:, :head_width] / total[:, head_width:]).astype(jnp.bfloat16)
        for i in range(together):
            head = first + i
            columns = slice(head * head_width, (head + 1) * head_width)
            out[:, columns] = result[i * text : (i + 1) * text]


def attend(request, queries, parts, kv_flat, q_gain, k_gain, scalars):
    _, text, width = queries.shape
    heads_here, rank_width, pair_width = kv_flat.shape
    head_width = q_gain.shape[1]
    part_slots = parts[0].shape[1]
    slots = len(parts) * part_slots
    here = lambda g: (request, 0, 0)
    return pl.pallas_call(
        functools.partial(attend_kernel, len(parts)),
        grid=(heads_here,),
        in_specs=[
            pl.BlockSpec(memory_space=pltpu.SMEM),
            pl.BlockSpec((1, text, width // heads_here), lambda g: (request, 0, g)),
        ]
        + [pl.BlockSpec((1, part_slots, rank_width), here) for _ in parts]
        + [
            pl.BlockSpec((None, rank_width, pair_width), lambda g: (g, 0, 0)),
            pl.BlockSpec((1, head_width), lambda g: (0, 0)),
            pl.BlockSpec((1, head_width), lambda g: (0, 0)),
        ],
        out_specs=pl.BlockSpec((text, width // heads_here), lambda g: (0, g)),
        out_shape=jax.ShapeDtypeStruct((text, width), jnp.bfloat16),
        scratch_shapes=[
            pltpu.VMEM((slots, head_width), jnp.bfloat16),
            pltpu.VMEM((slots, 2 * head_width), jnp.bfloat16),
        ],
        compiler_params=pltpu.CompilerParams(vmem_limit_bytes=32 * 1024 * 1024),
        cost_estimate=pl.CostEstimate(
            flops=4 * text * width * slots + 2 * slots * rank_width * heads_here * pair_width,
            bytes_accessed=4 * text * width + 2 * slots * rank_width,
            transcendentals=text * slots * (width // head_width),
        ),
    )(scalars, queries, *parts, kv_flat, q_gain, k_gain)


def per_device(
    queries,
    latent_store,
    kv_up,
    q_gain,
    k_gain,
    out_weight,
    place_holder,
    place_block,
    image_count,
    serving_request,
):
    pool_size = lax.axis_size("pool")
    pool_index = lax.axis_index("pool")
    heads_size = lax.axis_size("heads")
    sub_size = lax.axis_size("sub")
    share_count = heads_size * sub_size
    share = lax.axis_index(("heads", "sub"))
    requests_here, text_rows, _ = queries.shape
    blocks_each = place_holder.shape[1]
    items = requests_here * blocks_each
    selector, chosen = fetch_latents(
        latent_store, place_holder, place_block, serving_request, items
    )
    rank_width = chosen.shape[2]
    chosen = chosen.reshape(requests_here, -1, rank_width)
    over_heads = [chosen] + [swap(chosen, "heads", flip) for flip in range(1, heads_size)]
    parts = []
    for part in over_heads:
        parts += [part] + [swap(part, "sub", flip) for flip in range(1, sub_size)]
    kv_flat = jnp.moveaxis(kv_up.reshape(rank_width, kv_up.shape[1], -1), 1, 0)
    gains = q_gain.reshape(1, -1), k_gain.reshape(1, -1)
    count_here = lax.dynamic_slice_in_dim(
        jnp.dot(selector, image_count), pool_index * requests_here, requests_here
    )

    def attended(request):
        scalars = jnp.stack([count_here[request], share])
        return attend(request, queries, parts, kv_flat, *gains, scalars)

    columns = out_weight.shape[1]
    part_rows = requests_here * text_rows // share_count
    if pool_size != 4 or requests_here != 2:
        block = jnp.concatenate([attended(request) for request in range(requests_here)])
        rows = lax.all_gather(block, "pool", axis=0)
        blocks = [rows[i] for i in range(pool_size)]
        mine = jnp.stack(sum_in_turn(project_out(blocks, out_weight), pool_size))
        back = lax.all_to_all(mine, "pool", split_axis=0, concat_axis=0, tiled=True)
        return jnp.moveaxis(back, 0, 1).reshape(part_rows, pool_size * columns)

    tie = lax.optimization_barrier
    first = attended(0)
    across0, beside0 = swap(first, "pool", 3), swap(first, "pool", 1)
    last = attended(1)
    first, last, across0, beside0 = tie((first, last, across0, beside0))
    across1, beside1 = swap(last, "pool", 3), swap(last, "pool", 1)
    partial0 = project_out([first, last, beside0, across0], out_weight)
    first, last, across0, across1, beside1, partial0 = tie(
        (first, last, across0, across1, beside1, partial0)
    )
    second0 = second_hop(first, across0)
    partial1 = project_out([beside1, across1], out_weight)
    second0, partial0, partial1, last, across1 = tie((second0, partial0, partial1, last, across1))
    second1 = second_hop(last, across1)
    half = partial1.shape[0] // 2
    own, partial0 = partial0[: 2 * half], partial0[2 * half :]
    partial = [partial0[:half], partial1[:half], partial0[half:], partial1[half:]]
    out_beside, out_across = sum_in_turn(jnp.concatenate(partial), 2)
    second0, second1, out_beside, out_across, own = tie(
        (second0, second1, out_beside, out_across, own)
    )
    back_beside, back_across = swap(out_beside, "pool", 1), swap(out_across, "pool", 3)
    (out_second,) = sum_in_turn(project_out([second0, second1], out_weight), 1)
    back_beside, back_across, out_second, own = tie((back_beside, back_across, out_second, own))
    back_second = swap(out_second, "pool", 2)
    (own,) = sum_in_turn(own, 1)
    output = jnp.zeros((part_rows, pool_size * columns), jnp.bfloat16)
    backs = [own, back_beside, back_second, back_across]
    for flip in (0, 1, 3, 2):
        output = lax.dynamic_update_slice(output, backs[flip], (0, (pool_index ^ flip) * columns))
    return output


def solution(mesh):
    in_specs = (
        P(("groups", "pool"), None, ("heads", "sub")),
        P(("groups", "pool"), None),
        P(None, ("heads", "sub"), None, None),
        P(),
        P(),
        P(("heads", "sub"), "pool"),
        P("groups", None),
        P("groups", None),
        P("groups"),
        P("groups"),
    )
    out_specs = P(("groups", "pool", "heads", "sub"), None)
    return jax.shard_map(
        per_device, mesh=mesh, in_specs=in_specs, out_specs=out_specs, check_vma=False
    )
```

```python
import functools
import math

import jax
import jax.numpy as jnp
from jax import lax
from jax.experimental import pallas as pl
from jax.experimental.pallas import tpu as pltpu
from jax.sharding import PartitionSpec as P

BLK = 128
CHUNKS = 2


def rms_scale(values, gain):
    return values * lax.rsqrt(jnp.mean(values * values, axis=-1, keepdims=True) + 1e-05) * gain


def pair_rank(holders):
    count = holders.shape[1]
    same = holders[:, :, None] == holders[:, None, :]
    earlier = jnp.arange(count)[None, :] < jnp.arange(count)[:, None]
    return jnp.sum((same & earlier[None]).astype(jnp.int32), axis=2)


def swap(values, axis, flip):
    return lax.ppermute(values, axis, [(i, i ^ flip) for i in range(lax.axis_size(axis))])


def second_hop(block, across):
    index = lax.axis_index("pool")
    at_end = (index == 0) | (index == 3)
    passed = jnp.where(at_end, block, across)
    return lax.ppermute(passed, "pool", [(0, 2), (3, 1), (1, 0), (2, 3)])


def exchange_sum(pieces, axis):
    index = lax.axis_index(axis)
    total = lax.dynamic_index_in_dim(pieces, index, 0, keepdims=False).astype(jnp.float32)
    for flip in range(1, lax.axis_size(axis)):
        away = lax.dynamic_index_in_dim(pieces, index ^ flip, 0, keepdims=False)
        total = total + swap(away.astype(jnp.bfloat16), axis, flip).astype(jnp.float32)
    return total


def project_out(blocks, out_weight):
    rows = jnp.concatenate(blocks, axis=0)
    partial = jnp.dot(rows, out_weight, preferred_element_type=jnp.float32)
    return partial.astype(jnp.bfloat16)


def sum_shares(partial, count):
    axes = ("heads", "sub")
    pieces = partial.reshape(count, lax.axis_size(axes), -1, partial.shape[1])
    total = exchange_sum(jnp.moveaxis(pieces, 1, 0), axes).astype(jnp.bfloat16)
    return [total[i] for i in range(count)]


def find_blocks(place_holder, place_block, serving_request, items):
    pool_size = lax.axis_size("pool")
    pool_index = lax.axis_index("pool")
    capacity = 2 * ((items + pool_size - 1) // pool_size)
    total_requests = serving_request.shape[0]
    request_ids = jnp.arange(total_requests, dtype=jnp.int32)
    selector = (serving_request[:, None] == request_ids[None, :]).astype(jnp.int32)
    holders = jnp.dot(selector, place_holder).reshape(pool_size, items)
    blocks = jnp.dot(selector, place_block).reshape(pool_size, items)
    ranks = pair_rank(holders)
    slot_ids = jnp.arange(capacity, dtype=jnp.int32)
    matched = (holders[:, None, :] == pool_index) & (ranks[:, None, :] == slot_ids[None, :, None])
    send_block = jnp.sum(jnp.where(matched, blocks[:, None, :], 0), axis=2)
    partners = jnp.arange(pool_size, dtype=jnp.int32) ^ pool_index
    wanted = send_block.at[partners].get(mode="promise_in_bounds")
    my_holders = lax.dynamic_index_in_dim(holders, pool_index, 0, keepdims=False)
    my_ranks = lax.dynamic_index_in_dim(ranks, pool_index, 0, keepdims=False)
    return selector, wanted, (my_holders ^ pool_index) * capacity + my_ranks


def fetch_pieces(latent_store, wanted):
    share_count = lax.axis_size(("heads", "sub"))
    share = lax.axis_index(("heads", "sub"))
    rows = BLK // share_count
    store = latent_store.reshape(-1, rows, latent_store.shape[1])
    outgoing = store.at[wanted.reshape(-1) * share_count + share].get(mode="promise_in_bounds")
    outgoing = outgoing.reshape(*wanted.shape, rows, -1)
    arriving = {flip: swap(outgoing[flip], "pool", flip) for flip in (*range(2, len(wanted)), 1)}
    return [outgoing[0]] + [arriving[flip] for flip in range(1, len(wanted))]


def attend_kernel(share_count, scalars, queries, *refs):
    parts, (kv_up, q_gain, k_gain, out, keys, values) = refs[:share_count], refs[share_count:]
    request = pl.program_id(0)
    head_width = q_gain.shape[1]
    text, width = out.shape
    per_group = width // head_width
    part_slots = parts[0].shape[1]
    share_rows = BLK // share_count
    count, share = scalars[1 + request], scalars[0]
    for flip in range(share_count):
        rows = pl.ds(flip * part_slots, part_slots)
        projected = jnp.dot(parts[flip][request], kv_up[...], preferred_element_type=jnp.float32)
        key = rms_scale(projected[:, :head_width], k_gain[...])
        keys[rows, :] = key.astype(jnp.bfloat16)
        slot = lax.broadcasted_iota(jnp.int32, (part_slots, head_width), 0)
        position = (slot // share_rows) * BLK + (share ^ flip) * share_rows + slot % share_rows
        live = jnp.where(position < count, 1.0, 0.0)
        values[rows, :head_width] = (projected[:, head_width:] * live).astype(jnp.bfloat16)
        values[rows, head_width:] = live.astype(jnp.bfloat16)
    scale = math.log2(math.e) / math.sqrt(head_width)
    together = min(per_group, max(1, 256 // text))
    for first in range(0, per_group, together):
        normed = []
        for head in range(first, first + together):
            query = queries[0, :, 0, :, head * head_width : (head + 1) * head_width]
            query = query.reshape(text, head_width).astype(jnp.float32)
            normed.append(rms_scale(query, q_gain[...]).astype(jnp.bfloat16))
        scores = lax.dot_general(
            jnp.concatenate(normed, axis=0),
            keys[...],
            (((1,), (1,)), ((), ())),
            preferred_element_type=jnp.float32,
        )
        expo = jnp.exp2(scores * scale).astype(jnp.bfloat16)
        total = jnp.dot(expo, values[...], preferred_element_type=jnp.float32)
        result = (total[:, :head_width] / total[:, head_width:]).astype(jnp.bfloat16)
        for i in range(together):
            head = first + i
            columns = slice(head * head_width, (head + 1) * head_width)
            out[:, columns] = result[i * text : (i + 1) * text]


def attend(chunk, queries, parts, kv_flat, q_gain, k_gain, scalars):
    requests, request_shares, _, part_rows, width = queries.shape
    heads_here, rank_width, pair_width = kv_flat.shape
    head_width = q_gain.shape[1]
    slots = len(parts) * parts[0].shape[1]
    text = request_shares * part_rows
    whole = pl.BlockSpec(memory_space=pltpu.VMEM)
    return pl.pallas_call(
        functools.partial(attend_kernel, len(parts)),
        grid=(requests, heads_here),
        in_specs=[
            pl.BlockSpec(memory_space=pltpu.SMEM),
            pl.BlockSpec(
                (1, request_shares, 1, part_rows, width // heads_here),
                lambda r, g: (r, 0, chunk, 0, g),
            ),
        ]
        + [whole for _ in parts]
        + [pl.BlockSpec((None, rank_width, pair_width), lambda r, g: (g, 0, 0)), whole, whole],
        out_specs=pl.BlockSpec((text, width // heads_here), lambda r, g: (r, g)),
        out_shape=jax.ShapeDtypeStruct((requests * text, width), jnp.bfloat16),
        scratch_shapes=[
            pltpu.VMEM((slots, head_width), jnp.bfloat16),
            pltpu.VMEM((slots, 2 * head_width), jnp.bfloat16),
        ],
        compiler_params=pltpu.CompilerParams(vmem_limit_bytes=32 * 1024 * 1024),
        cost_estimate=pl.CostEstimate(
            flops=requests
            * slots
            * (4 * text * width + 2 * rank_width * heads_here * pair_width),
            bytes_accessed=requests * (4 * text * width + 2 * slots * rank_width),
            transcendentals=requests * text * slots * (width // head_width),
        ),
    )(scalars, queries, *parts, kv_flat, q_gain, k_gain)


def per_device(
    queries,
    latent_store,
    kv_up,
    q_gain,
    k_gain,
    out_weight,
    place_holder,
    place_block,
    image_count,
    serving_request,
):
    pool_size = lax.axis_size("pool")
    pool_index = lax.axis_index("pool")
    heads_size = lax.axis_size("heads")
    sub_size = lax.axis_size("sub")
    share_count = heads_size * sub_size
    share = lax.axis_index(("heads", "sub"))
    requests_here, text_rows, _ = queries.shape
    blocks_each = place_holder.shape[1]
    items = requests_here * blocks_each
    rank_width = latent_store.shape[1]
    tie = lax.optimization_barrier
    selector, wanted, where = find_blocks(place_holder, place_block, serving_request, items)
    kv_flat = jnp.moveaxis(kv_up.reshape(rank_width, kv_up.shape[1], -1), 1, 0)
    gains = q_gain.reshape(1, -1), k_gain.reshape(1, -1)
    count_here = lax.dynamic_slice_in_dim(
        jnp.dot(selector, image_count), pool_index * requests_here, requests_here
    )
    scalars = jnp.concatenate([share.reshape(1), count_here])
    pieces = fetch_pieces(latent_store, wanted)
    pieces, kv_flat, scalars = tie((pieces, kv_flat, scalars))
    chosen = jnp.concatenate(pieces, axis=0).at[where].get(mode="promise_in_bounds")
    chosen = chosen.reshape(requests_here, -1, rank_width)
    over_heads = [chosen] + [swap(chosen, "heads", flip) for flip in range(1, heads_size)]
    parts = []
    for part in over_heads:
        parts += [part] + [swap(part, "sub", flip) for flip in range(1, sub_size)]
    part_rows = requests_here * text_rows // share_count
    shaped = queries.reshape(
        requests_here, share_count // requests_here, CHUNKS, part_rows // CHUNKS, -1
    )

    def attended(chunk):
        return attend(chunk, shaped, parts, kv_flat, *gains, scalars)

    columns = out_weight.shape[1]
    if pool_size != 4:
        outputs = []
        for chunk in range(CHUNKS):
            rows = lax.all_gather(attended(chunk), "pool", axis=0)
            blocks = [rows[i] for i in range(pool_size)]
            mine = jnp.stack(sum_shares(project_out(blocks, out_weight), pool_size))
            back = lax.all_to_all(mine, "pool", split_axis=0, concat_axis=0, tiled=True)
            outputs.append(jnp.moveaxis(back, 0, 1).reshape(-1, pool_size * columns))
        return jnp.concatenate(outputs, axis=0)

    first = attended(0)
    across0, beside0 = swap(first, "pool", 3), swap(first, "pool", 1)
    last = attended(1)
    first, last, across0, beside0 = tie((first, last, across0, beside0))
    across1, beside1 = swap(last, "pool", 3), swap(last, "pool", 1)
    partial = project_out([first, last, beside0, across0], out_weight)
    first, last, across0, across1, beside1, partial = tie(
        (first, last, across0, across1, beside1, partial)
    )
    half = partial.shape[0] // 2
    own, partial = partial[:half], partial[half:]
    second0 = second_hop(first, across0)
    out_beside0, out_across0 = sum_shares(partial, 2)
    partial = project_out([beside1, across1], out_weight)
    second0, out_beside0, out_across0, partial, own, last, across1 = tie(
        (second0, out_beside0, out_across0, partial, own, last, across1)
    )
    second1 = second_hop(last, across1)
    out_beside1, out_across1 = sum_shares(partial, 2)
    partial = project_out([second0], out_weight)
    second1, out_beside1, out_across1, partial, out_beside0, out_across0, own = tie(
        (second1, out_beside1, out_across1, partial, out_beside0, out_across0, own)
    )
    back_across = swap(jnp.concatenate([out_across0, out_across1]), "pool", 3)
    back_beside = swap(jnp.concatenate([out_beside0, out_beside1]), "pool", 1)
    partial = jnp.concatenate([partial, project_out([second1], out_weight)])
    out_second = jnp.concatenate(sum_shares(partial, 2))
    back_across, back_beside, out_second, own = tie((back_across, back_beside, out_second, own))
    back_second = swap(out_second, "pool", 2)
    own = jnp.concatenate(sum_shares(own, 2))
    output = jnp.zeros((part_rows, pool_size * columns), jnp.bfloat16)
    backs = [own, back_beside, back_second, back_across]
    for flip in (0, 1, 3, 2):
        output = lax.dynamic_update_slice(output, backs[flip], (0, (pool_index ^ flip) * columns))
    return output


def solution(mesh):
    in_specs = (
        P(("groups", "pool"), None, ("heads", "sub")),
        P(("groups", "pool"), None),
        P(None, ("heads", "sub"), None, None),
        P(),
        P(),
        P(("heads", "sub"), "pool"),
        P("groups", None),
        P("groups", None),
        P("groups"),
        P("groups"),
    )
    out_specs = P(("groups", "pool", "heads", "sub"), None)
    return jax.shard_map(
        per_device, mesh=mesh, in_specs=in_specs, out_specs=out_specs, check_vma=False
    )
```

```python
import functools
import math

import jax
import jax.numpy as jnp
from jax import lax
from jax.experimental import pallas as pl
from jax.experimental.pallas import tpu as pltpu
from jax.sharding import PartitionSpec as P

BLK = 128
CHUNKS = 2
LIGHT = pl.CostEstimate(flops=1, bytes_accessed=1, transcendentals=0)


def rms_scale(values, gain):
    return values * lax.rsqrt(jnp.mean(values * values, axis=-1, keepdims=True) + 1e-05) * gain


def pair_rank(holders):
    count = holders.shape[1]
    same = holders[:, :, None] == holders[:, None, :]
    earlier = jnp.arange(count)[None, :] < jnp.arange(count)[:, None]
    return jnp.sum((same & earlier[None]).astype(jnp.int32), axis=2)


def swap(values, axis, flip):
    return lax.ppermute(values, axis, [(i, i ^ flip) for i in range(lax.axis_size(axis))])


def second_hop(block, across):
    index = lax.axis_index("pool")
    at_end = (index == 0) | (index == 3)
    passed = jnp.where(at_end, block, across)
    return lax.ppermute(passed, "pool", [(0, 2), (3, 1), (1, 0), (2, 3)])


def project_kernel(block_count, share_count, share, *refs):
    blocks, weight, outs = refs[:block_count], refs[block_count], refs[block_count + 1 :]
    part_rows = blocks[0].shape[0] // share_count
    picked = []
    for flip in range(share_count):
        start = pl.multiple_of((share[0] ^ flip) * part_rows, part_rows)
        picked += [block[pl.ds(start, part_rows), :] for block in blocks]
    product = jnp.dot(
        jnp.concatenate(picked, axis=0), weight[...], preferred_element_type=jnp.float32
    )
    rows = block_count * part_rows
    for flip in range(share_count):
        outs[flip][...] = product[flip * rows : (flip + 1) * rows].astype(outs[flip].dtype)


def project_out(blocks, out_weight):
    axes = ("heads", "sub")
    share_count = lax.axis_size(axes)
    share = lax.axis_index(axes).astype(jnp.int32).reshape(1)
    depth, columns = out_weight.shape
    rows = sum(block.shape[0] for block in blocks) // share_count
    tile = min(columns, 512)
    whole = pl.BlockSpec(memory_space=pltpu.VMEM)
    return pl.pallas_call(
        functools.partial(project_kernel, len(blocks), share_count),
        grid=(columns // tile,),
        in_specs=[pl.BlockSpec(memory_space=pltpu.SMEM)]
        + [whole for _ in blocks]
        + [pl.BlockSpec((depth, tile), lambda n: (0, n))],
        out_specs=[pl.BlockSpec((rows, tile), lambda n: (0, n))] * share_count,
        out_shape=[
            jax.ShapeDtypeStruct((rows, columns), jnp.bfloat16 if flip else jnp.float32)
            for flip in range(share_count)
        ],
        compiler_params=pltpu.CompilerParams(vmem_limit_bytes=32 * 1024 * 1024),
        cost_estimate=LIGHT,
    )(share, *blocks, out_weight)


def sum_shares(pieces):
    total = pieces[0]
    for flip in range(1, len(pieces)):
        total = total + swap(pieces[flip], ("heads", "sub"), flip).astype(jnp.float32)
    return total.astype(jnp.bfloat16)


def find_blocks(place_holder, place_block, serving_request, items):
    pool_size = lax.axis_size("pool")
    pool_index = lax.axis_index("pool")
    capacity = 2 * ((items + pool_size - 1) // pool_size)
    total_requests = serving_request.shape[0]
    request_ids = jnp.arange(total_requests, dtype=jnp.int32)
    selector = (serving_request[:, None] == request_ids[None, :]).astype(jnp.int32)
    holders = jnp.dot(selector, place_holder).reshape(pool_size, items)
    blocks = jnp.dot(selector, place_block).reshape(pool_size, items)
    ranks = pair_rank(holders)
    slot_ids = jnp.arange(capacity, dtype=jnp.int32)
    matched = (holders[:, None, :] == pool_index) & (ranks[:, None, :] == slot_ids[None, :, None])
    send_block = jnp.sum(jnp.where(matched, blocks[:, None, :], 0), axis=2)
    partners = jnp.arange(pool_size, dtype=jnp.int32) ^ pool_index
    wanted = send_block.at[partners].get(mode="promise_in_bounds")
    my_holders = lax.dynamic_index_in_dim(holders, pool_index, 0, keepdims=False)
    my_ranks = lax.dynamic_index_in_dim(ranks, pool_index, 0, keepdims=False)
    return selector, wanted, (my_holders ^ pool_index) * capacity + my_ranks


def fetch_pieces(latent_store, wanted):
    share_count = lax.axis_size(("heads", "sub"))
    share = lax.axis_index(("heads", "sub"))
    rows = BLK // share_count
    store = latent_store.reshape(-1, rows, latent_store.shape[1])
    outgoing = store.at[wanted.reshape(-1) * share_count + share].get(mode="promise_in_bounds")
    outgoing = outgoing.reshape(*wanted.shape, rows, -1)
    arriving = {flip: swap(outgoing[flip], "pool", flip) for flip in (*range(2, len(wanted)), 1)}
    return [outgoing[0]] + [arriving[flip] for flip in range(1, len(wanted))]


def attend_kernel(share_count, scalars, queries, *refs):
    parts, (kv_up, q_gain, k_gain, out, keys, values) = refs[:share_count], refs[share_count:]
    request = pl.program_id(0)
    head_width = q_gain.shape[1]
    text, width = out.shape
    per_group = width // head_width
    part_slots = parts[0].shape[1]
    share_rows = BLK // share_count
    count, share = scalars[1 + request], scalars[0]
    for flip in range(share_count):
        rows = pl.ds(flip * part_slots, part_slots)
        projected = jnp.dot(parts[flip][request], kv_up[...], preferred_element_type=jnp.float32)
        key = rms_scale(projected[:, :head_width], k_gain[...])
        keys[rows, :] = key.astype(jnp.bfloat16)
        slot = lax.broadcasted_iota(jnp.int32, (part_slots, head_width), 0)
        position = (slot // share_rows) * BLK + (share ^ flip) * share_rows + slot % share_rows
        live = jnp.where(position < count, 1.0, 0.0)
        values[rows, :head_width] = (projected[:, head_width:] * live).astype(jnp.bfloat16)
        values[rows, head_width:] = live.astype(jnp.bfloat16)
    scale = math.log2(math.e) / math.sqrt(head_width)
    together = min(per_group, max(1, 256 // text))
    for first in range(0, per_group, together):
        normed = []
        for head in range(first, first + together):
            query = queries[0, :, 0, :, head * head_width : (head + 1) * head_width]
            query = query.reshape(text, head_width).astype(jnp.float32)
            normed.append(rms_scale(query, q_gain[...]).astype(jnp.bfloat16))
        scores = lax.dot_general(
            jnp.concatenate(normed, axis=0),
            keys[...],
            (((1,), (1,)), ((), ())),
            preferred_element_type=jnp.float32,
        )
        expo = jnp.exp2(scores * scale).astype(jnp.bfloat16)
        total = jnp.dot(expo, values[...], preferred_element_type=jnp.float32)
        result = (total[:, :head_width] / total[:, head_width:]).astype(jnp.bfloat16)
        for i in range(together):
            head = first + i
            columns = slice(head * head_width, (head + 1) * head_width)
            out[:, columns] = result[i * text : (i + 1) * text]


def attend(chunk, queries, parts, kv_flat, q_gain, k_gain, scalars):
    requests, request_shares, _, part_rows, width = queries.shape
    heads_here, rank_width, pair_width = kv_flat.shape
    head_width = q_gain.shape[1]
    slots = len(parts) * parts[0].shape[1]
    text = request_shares * part_rows
    whole = pl.BlockSpec(memory_space=pltpu.VMEM)
    return pl.pallas_call(
        functools.partial(attend_kernel, len(parts)),
        grid=(requests, heads_here),
        in_specs=[
            pl.BlockSpec(memory_space=pltpu.SMEM),
            pl.BlockSpec(
                (1, request_shares, 1, part_rows, width // heads_here),
                lambda r, g: (r, 0, chunk, 0, g),
            ),
        ]
        + [whole for _ in parts]
        + [pl.BlockSpec((None, rank_width, pair_width), lambda r, g: (g, 0, 0)), whole, whole],
        out_specs=pl.BlockSpec((text, width // heads_here), lambda r, g: (r, g)),
        out_shape=jax.ShapeDtypeStruct((requests * text, width), jnp.bfloat16),
        scratch_shapes=[
            pltpu.VMEM((slots, head_width), jnp.bfloat16),
            pltpu.VMEM((slots, 2 * head_width), jnp.bfloat16),
        ],
        compiler_params=pltpu.CompilerParams(vmem_limit_bytes=32 * 1024 * 1024),
        cost_estimate=LIGHT,
    )(scalars, queries, *parts, kv_flat, q_gain, k_gain)


def per_device(
    queries,
    latent_store,
    kv_up,
    q_gain,
    k_gain,
    out_weight,
    place_holder,
    place_block,
    image_count,
    serving_request,
):
    pool_size = lax.axis_size("pool")
    pool_index = lax.axis_index("pool")
    heads_size = lax.axis_size("heads")
    sub_size = lax.axis_size("sub")
    share_count = heads_size * sub_size
    share = lax.axis_index(("heads", "sub"))
    requests_here, text_rows, _ = queries.shape
    blocks_each = place_holder.shape[1]
    items = requests_here * blocks_each
    rank_width = latent_store.shape[1]
    tie = lax.optimization_barrier
    selector, wanted, where = find_blocks(place_holder, place_block, serving_request, items)
    kv_flat = jnp.moveaxis(kv_up.reshape(rank_width, kv_up.shape[1], -1), 1, 0)
    gains = q_gain.reshape(1, -1), k_gain.reshape(1, -1)
    count_here = lax.dynamic_slice_in_dim(
        jnp.dot(selector, image_count), pool_index * requests_here, requests_here
    )
    scalars = jnp.concatenate([share.reshape(1), count_here])
    pieces = jnp.concatenate(fetch_pieces(latent_store, wanted), axis=0)
    chosen = pieces.at[where].get(mode="promise_in_bounds")
    chosen, kv_flat, scalars = tie((chosen, kv_flat, scalars))
    chosen = chosen.reshape(requests_here, -1, rank_width)
    over_heads = [chosen] + [swap(chosen, "heads", flip) for flip in range(1, heads_size)]
    parts = []
    for part in over_heads:
        parts += [part] + [swap(part, "sub", flip) for flip in range(1, sub_size)]
    part_rows = requests_here * text_rows // share_count
    shaped = queries.reshape(
        requests_here, share_count // requests_here, CHUNKS, part_rows // CHUNKS, -1
    )

    def attended(chunk):
        return attend(chunk, shaped, parts, kv_flat, *gains, scalars)

    columns = out_weight.shape[1]
    if pool_size != 4:
        outputs = []
        for chunk in range(CHUNKS):
            rows = lax.all_gather(attended(chunk), "pool", axis=0)
            mine = sum_shares(project_out([rows[i] for i in range(pool_size)], out_weight))
            mine = mine.reshape(pool_size, -1, columns)
            back = lax.all_to_all(mine, "pool", split_axis=0, concat_axis=0, tiled=True)
            outputs.append(jnp.moveaxis(back, 0, 1).reshape(-1, pool_size * columns))
        return jnp.concatenate(outputs, axis=0)

    first = attended(0)
    across0, beside0 = swap(first, "pool", 3), swap(first, "pool", 1)
    last = attended(1)
    across1, beside1 = swap(last, "pool", 3), swap(last, "pool", 1)
    own = project_out([first, last], out_weight)
    across0, beside0, own = tie((across0, beside0, own))
    second0 = second_hop(first, across0)
    own = sum_shares(own)
    pieces = project_out([beside0, across0], out_weight)
    across1, beside1, own, pieces = tie((across1, beside1, own, pieces))
    second1 = second_hop(last, across1)
    near0 = sum_shares(pieces)
    pieces = project_out([beside1, across1], out_weight)
    second0, near0, pieces = tie((second0, near0, pieces))
    half = near0.shape[0] // 2
    back0 = swap(near0[:half], "pool", 1), swap(near0[half:], "pool", 3)
    near1 = sum_shares(pieces)
    pieces = project_out([second0], out_weight)
    second1, near1, pieces, back0 = tie((second1, near1, pieces, back0))
    back1 = swap(near1[:half], "pool", 1), swap(near1[half:], "pool", 3)
    back_second0 = swap(sum_shares(pieces), "pool", 2)
    far1 = sum_shares(project_out([second1], out_weight))
    back1, back_second0, far1 = tie((back1, back_second0, far1))
    back_second1 = swap(far1, "pool", 2)
    backs = [
        [own[:half], back0[0], back_second0, back0[1]],
        [own[half:], back1[0], back_second1, back1[1]],
    ]
    output = jnp.zeros((part_rows, pool_size * columns), jnp.bfloat16)
    for chunk in range(CHUNKS):
        for flip in (0, 1, 3, 2):
            output = lax.dynamic_update_slice(
                output, backs[chunk][flip], (chunk * half, (pool_index ^ flip) * columns)
            )
    return output


def solution(mesh):
    in_specs = (
        P(("groups", "pool"), None, ("heads", "sub")),
        P(("groups", "pool"), None),
        P(None, ("heads", "sub"), None, None),
        P(),
        P(),
        P(("heads", "sub"), "pool"),
        P("groups", None),
        P("groups", None),
        P("groups"),
        P("groups"),
    )
    out_specs = P(("groups", "pool", "heads", "sub"), None)
    return jax.shard_map(
        per_device, mesh=mesh, in_specs=in_specs, out_specs=out_specs, check_vma=False
    )
```

```python
import functools
import math

import jax
import jax.numpy as jnp
from jax import lax
from jax.experimental import pallas as pl
from jax.experimental.pallas import tpu as pltpu
from jax.sharding import PartitionSpec as P

BLK = 128
CHUNKS = 2
LIGHT = pl.CostEstimate(flops=1, bytes_accessed=1, transcendentals=0)


def rms_scale(values, gain):
    return values * lax.rsqrt(jnp.mean(values * values, axis=-1, keepdims=True) + 1e-05) * gain


def pair_rank(holders):
    count = holders.shape[1]
    same = holders[:, :, None] == holders[:, None, :]
    earlier = jnp.arange(count)[None, :] < jnp.arange(count)[:, None]
    return jnp.sum((same & earlier[None]).astype(jnp.int32), axis=2)


def swap(values, axis, flip):
    return lax.ppermute(values, axis, [(i, i ^ flip) for i in range(lax.axis_size(axis))])


def second_hop(block, across):
    index = lax.axis_index("pool")
    at_end = (index == 0) | (index == 3)
    passed = jnp.where(at_end, block, across)
    return lax.ppermute(passed, "pool", [(0, 2), (3, 1), (1, 0), (2, 3)])


def project_kernel(block_count, share_count, share, *refs):
    blocks, weight, outs = refs[:block_count], refs[block_count], refs[block_count + 1 :]
    part_rows = blocks[0].shape[0] // share_count
    picked = []
    for flip in range(share_count):
        start = pl.multiple_of((share[0] ^ flip) * part_rows, part_rows)
        picked += [block[pl.ds(start, part_rows), :] for block in blocks]
    product = jnp.dot(
        jnp.concatenate(picked, axis=0), weight[...], preferred_element_type=jnp.float32
    )
    rows = block_count * part_rows
    for flip in range(share_count):
        outs[flip][...] = product[flip * rows : (flip + 1) * rows].astype(outs[flip].dtype)


def project_out(blocks, out_weight):
    axes = ("heads", "sub")
    share_count = lax.axis_size(axes)
    share = lax.axis_index(axes).astype(jnp.int32).reshape(1)
    depth, columns = out_weight.shape
    rows = sum(block.shape[0] for block in blocks) // share_count
    tile = min(columns, 512)
    whole = pl.BlockSpec(memory_space=pltpu.VMEM)
    return pl.pallas_call(
        functools.partial(project_kernel, len(blocks), share_count),
        grid=(columns // tile,),
        in_specs=[pl.BlockSpec(memory_space=pltpu.SMEM)]
        + [whole for _ in blocks]
        + [pl.BlockSpec((depth, tile), lambda n: (0, n))],
        out_specs=[pl.BlockSpec((rows, tile), lambda n: (0, n))] * share_count,
        out_shape=[
            jax.ShapeDtypeStruct((rows, columns), jnp.bfloat16 if flip else jnp.float32)
            for flip in range(share_count)
        ],
        compiler_params=pltpu.CompilerParams(vmem_limit_bytes=32 * 1024 * 1024),
        cost_estimate=LIGHT,
    )(share, *blocks, out_weight)


def sum_shares(pieces):
    total = pieces[0]
    for flip in range(1, len(pieces)):
        total = total + swap(pieces[flip], ("heads", "sub"), flip).astype(jnp.float32)
    return total.astype(jnp.bfloat16)


def sum_in_turn(pieces):
    sub_size = lax.axis_size("sub")
    by_sub = []
    for first in range(0, len(pieces), sub_size):
        total = pieces[first].astype(jnp.float32)
        for flip in range(1, sub_size):
            total = total + swap(pieces[first + flip], "sub", flip).astype(jnp.float32)
        by_sub.append(total)
    total = by_sub[0]
    for flip in range(1, len(by_sub)):
        total = total + swap(by_sub[flip].astype(jnp.bfloat16), "heads", flip).astype(jnp.float32)
    return total.astype(jnp.bfloat16)


def find_blocks(place_holder, place_block, serving_request, items):
    pool_size = lax.axis_size("pool")
    pool_index = lax.axis_index("pool")
    capacity = 2 * ((items + pool_size - 1) // pool_size)
    total_requests = serving_request.shape[0]
    request_ids = jnp.arange(total_requests, dtype=jnp.int32)
    selector = (serving_request[:, None] == request_ids[None, :]).astype(jnp.int32)
    holders = jnp.dot(selector, place_holder).reshape(pool_size, items)
    blocks = jnp.dot(selector, place_block).reshape(pool_size, items)
    ranks = pair_rank(holders)
    slot_ids = jnp.arange(capacity, dtype=jnp.int32)
    matched = (holders[:, None, :] == pool_index) & (ranks[:, None, :] == slot_ids[None, :, None])
    send_block = jnp.sum(jnp.where(matched, blocks[:, None, :], 0), axis=2)
    partners = jnp.arange(pool_size, dtype=jnp.int32) ^ pool_index
    wanted = send_block.at[partners].get(mode="promise_in_bounds")
    my_holders = lax.dynamic_index_in_dim(holders, pool_index, 0, keepdims=False)
    my_ranks = lax.dynamic_index_in_dim(ranks, pool_index, 0, keepdims=False)
    return selector, wanted, (my_holders ^ pool_index) * capacity + my_ranks


def fetch_pieces(latent_store, wanted):
    share_count = lax.axis_size(("heads", "sub"))
    share = lax.axis_index(("heads", "sub"))
    rows = BLK // share_count
    store = latent_store.reshape(-1, rows, latent_store.shape[1])
    outgoing = store.at[wanted.reshape(-1) * share_count + share].get(mode="promise_in_bounds")
    outgoing = outgoing.reshape(*wanted.shape, rows, -1)
    arriving = {flip: swap(outgoing[flip], "pool", flip) for flip in (*range(2, len(wanted)), 1)}
    return [outgoing[0]] + [arriving[flip] for flip in range(1, len(wanted))]


def attend_kernel(share_count, scalars, queries, *refs):
    parts, (kv_up, q_gain, k_gain, out, keys, values) = refs[:share_count], refs[share_count:]
    request = pl.program_id(0)
    head_width = q_gain.shape[1]
    text, width = out.shape
    per_group = width // head_width
    part_slots = parts[0].shape[1]
    share_rows = BLK // share_count
    count, share = scalars[1 + request], scalars[0]
    for flip in range(share_count):
        rows = pl.ds(flip * part_slots, part_slots)
        projected = jnp.dot(parts[flip][request], kv_up[...], preferred_element_type=jnp.float32)
        key = rms_scale(projected[:, :head_width], k_gain[...])
        keys[rows, :] = key.astype(jnp.bfloat16)
        slot = lax.broadcasted_iota(jnp.int32, (part_slots, head_width), 0)
        position = (slot // share_rows) * BLK + (share ^ flip) * share_rows + slot % share_rows
        live = jnp.where(position < count, 1.0, 0.0)
        values[rows, :head_width] = (projected[:, head_width:] * live).astype(jnp.bfloat16)
        values[rows, head_width:] = live.astype(jnp.bfloat16)
    scale = math.log2(math.e) / math.sqrt(head_width)
    together = min(per_group, max(1, 256 // text))
    for first in range(0, per_group, together):
        normed = []
        for head in range(first, first + together):
            query = queries[0, :, 0, :, head * head_width : (head + 1) * head_width]
            query = query.reshape(text, head_width).astype(jnp.float32)
            normed.append(rms_scale(query, q_gain[...]).astype(jnp.bfloat16))
        scores = lax.dot_general(
            jnp.concatenate(normed, axis=0),
            keys[...],
            (((1,), (1,)), ((), ())),
            preferred_element_type=jnp.float32,
        )
        expo = jnp.exp2(scores * scale).astype(jnp.bfloat16)
        total = jnp.dot(expo, values[...], preferred_element_type=jnp.float32)
        result = (total[:, :head_width] / total[:, head_width:]).astype(jnp.bfloat16)
        for i in range(together):
            head = first + i
            columns = slice(head * head_width, (head + 1) * head_width)
            out[:, columns] = result[i * text : (i + 1) * text]


def attend(chunk, queries, parts, kv_flat, q_gain, k_gain, scalars):
    requests, request_shares, _, part_rows, width = queries.shape
    heads_here, rank_width, pair_width = kv_flat.shape
    head_width = q_gain.shape[1]
    slots = len(parts) * parts[0].shape[1]
    text = request_shares * part_rows
    whole = pl.BlockSpec(memory_space=pltpu.VMEM)
    return pl.pallas_call(
        functools.partial(attend_kernel, len(parts)),
        grid=(requests, heads_here),
        in_specs=[
            pl.BlockSpec(memory_space=pltpu.SMEM),
            pl.BlockSpec(
                (1, request_shares, 1, part_rows, width // heads_here),
                lambda r, g: (r, 0, chunk, 0, g),
            ),
        ]
        + [whole for _ in parts]
        + [pl.BlockSpec((None, rank_width, pair_width), lambda r, g: (g, 0, 0)), whole, whole],
        out_specs=pl.BlockSpec((text, width // heads_here), lambda r, g: (r, g)),
        out_shape=jax.ShapeDtypeStruct((requests * text, width), jnp.bfloat16),
        scratch_shapes=[
            pltpu.VMEM((slots, head_width), jnp.bfloat16),
            pltpu.VMEM((slots, 2 * head_width), jnp.bfloat16),
        ],
        compiler_params=pltpu.CompilerParams(vmem_limit_bytes=32 * 1024 * 1024),
        cost_estimate=LIGHT,
    )(scalars, queries, *parts, kv_flat, q_gain, k_gain)


def per_device(
    queries,
    latent_store,
    kv_up,
    q_gain,
    k_gain,
    out_weight,
    place_holder,
    place_block,
    image_count,
    serving_request,
):
    pool_size = lax.axis_size("pool")
    pool_index = lax.axis_index("pool")
    heads_size = lax.axis_size("heads")
    sub_size = lax.axis_size("sub")
    share_count = heads_size * sub_size
    share = lax.axis_index(("heads", "sub"))
    requests_here, text_rows, _ = queries.shape
    blocks_each = place_holder.shape[1]
    items = requests_here * blocks_each
    rank_width = latent_store.shape[1]
    tie = lax.optimization_barrier
    selector, wanted, where = find_blocks(place_holder, place_block, serving_request, items)
    kv_flat = jnp.moveaxis(kv_up.reshape(rank_width, kv_up.shape[1], -1), 1, 0)
    gains = q_gain.reshape(1, -1), k_gain.reshape(1, -1)
    count_here = lax.dynamic_slice_in_dim(
        jnp.dot(selector, image_count), pool_index * requests_here, requests_here
    )
    scalars = jnp.concatenate([share.reshape(1), count_here])
    pieces = jnp.concatenate(fetch_pieces(latent_store, wanted), axis=0)
    chosen = pieces.at[where].get(mode="promise_in_bounds")
    chosen, kv_flat, scalars = tie((chosen, kv_flat, scalars))
    chosen = chosen.reshape(requests_here, -1, rank_width)
    over_heads = [chosen] + [swap(chosen, "heads", flip) for flip in range(1, heads_size)]
    parts = []
    for part in over_heads:
        parts += [part] + [swap(part, "sub", flip) for flip in range(1, sub_size)]
    part_rows = requests_here * text_rows // share_count
    shaped = queries.reshape(
        requests_here, share_count // requests_here, CHUNKS, part_rows // CHUNKS, -1
    )

    def attended(chunk):
        return attend(chunk, shaped, parts, kv_flat, *gains, scalars)

    columns = out_weight.shape[1]
    if pool_size != 4:
        outputs = []
        for chunk in range(CHUNKS):
            rows = lax.all_gather(attended(chunk), "pool", axis=0)
            mine = sum_shares(project_out([rows[i] for i in range(pool_size)], out_weight))
            mine = mine.reshape(pool_size, -1, columns)
            back = lax.all_to_all(mine, "pool", split_axis=0, concat_axis=0, tiled=True)
            outputs.append(jnp.moveaxis(back, 0, 1).reshape(-1, pool_size * columns))
        return jnp.concatenate(outputs, axis=0)

    first = attended(0)
    across0, beside0 = swap(first, "pool", 3), swap(first, "pool", 1)
    last = attended(1)
    across1, beside1 = swap(last, "pool", 3), swap(last, "pool", 1)
    own = project_out([first, last], out_weight)
    across0, beside0, own = tie((across0, beside0, own))
    second0 = second_hop(first, across0)
    own = sum_in_turn(own)
    near0 = sum_shares(project_out([beside0, across0], out_weight))
    across1, beside1, own, near0 = tie((across1, beside1, own, near0))
    second1 = second_hop(last, across1)
    half = near0.shape[0] // 2
    back0 = swap(near0[:half], "pool", 1), swap(near0[half:], "pool", 3)
    near1 = sum_shares(project_out([beside1, across1], out_weight))
    second0, near1, back0 = tie((second0, near1, back0))
    back1 = swap(near1[:half], "pool", 1), swap(near1[half:], "pool", 3)
    far0 = sum_shares(project_out([second0], out_weight))
    second1, far0, back1 = tie((second1, far0, back1))
    back_second0 = swap(far0, "pool", 2)
    far1 = sum_shares(project_out([second1], out_weight))
    back_second0, far1 = tie((back_second0, far1))
    back_second1 = swap(far1, "pool", 2)
    backs = [
        [own[:half], back0[0], back_second0, back0[1]],
        [own[half:], back1[0], back_second1, back1[1]],
    ]
    output = jnp.zeros((part_rows, pool_size * columns), jnp.bfloat16)
    for chunk in range(CHUNKS):
        for flip in (0, 1, 3, 2):
            output = lax.dynamic_update_slice(
                output, backs[chunk][flip], (chunk * half, (pool_index ^ flip) * columns)
            )
    return output


def solution(mesh):
    in_specs = (
        P(("groups", "pool"), None, ("heads", "sub")),
        P(("groups", "pool"), None),
        P(None, ("heads", "sub"), None, None),
        P(),
        P(),
        P(("heads", "sub"), "pool"),
        P("groups", None),
        P("groups", None),
        P("groups"),
        P("groups"),
    )
    out_specs = P(("groups", "pool", "heads", "sub"), None)
    return jax.shard_map(
        per_device, mesh=mesh, in_specs=in_specs, out_specs=out_specs, check_vma=False
    )
```

```python
import functools
import math

import jax
import jax.numpy as jnp
from jax import lax
from jax.experimental import pallas as pl
from jax.experimental.pallas import tpu as pltpu
from jax.sharding import PartitionSpec as P

BLK = 128
CHUNKS = 2
LIGHT = pl.CostEstimate(flops=1, bytes_accessed=1, transcendentals=0)


def rms_scale(values, gain):
    return values * lax.rsqrt(jnp.mean(values * values, axis=-1, keepdims=True) + 1e-05) * gain


def pair_rank(holders):
    count = holders.shape[1]
    same = holders[:, :, None] == holders[:, None, :]
    earlier = jnp.arange(count)[None, :] < jnp.arange(count)[:, None]
    return jnp.sum((same & earlier[None]).astype(jnp.int32), axis=2)


def swap(values, axis, flip):
    return lax.ppermute(values, axis, [(i, i ^ flip) for i in range(lax.axis_size(axis))])


def second_hop(block, across):
    index = lax.axis_index("pool")
    at_end = (index == 0) | (index == 3)
    passed = jnp.where(at_end, block, across)
    return lax.ppermute(passed, "pool", [(0, 2), (3, 1), (1, 0), (2, 3)])


def project_kernel(widths, share_count, share, *refs):
    count = sum(widths)
    parts, weight, outs = list(refs[:count]), refs[count], refs[count + 1 :]
    part_rows = parts[0].shape[0] // share_count
    blocks = [[parts.pop(0) for _ in range(width)] for width in widths]
    picked = []
    for flip in range(share_count):
        start = pl.multiple_of((share[0] ^ flip) * part_rows, part_rows)
        for block in blocks:
            pieces = [part[pl.ds(start, part_rows), :] for part in block]
            picked.append(jnp.concatenate(pieces, axis=1) if len(pieces) > 1 else pieces[0])
    product = jnp.dot(
        jnp.concatenate(picked, axis=0), weight[...], preferred_element_type=jnp.float32
    )
    rows = len(blocks) * part_rows
    for flip in range(share_count):
        outs[flip][...] = product[flip * rows : (flip + 1) * rows].astype(outs[flip].dtype)


def project_out(blocks, out_weight):
    axes = ("heads", "sub")
    share_count = lax.axis_size(axes)
    share = lax.axis_index(axes).astype(jnp.int32).reshape(1)
    depth, columns = out_weight.shape
    parts = [part for block in blocks for part in block]
    rows = len(blocks) * parts[0].shape[0] // share_count
    tile = min(columns, 512)
    whole = pl.BlockSpec(memory_space=pltpu.VMEM)
    return pl.pallas_call(
        functools.partial(project_kernel, [len(block) for block in blocks], share_count),
        grid=(columns // tile,),
        in_specs=[pl.BlockSpec(memory_space=pltpu.SMEM)]
        + [whole for _ in parts]
        + [pl.BlockSpec((depth, tile), lambda n: (0, n))],
        out_specs=[pl.BlockSpec((rows, tile), lambda n: (0, n))] * share_count,
        out_shape=[
            jax.ShapeDtypeStruct((rows, columns), jnp.bfloat16 if flip else jnp.float32)
            for flip in range(share_count)
        ],
        compiler_params=pltpu.CompilerParams(vmem_limit_bytes=32 * 1024 * 1024),
        cost_estimate=LIGHT,
    )(share, *parts, out_weight)


def sum_shares(pieces):
    total = pieces[0]
    for flip in range(1, len(pieces)):
        total = total + swap(pieces[flip], ("heads", "sub"), flip).astype(jnp.float32)
    return total.astype(jnp.bfloat16)


def sum_in_turn(pieces):
    sub_size = lax.axis_size("sub")
    by_sub = []
    for first in range(0, len(pieces), sub_size):
        total = pieces[first].astype(jnp.float32)
        for flip in range(1, sub_size):
            total = total + swap(pieces[first + flip], "sub", flip).astype(jnp.float32)
        by_sub.append(total)
    total = by_sub[0]
    for flip in range(1, len(by_sub)):
        total = total + swap(by_sub[flip].astype(jnp.bfloat16), "heads", flip).astype(jnp.float32)
    return total.astype(jnp.bfloat16)


def find_blocks(place_holder, place_block, serving_request, items):
    pool_size = lax.axis_size("pool")
    pool_index = lax.axis_index("pool")
    capacity = 2 * ((items + pool_size - 1) // pool_size)
    total_requests = serving_request.shape[0]
    request_ids = jnp.arange(total_requests, dtype=jnp.int32)
    selector = (serving_request[:, None] == request_ids[None, :]).astype(jnp.int32)
    holders = jnp.dot(selector, place_holder).reshape(pool_size, items)
    blocks = jnp.dot(selector, place_block).reshape(pool_size, items)
    ranks = pair_rank(holders)
    slot_ids = jnp.arange(capacity, dtype=jnp.int32)
    matched = (holders[:, None, :] == pool_index) & (ranks[:, None, :] == slot_ids[None, :, None])
    send_block = jnp.sum(jnp.where(matched, blocks[:, None, :], 0), axis=2)
    partners = jnp.arange(pool_size, dtype=jnp.int32) ^ pool_index
    wanted = send_block.at[partners].get(mode="promise_in_bounds")
    my_holders = lax.dynamic_index_in_dim(holders, pool_index, 0, keepdims=False)
    my_ranks = lax.dynamic_index_in_dim(ranks, pool_index, 0, keepdims=False)
    return selector, wanted, (my_holders ^ pool_index) * capacity + my_ranks


def fetch_pieces(latent_store, wanted):
    share_count = lax.axis_size(("heads", "sub"))
    share = lax.axis_index(("heads", "sub"))
    rows = BLK // share_count
    store = latent_store.reshape(-1, rows, latent_store.shape[1])
    outgoing = store.at[wanted.reshape(-1) * share_count + share].get(mode="promise_in_bounds")
    outgoing = outgoing.reshape(*wanted.shape, rows, -1)
    arriving = {flip: swap(outgoing[flip], "pool", flip) for flip in (*range(2, len(wanted)), 1)}
    return [outgoing[0]] + [arriving[flip] for flip in range(1, len(wanted))]


def attend_kernel(share_count, scalars, queries, *refs):
    parts, (kv_up, q_gain, k_gain, out, keys, values) = refs[:share_count], refs[share_count:]
    request = pl.program_id(0)
    head_width = q_gain.shape[1]
    text, width = out.shape
    per_group = width // head_width
    part_slots = parts[0].shape[1]
    share_rows = BLK // share_count
    count, share = scalars[1 + request], scalars[0]
    for flip in range(share_count):
        rows = pl.ds(flip * part_slots, part_slots)
        projected = jnp.dot(parts[flip][request], kv_up[...], preferred_element_type=jnp.float32)
        key = rms_scale(projected[:, :head_width], k_gain[...])
        keys[rows, :] = key.astype(jnp.bfloat16)
        slot = lax.broadcasted_iota(jnp.int32, (part_slots, head_width), 0)
        position = (slot // share_rows) * BLK + (share ^ flip) * share_rows + slot % share_rows
        live = jnp.where(position < count, 1.0, 0.0)
        values[rows, :head_width] = (projected[:, head_width:] * live).astype(jnp.bfloat16)
        values[rows, head_width:] = live.astype(jnp.bfloat16)
    scale = math.log2(math.e) / math.sqrt(head_width)
    together = min(per_group, max(1, 256 // text))
    for first in range(0, per_group, together):
        normed = []
        for head in range(first, first + together):
            query = queries[0, :, 0, :, head * head_width : (head + 1) * head_width]
            query = query.reshape(text, head_width).astype(jnp.float32)
            normed.append(rms_scale(query, q_gain[...]).astype(jnp.bfloat16))
        scores = lax.dot_general(
            jnp.concatenate(normed, axis=0),
            keys[...],
            (((1,), (1,)), ((), ())),
            preferred_element_type=jnp.float32,
        )
        expo = jnp.exp2(scores * scale).astype(jnp.bfloat16)
        total = jnp.dot(expo, values[...], preferred_element_type=jnp.float32)
        result = (total[:, :head_width] / total[:, head_width:]).astype(jnp.bfloat16)
        for i in range(together):
            head = first + i
            columns = slice(head * head_width, (head + 1) * head_width)
            out[:, columns] = result[i * text : (i + 1) * text]


def attend(chunk, queries, parts, kv_flat, q_gain, k_gain, scalars):
    requests, request_shares, _, part_rows, width = queries.shape
    heads_here, rank_width, pair_width = kv_flat.shape
    head_width = q_gain.shape[1]
    slots = len(parts) * parts[0].shape[1]
    text = request_shares * part_rows
    whole = pl.BlockSpec(memory_space=pltpu.VMEM)
    return pl.pallas_call(
        functools.partial(attend_kernel, len(parts)),
        grid=(requests, heads_here),
        in_specs=[
            pl.BlockSpec(memory_space=pltpu.SMEM),
            pl.BlockSpec(
                (1, request_shares, 1, part_rows, width // heads_here),
                lambda r, g: (r, 0, chunk, 0, g),
            ),
        ]
        + [whole for _ in parts]
        + [pl.BlockSpec((None, rank_width, pair_width), lambda r, g: (g, 0, 0)), whole, whole],
        out_specs=pl.BlockSpec((text, width // heads_here), lambda r, g: (r, g)),
        out_shape=jax.ShapeDtypeStruct((requests * text, width), jnp.bfloat16),
        scratch_shapes=[
            pltpu.VMEM((slots, head_width), jnp.bfloat16),
            pltpu.VMEM((slots, 2 * head_width), jnp.bfloat16),
        ],
        compiler_params=pltpu.CompilerParams(vmem_limit_bytes=32 * 1024 * 1024),
        cost_estimate=LIGHT,
    )(scalars, queries, *parts, kv_flat, q_gain, k_gain)


def per_device(
    queries,
    latent_store,
    kv_up,
    q_gain,
    k_gain,
    out_weight,
    place_holder,
    place_block,
    image_count,
    serving_request,
):
    pool_size = lax.axis_size("pool")
    pool_index = lax.axis_index("pool")
    heads_size = lax.axis_size("heads")
    sub_size = lax.axis_size("sub")
    share_count = heads_size * sub_size
    share = lax.axis_index(("heads", "sub"))
    requests_here, text_rows, _ = queries.shape
    blocks_each = place_holder.shape[1]
    items = requests_here * blocks_each
    rank_width = latent_store.shape[1]
    tie = lax.optimization_barrier
    selector, wanted, where = find_blocks(place_holder, place_block, serving_request, items)
    kv_flat = jnp.moveaxis(kv_up.reshape(rank_width, kv_up.shape[1], -1), 1, 0)
    gains = q_gain.reshape(1, -1), k_gain.reshape(1, -1)
    count_here = lax.dynamic_slice_in_dim(
        jnp.dot(selector, image_count), pool_index * requests_here, requests_here
    )
    scalars = jnp.concatenate([share.reshape(1), count_here])
    pieces = jnp.concatenate(fetch_pieces(latent_store, wanted), axis=0)
    chosen = pieces.at[where].get(mode="promise_in_bounds")
    chosen, kv_flat, scalars = tie((chosen, kv_flat, scalars))
    chosen = chosen.reshape(requests_here, -1, rank_width)
    over_heads = [chosen] + [swap(chosen, "heads", flip) for flip in range(1, heads_size)]
    parts = []
    for part in over_heads:
        parts += [part] + [swap(part, "sub", flip) for flip in range(1, sub_size)]
    part_rows = requests_here * text_rows // share_count
    shaped = queries.reshape(
        requests_here, share_count // requests_here, CHUNKS, part_rows // CHUNKS, -1
    )

    def attended(chunk):
        return attend(chunk, shaped, parts, kv_flat, *gains, scalars)

    columns = out_weight.shape[1]
    if pool_size != 4:
        outputs = []
        for chunk in range(CHUNKS):
            rows = lax.all_gather(attended(chunk), "pool", axis=0)
            mine = sum_shares(project_out([[rows[i]] for i in range(pool_size)], out_weight))
            mine = mine.reshape(pool_size, -1, columns)
            back = lax.all_to_all(mine, "pool", split_axis=0, concat_axis=0, tiled=True)
            outputs.append(jnp.moveaxis(back, 0, 1).reshape(-1, pool_size * columns))
        return jnp.concatenate(outputs, axis=0)

    first = attended(0)
    across0, beside0 = swap(first, "pool", 3), swap(first, "pool", 1)
    last = attended(1)
    across1, beside1 = swap(last, "pool", 3), swap(last, "pool", 1)
    own = project_out([[first], [last]], out_weight)
    across0, beside0, own = tie((across0, beside0, own))
    second0 = second_hop(first, across0)
    near0 = sum_shares(project_out([[beside0], [across0]], out_weight))
    across1, beside1, near0 = tie((across1, beside1, near0))
    width = last.shape[1] // 2
    second1 = [
        second_hop(last[:, i : i + width], across1[:, i : i + width]) for i in (0, width)
    ]
    half = near0.shape[0] // 2
    back0 = swap(near0[:half], "pool", 1), swap(near0[half:], "pool", 3)
    near1 = sum_shares(project_out([[beside1], [across1]], out_weight))
    second0, second1[0], near1, back0 = tie((second0, second1[0], near1, back0))
    back1 = swap(near1[:half], "pool", 1), swap(near1[half:], "pool", 3)
    far0 = sum_shares(project_out([[second0]], out_weight))
    second1, far0, back1 = tie((second1, far0, back1))
    back_second0 = swap(far0, "pool", 2)
    far1 = sum_shares(project_out([second1], out_weight))
    back_second0, far1 = tie((back_second0, far1))
    back_second1 = swap(far1, "pool", 2)
    own = sum_in_turn(own)
    backs = [(0, 1, back0[0]), (0, 3, back0[1]), (1, 1, back1[0]), (1, 3, back1[1])]
    backs += [(0, 2, back_second0), (0, 0, own), (1, 2, back_second1)]
    output = jnp.zeros((part_rows, pool_size * columns), jnp.bfloat16)
    for chunk, flip, block in backs:
        output = lax.dynamic_update_slice(
            output, block, (chunk * half, (pool_index ^ flip) * columns)
        )
    return output


def solution(mesh):
    in_specs = (
        P(("groups", "pool"), None, ("heads", "sub")),
        P(("groups", "pool"), None),
        P(None, ("heads", "sub"), None, None),
        P(),
        P(),
        P(("heads", "sub"), "pool"),
        P("groups", None),
        P("groups", None),
        P("groups"),
        P("groups"),
    )
    out_specs = P(("groups", "pool", "heads", "sub"), None)
    return jax.shard_map(
        per_device, mesh=mesh, in_specs=in_specs, out_specs=out_specs, check_vma=False
    )
```

```python
import functools
import math

import jax
import jax.numpy as jnp
from jax import lax
from jax.experimental import pallas as pl
from jax.experimental.pallas import tpu as pltpu
from jax.sharding import PartitionSpec as P

BLK = 128
LIGHT = pl.CostEstimate(flops=1, bytes_accessed=1, transcendentals=0)


def rms_scale(values, gain):
    return values * lax.rsqrt(jnp.mean(values * values, axis=-1, keepdims=True) + 1e-05) * gain


def pair_rank(holders):
    count = holders.shape[1]
    same = holders[:, :, None] == holders[:, None, :]
    earlier = jnp.arange(count)[None, :] < jnp.arange(count)[:, None]
    return jnp.sum((same & earlier[None]).astype(jnp.int32), axis=2)


def swap(values, axis, flip):
    return lax.ppermute(values, axis, [(i, i ^ flip) for i in range(lax.axis_size(axis))])


def second_hop(block, across):
    index = lax.axis_index("pool")
    at_end = (index == 0) | (index == 3)
    passed = jnp.where(at_end, block, across)
    return lax.ppermute(passed, "pool", [(0, 2), (3, 1), (1, 0), (2, 3)])


def project_kernel(block_count, share_count, share, *refs):
    blocks, weight, outs = refs[:block_count], refs[block_count], refs[block_count + 1 :]
    picked = []
    for flip in range(share_count):
        for block in blocks:
            part_rows = block.shape[0] // share_count
            start = pl.multiple_of((share[0] ^ flip) * part_rows, part_rows)
            picked.append(block[pl.ds(start, part_rows), :])
    product = jnp.dot(
        jnp.concatenate(picked, axis=0), weight[...], preferred_element_type=jnp.float32
    )
    rows = product.shape[0] // share_count
    for flip in range(share_count):
        outs[flip][...] = product[flip * rows : (flip + 1) * rows].astype(outs[flip].dtype)


def project_out(blocks, out_weight):
    axes = ("heads", "sub")
    share_count = lax.axis_size(axes)
    share = lax.axis_index(axes).astype(jnp.int32).reshape(1)
    depth, columns = out_weight.shape
    rows = sum(block.shape[0] for block in blocks) // share_count
    tile = min(columns, 512)
    whole = pl.BlockSpec(memory_space=pltpu.VMEM)
    return pl.pallas_call(
        functools.partial(project_kernel, len(blocks), share_count),
        grid=(columns // tile,),
        in_specs=[pl.BlockSpec(memory_space=pltpu.SMEM)]
        + [whole for _ in blocks]
        + [pl.BlockSpec((depth, tile), lambda n: (0, n))],
        out_specs=[pl.BlockSpec((rows, tile), lambda n: (0, n))] * share_count,
        out_shape=[
            jax.ShapeDtypeStruct((rows, columns), jnp.bfloat16 if flip else jnp.float32)
            for flip in range(share_count)
        ],
        compiler_params=pltpu.CompilerParams(vmem_limit_bytes=32 * 1024 * 1024),
        cost_estimate=LIGHT,
    )(share, *blocks, out_weight)


def send_shares(pieces):
    axes = ("heads", "sub")
    return [pieces[0]] + [swap(pieces[flip], axes, flip) for flip in range(1, len(pieces))]


def add_shares(pieces):
    return sum(piece.astype(jnp.float32) for piece in pieces).astype(jnp.bfloat16)


def sum_in_turn(pieces):
    sub_size = lax.axis_size("sub")
    by_sub = []
    for first in range(0, len(pieces), sub_size):
        total = pieces[first].astype(jnp.float32)
        for flip in range(1, sub_size):
            total = total + swap(pieces[first + flip], "sub", flip).astype(jnp.float32)
        by_sub.append(total)
    total = by_sub[0]
    for flip in range(1, len(by_sub)):
        total = total + swap(by_sub[flip].astype(jnp.bfloat16), "heads", flip).astype(jnp.float32)
    return total.astype(jnp.bfloat16)


def find_blocks(place_holder, place_block, serving_request, items):
    pool_size = lax.axis_size("pool")
    pool_index = lax.axis_index("pool")
    capacity = 2 * ((items + pool_size - 1) // pool_size)
    total_requests = serving_request.shape[0]
    request_ids = jnp.arange(total_requests, dtype=jnp.int32)
    selector = (serving_request[:, None] == request_ids[None, :]).astype(jnp.int32)
    holders = jnp.dot(selector, place_holder).reshape(pool_size, items)
    blocks = jnp.dot(selector, place_block).reshape(pool_size, items)
    ranks = pair_rank(holders)
    slot_ids = jnp.arange(capacity, dtype=jnp.int32)
    matched = (holders[:, None, :] == pool_index) & (ranks[:, None, :] == slot_ids[None, :, None])
    send_block = jnp.sum(jnp.where(matched, blocks[:, None, :], 0), axis=2)
    partners = jnp.arange(pool_size, dtype=jnp.int32) ^ pool_index
    wanted = send_block.at[partners].get(mode="promise_in_bounds")
    my_holders = lax.dynamic_index_in_dim(holders, pool_index, 0, keepdims=False)
    my_ranks = lax.dynamic_index_in_dim(ranks, pool_index, 0, keepdims=False)
    return selector, wanted, (my_holders ^ pool_index) * capacity + my_ranks


def fetch_pieces(latent_store, wanted):
    share_count = lax.axis_size(("heads", "sub"))
    share = lax.axis_index(("heads", "sub"))
    rows = BLK // share_count
    store = latent_store.reshape(-1, rows, latent_store.shape[1])
    outgoing = store.at[wanted.reshape(-1) * share_count + share].get(mode="promise_in_bounds")
    outgoing = outgoing.reshape(*wanted.shape, rows, -1)
    arriving = {flip: swap(outgoing[flip], "pool", flip) for flip in (*range(2, len(wanted)), 1)}
    return [outgoing[0]] + [arriving[flip] for flip in range(1, len(wanted))]


def attend_kernel(share_count, scalars, queries, *refs):
    parts, (kv_up, q_gain, k_gain, out, keys, values) = refs[:share_count], refs[share_count:]
    request = pl.program_id(0)
    head_width = q_gain.shape[1]
    text, width = out.shape
    per_group = width // head_width
    part_slots = parts[0].shape[1]
    share_rows = BLK // share_count
    count, share = scalars[1 + request], scalars[0]
    for flip in range(share_count):
        rows = pl.ds(flip * part_slots, part_slots)
        projected = jnp.dot(parts[flip][request], kv_up[...], preferred_element_type=jnp.float32)
        key = rms_scale(projected[:, :head_width], k_gain[...])
        keys[rows, :] = key.astype(jnp.bfloat16)
        slot = lax.broadcasted_iota(jnp.int32, (part_slots, head_width), 0)
        position = (slot // share_rows) * BLK + (share ^ flip) * share_rows + slot % share_rows
        live = jnp.where(position < count, 1.0, 0.0)
        values[rows, :head_width] = (projected[:, head_width:] * live).astype(jnp.bfloat16)
        values[rows, head_width:] = live.astype(jnp.bfloat16)
    scale = math.log2(math.e) / math.sqrt(head_width)
    together = min(per_group, max(1, 256 // text))
    for first in range(0, per_group, together):
        normed = []
        for head in range(first, first + together):
            query = queries[0, :, :, head * head_width : (head + 1) * head_width]
            query = query.reshape(text, head_width).astype(jnp.float32)
            normed.append(rms_scale(query, q_gain[...]).astype(jnp.bfloat16))
        scores = lax.dot_general(
            jnp.concatenate(normed, axis=0),
            keys[...],
            (((1,), (1,)), ((), ())),
            preferred_element_type=jnp.float32,
        )
        expo = jnp.exp2(scores * scale).astype(jnp.bfloat16)
        total = jnp.dot(expo, values[...], preferred_element_type=jnp.float32)
        result = (total[:, :head_width] / total[:, head_width:]).astype(jnp.bfloat16)
        for i in range(together):
            head = first + i
            columns = slice(head * head_width, (head + 1) * head_width)
            out[:, columns] = result[i * text : (i + 1) * text]


def attend(chunk, rows, queries, parts, kv_flat, q_gain, k_gain, scalars):
    requests, request_shares, _, width = queries.shape
    heads_here, rank_width, pair_width = kv_flat.shape
    head_width = q_gain.shape[1]
    slots = len(parts) * parts[0].shape[1]
    text = request_shares * rows
    whole = pl.BlockSpec(memory_space=pltpu.VMEM)
    return pl.pallas_call(
        functools.partial(attend_kernel, len(parts)),
        grid=(requests, heads_here),
        in_specs=[
            pl.BlockSpec(memory_space=pltpu.SMEM),
            pl.BlockSpec(
                (1, request_shares, rows, width // heads_here),
                lambda r, g: (r, 0, chunk, g),
            ),
        ]
        + [whole for _ in parts]
        + [pl.BlockSpec((None, rank_width, pair_width), lambda r, g: (g, 0, 0)), whole, whole],
        out_specs=pl.BlockSpec((text, width // heads_here), lambda r, g: (r, g)),
        out_shape=jax.ShapeDtypeStruct((requests * text, width), jnp.bfloat16),
        scratch_shapes=[
            pltpu.VMEM((slots, head_width), jnp.bfloat16),
            pltpu.VMEM((slots, 2 * head_width), jnp.bfloat16),
        ],
        compiler_params=pltpu.CompilerParams(vmem_limit_bytes=32 * 1024 * 1024),
        cost_estimate=LIGHT,
    )(scalars, queries, *parts, kv_flat, q_gain, k_gain)


def per_device(
    queries,
    latent_store,
    kv_up,
    q_gain,
    k_gain,
    out_weight,
    place_holder,
    place_block,
    image_count,
    serving_request,
):
    pool_size = lax.axis_size("pool")
    pool_index = lax.axis_index("pool")
    heads_size = lax.axis_size("heads")
    sub_size = lax.axis_size("sub")
    share_count = heads_size * sub_size
    share = lax.axis_index(("heads", "sub"))
    requests_here, text_rows, _ = queries.shape
    blocks_each = place_holder.shape[1]
    items = requests_here * blocks_each
    rank_width = latent_store.shape[1]
    tie = lax.optimization_barrier
    selector, wanted, where = find_blocks(place_holder, place_block, serving_request, items)
    kv_flat = jnp.moveaxis(kv_up.reshape(rank_width, kv_up.shape[1], -1), 1, 0)
    gains = q_gain.reshape(1, -1), k_gain.reshape(1, -1)
    count_here = lax.dynamic_slice_in_dim(
        jnp.dot(selector, image_count), pool_index * requests_here, requests_here
    )
    scalars = jnp.concatenate([share.reshape(1), count_here])
    pieces = jnp.concatenate(fetch_pieces(latent_store, wanted), axis=0)
    chosen = pieces.at[where].get(mode="promise_in_bounds")
    chosen, kv_flat, scalars = tie((chosen, kv_flat, scalars))
    chosen = chosen.reshape(requests_here, -1, rank_width)
    over_heads = [chosen] + [swap(chosen, "heads", flip) for flip in range(1, heads_size)]
    parts = []
    for part in over_heads:
        parts += [part] + [swap(part, "sub", flip) for flip in range(1, sub_size)]
    part_rows = requests_here * text_rows // share_count
    shaped = queries.reshape(requests_here, share_count // requests_here, part_rows, -1)
    few = part_rows // 2
    chunk_rows = part_rows - few, few

    def attended(chunk):
        rows = chunk_rows[chunk]
        start = sum(chunk_rows[:chunk]) // rows
        return attend(start, rows, shaped, parts, kv_flat, *gains, scalars)

    columns = out_weight.shape[1]
    if pool_size != 4:
        outputs = []
        for chunk in range(len(chunk_rows)):
            rows = lax.all_gather(attended(chunk), "pool", axis=0)
            mine = add_shares(send_shares(project_out([rows[i] for i in range(pool_size)], out_weight)))
            mine = mine.reshape(pool_size, -1, columns)
            back = lax.all_to_all(mine, "pool", split_axis=0, concat_axis=0, tiled=True)
            outputs.append(jnp.moveaxis(back, 0, 1).reshape(-1, pool_size * columns))
        return jnp.concatenate(outputs, axis=0)

    first = attended(0)
    across0, beside0 = swap(first, "pool", 3), swap(first, "pool", 1)
    last = attended(1)
    across1, beside1 = swap(last, "pool", 3), swap(last, "pool", 1)
    own = project_out([first, last], out_weight)
    across0, beside0, own = tie((across0, beside0, own))
    second0 = second_hop(first, across0)
    near0 = send_shares(project_out([beside0, across0], out_weight))
    across1, beside1, near0 = tie((across1, beside1, near0))
    second1 = second_hop(last, across1)
    many, few = chunk_rows
    near0 = add_shares(near0)
    back0 = swap(near0[:many], "pool", 1), swap(near0[many:], "pool", 3)
    near1 = send_shares(project_out([beside1, across1], out_weight))
    second0, near1, back0 = tie((second0, near1, back0))
    far0 = send_shares(project_out([second0], out_weight))
    near1 = add_shares(near1)
    back1 = swap(near1[:few], "pool", 1), swap(near1[few:], "pool", 3)
    second1, far0, back1 = tie((second1, far0, back1))
    back_second0 = swap(add_shares(far0), "pool", 2)
    far1 = send_shares(project_out([second1], out_weight))
    back_second0, far1 = tie((back_second0, far1))
    back_second1 = swap(add_shares(far1), "pool", 2)
    own = sum_in_turn(own)
    backs = [(0, 1, back0[0]), (0, 3, back0[1]), (many, 1, back1[0]), (many, 3, back1[1])]
    backs += [(0, 2, back_second0), (0, 0, own), (many, 2, back_second1)]
    output = jnp.zeros((part_rows, pool_size * columns), jnp.bfloat16)
    for row, flip, block in backs:
        output = lax.dynamic_update_slice(output, block, (row, (pool_index ^ flip) * columns))
    return output


def solution(mesh):
    in_specs = (
        P(("groups", "pool"), None, ("heads", "sub")),
        P(("groups", "pool"), None),
        P(None, ("heads", "sub"), None, None),
        P(),
        P(),
        P(("heads", "sub"), "pool"),
        P("groups", None),
        P("groups", None),
        P("groups"),
        P("groups"),
    )
    out_specs = P(("groups", "pool", "heads", "sub"), None)
    return jax.shard_map(
        per_device, mesh=mesh, in_specs=in_specs, out_specs=out_specs, check_vma=False
    )
```

```python
import functools
import math

import jax
import jax.numpy as jnp
from jax import lax
from jax.experimental import pallas as pl
from jax.experimental.pallas import tpu as pltpu
from jax.sharding import PartitionSpec as P

BLK = 128
LIGHT = pl.CostEstimate(flops=1, bytes_accessed=1, transcendentals=0)


def rms_scale(values, gain):
    return values * lax.rsqrt(jnp.mean(values * values, axis=-1, keepdims=True) + 1e-05) * gain


def pair_rank(holders):
    count = holders.shape[1]
    same = holders[:, :, None] == holders[:, None, :]
    earlier = jnp.arange(count)[None, :] < jnp.arange(count)[:, None]
    return jnp.sum((same & earlier[None]).astype(jnp.int32), axis=2)


def swap(values, axis, flip):
    return lax.ppermute(values, axis, [(i, i ^ flip) for i in range(lax.axis_size(axis))])


def second_hop(block, across):
    index = lax.axis_index("pool")
    at_end = (index == 0) | (index == 3)
    passed = jnp.where(at_end, block, across)
    return lax.ppermute(passed, "pool", [(0, 2), (3, 1), (1, 0), (2, 3)])


def project_kernel(block_count, flips, share, *refs):
    blocks, weight, outs = refs[:block_count], refs[block_count], refs[block_count + 1 :]
    picked = []
    for flip in flips:
        for block in blocks:
            part_rows = block.shape[0] // len(flips)
            start = pl.multiple_of((share[0] ^ flip) * part_rows, part_rows)
            picked.append(block[pl.ds(start, part_rows), :])
    product = jnp.dot(
        jnp.concatenate(picked, axis=0), weight[...], preferred_element_type=jnp.float32
    )
    rows = product.shape[0] // len(outs)
    for i, out in enumerate(outs):
        out[...] = product[i * rows : (i + 1) * rows].astype(out.dtype)


def project_out(blocks, out_weight, direct=False):
    axes = ("heads", "sub")
    share_count = lax.axis_size(axes)
    share = lax.axis_index(axes).astype(jnp.int32).reshape(1)
    depth, columns = out_weight.shape
    flips = [*range(0, share_count, 2), *range(1, share_count, 2)]
    count = share_count if direct else 2
    rows = sum(block.shape[0] for block in blocks) // count
    tile = min(columns, 512)
    whole = pl.BlockSpec(memory_space=pltpu.VMEM)
    return pl.pallas_call(
        functools.partial(
            project_kernel, len(blocks), list(range(share_count)) if direct else flips
        ),
        grid=(columns // tile,),
        in_specs=[pl.BlockSpec(memory_space=pltpu.SMEM)]
        + [whole for _ in blocks]
        + [pl.BlockSpec((depth, tile), lambda n: (0, n))],
        out_specs=[pl.BlockSpec((rows, tile), lambda n: (0, n))] * count,
        out_shape=[
            jax.ShapeDtypeStruct((rows, columns), jnp.bfloat16 if i else jnp.float32)
            for i in range(count)
        ],
        compiler_params=pltpu.CompilerParams(vmem_limit_bytes=32 * 1024 * 1024),
        cost_estimate=LIGHT,
    )(share, *blocks, out_weight)


def send_direct(pieces):
    axes = ("heads", "sub")
    return [pieces[0]] + [swap(pieces[flip], axes, flip) for flip in range(1, len(pieces))]


def add_direct(pieces):
    return sum(piece.astype(jnp.float32) for piece in pieces).astype(jnp.bfloat16)


def send_sub(pieces):
    keep, away = pieces
    return keep, swap(away, "sub", 1)


def send_heads(pieces):
    keep, got = pieces
    heads_size = lax.axis_size("heads")
    rows = keep.shape[0] // heads_size
    received = []
    for flip in range(1, heads_size):
        part = slice(flip * rows, (flip + 1) * rows)
        both = keep[part] + got[part].astype(jnp.float32)
        received.append(swap(both.astype(jnp.bfloat16), "heads", flip))
    return keep, got, received


def add_shares(pieces):
    keep, got, received = pieces
    rows = keep.shape[0] // (len(received) + 1)
    total = keep[:rows] + got[:rows].astype(jnp.float32)
    return sum((part.astype(jnp.float32) for part in received), total).astype(jnp.bfloat16)


def find_blocks(place_holder, place_block, serving_request, items):
    pool_size = lax.axis_size("pool")
    pool_index = lax.axis_index("pool")
    capacity = 2 * ((items + pool_size - 1) // pool_size)
    total_requests = serving_request.shape[0]
    request_ids = jnp.arange(total_requests, dtype=jnp.int32)
    selector = (serving_request[:, None] == request_ids[None, :]).astype(jnp.int32)
    holders = jnp.dot(selector, place_holder).reshape(pool_size, items)
    blocks = jnp.dot(selector, place_block).reshape(pool_size, items)
    ranks = pair_rank(holders)
    slot_ids = jnp.arange(capacity, dtype=jnp.int32)
    matched = (holders[:, None, :] == pool_index) & (ranks[:, None, :] == slot_ids[None, :, None])
    send_block = jnp.sum(jnp.where(matched, blocks[:, None, :], 0), axis=2)
    partners = jnp.arange(pool_size, dtype=jnp.int32) ^ pool_index
    wanted = send_block.at[partners].get(mode="promise_in_bounds")
    my_holders = lax.dynamic_index_in_dim(holders, pool_index, 0, keepdims=False)
    my_ranks = lax.dynamic_index_in_dim(ranks, pool_index, 0, keepdims=False)
    return selector, wanted, (my_holders ^ pool_index) * capacity + my_ranks


def fetch_pieces(latent_store, wanted):
    share_count = lax.axis_size(("heads", "sub"))
    share = lax.axis_index(("heads", "sub"))
    rows = BLK // share_count
    store = latent_store.reshape(-1, rows, latent_store.shape[1])
    outgoing = store.at[wanted.reshape(-1) * share_count + share].get(mode="promise_in_bounds")
    outgoing = outgoing.reshape(*wanted.shape, rows, -1)
    arriving = {flip: swap(outgoing[flip], "pool", flip) for flip in (*range(2, len(wanted)), 1)}
    return [outgoing[0]] + [arriving[flip] for flip in range(1, len(wanted))]


def attend_kernel(share_count, scalars, queries, *refs):
    parts, (kv_up, q_gain, k_gain, out, keys, values) = refs[:share_count], refs[share_count:]
    request = pl.program_id(0)
    head_width = q_gain.shape[1]
    text, width = out.shape
    per_group = width // head_width
    part_slots = parts[0].shape[1]
    share_rows = BLK // share_count
    count, share = scalars[1 + request], scalars[0]
    for flip in range(share_count):
        rows = pl.ds(flip * part_slots, part_slots)
        projected = jnp.dot(parts[flip][request], kv_up[...], preferred_element_type=jnp.float32)
        key = rms_scale(projected[:, :head_width], k_gain[...])
        keys[rows, :] = key.astype(jnp.bfloat16)
        slot = lax.broadcasted_iota(jnp.int32, (part_slots, head_width), 0)
        position = (slot // share_rows) * BLK + (share ^ flip) * share_rows + slot % share_rows
        live = jnp.where(position < count, 1.0, 0.0)
        values[rows, :head_width] = (projected[:, head_width:] * live).astype(jnp.bfloat16)
        values[rows, head_width:] = live.astype(jnp.bfloat16)
    scale = math.log2(math.e) / math.sqrt(head_width)
    together = min(per_group, max(1, 256 // text))
    for first in range(0, per_group, together):
        normed = []
        for head in range(first, first + together):
            query = queries[0, :, :, head * head_width : (head + 1) * head_width]
            query = query.reshape(text, head_width).astype(jnp.float32)
            normed.append(rms_scale(query, q_gain[...]).astype(jnp.bfloat16))
        scores = lax.dot_general(
            jnp.concatenate(normed, axis=0),
            keys[...],
            (((1,), (1,)), ((), ())),
            preferred_element_type=jnp.float32,
        )
        expo = jnp.exp2(scores * scale).astype(jnp.bfloat16)
        total = jnp.dot(expo, values[...], preferred_element_type=jnp.float32)
        result = (total[:, :head_width] / total[:, head_width:]).astype(jnp.bfloat16)
        for i in range(together):
            head = first + i
            columns = slice(head * head_width, (head + 1) * head_width)
            out[:, columns] = result[i * text : (i + 1) * text]


def attend(chunk, rows, queries, parts, kv_flat, q_gain, k_gain, scalars):
    requests, request_shares, _, width = queries.shape
    heads_here, rank_width, pair_width = kv_flat.shape
    head_width = q_gain.shape[1]
    slots = len(parts) * parts[0].shape[1]
    text = request_shares * rows
    whole = pl.BlockSpec(memory_space=pltpu.VMEM)
    return pl.pallas_call(
        functools.partial(attend_kernel, len(parts)),
        grid=(requests, heads_here),
        in_specs=[
            pl.BlockSpec(memory_space=pltpu.SMEM),
            pl.BlockSpec(
                (1, request_shares, rows, width // heads_here),
                lambda r, g: (r, 0, chunk, g),
            ),
        ]
        + [whole for _ in parts]
        + [pl.BlockSpec((None, rank_width, pair_width), lambda r, g: (g, 0, 0)), whole, whole],
        out_specs=pl.BlockSpec((text, width // heads_here), lambda r, g: (r, g)),
        out_shape=jax.ShapeDtypeStruct((requests * text, width), jnp.bfloat16),
        scratch_shapes=[
            pltpu.VMEM((slots, head_width), jnp.bfloat16),
            pltpu.VMEM((slots, 2 * head_width), jnp.bfloat16),
        ],
        compiler_params=pltpu.CompilerParams(vmem_limit_bytes=32 * 1024 * 1024),
        cost_estimate=LIGHT,
    )(scalars, queries, *parts, kv_flat, q_gain, k_gain)


def per_device(
    queries,
    latent_store,
    kv_up,
    q_gain,
    k_gain,
    out_weight,
    place_holder,
    place_block,
    image_count,
    serving_request,
):
    pool_size = lax.axis_size("pool")
    pool_index = lax.axis_index("pool")
    heads_size = lax.axis_size("heads")
    sub_size = lax.axis_size("sub")
    share_count = heads_size * sub_size
    share = lax.axis_index(("heads", "sub"))
    requests_here, text_rows, _ = queries.shape
    blocks_each = place_holder.shape[1]
    items = requests_here * blocks_each
    rank_width = latent_store.shape[1]
    tie = lax.optimization_barrier
    selector, wanted, where = find_blocks(place_holder, place_block, serving_request, items)
    kv_flat = jnp.moveaxis(kv_up.reshape(rank_width, kv_up.shape[1], -1), 1, 0)
    gains = q_gain.reshape(1, -1), k_gain.reshape(1, -1)
    count_here = lax.dynamic_slice_in_dim(
        jnp.dot(selector, image_count), pool_index * requests_here, requests_here
    )
    scalars = jnp.concatenate([share.reshape(1), count_here])
    pieces = jnp.concatenate(fetch_pieces(latent_store, wanted), axis=0)
    chosen = pieces.at[where].get(mode="promise_in_bounds")
    chosen, kv_flat, scalars = tie((chosen, kv_flat, scalars))
    chosen = chosen.reshape(requests_here, -1, rank_width)
    over_heads = [chosen] + [swap(chosen, "heads", flip) for flip in range(1, heads_size)]
    parts = []
    for part in over_heads:
        parts += [part] + [swap(part, "sub", flip) for flip in range(1, sub_size)]
    part_rows = requests_here * text_rows // share_count
    shaped = queries.reshape(requests_here, share_count // requests_here, part_rows, -1)
    few = part_rows // 2
    chunk_rows = part_rows - few, few

    def attended(chunk):
        rows = chunk_rows[chunk]
        start = sum(chunk_rows[:chunk]) // rows
        return attend(start, rows, shaped, parts, kv_flat, *gains, scalars)

    columns = out_weight.shape[1]
    if pool_size != 4:
        outputs = []
        for chunk in range(len(chunk_rows)):
            rows = lax.all_gather(attended(chunk), "pool", axis=0)
            mine = add_direct(
                send_direct(
                    project_out([rows[i] for i in range(pool_size)], out_weight, direct=True)
                )
            )
            mine = mine.reshape(pool_size, -1, columns)
            back = lax.all_to_all(mine, "pool", split_axis=0, concat_axis=0, tiled=True)
            outputs.append(jnp.moveaxis(back, 0, 1).reshape(-1, pool_size * columns))
        return jnp.concatenate(outputs, axis=0)

    first = attended(0)
    across0, beside0 = swap(first, "pool", 3), swap(first, "pool", 1)
    last = attended(1)
    across1, beside1 = swap(last, "pool", 3), swap(last, "pool", 1)
    own = project_out([first, last], out_weight)
    across0, beside0, own = tie((across0, beside0, own))
    second0 = second_hop(first, across0)
    near0 = send_direct(project_out([beside0, across0], out_weight, direct=True))
    across1, beside1, near0 = tie((across1, beside1, near0))
    second1 = second_hop(last, across1)
    many, few = chunk_rows
    near0 = add_direct(near0)
    back0 = swap(near0[:many], "pool", 1), swap(near0[many:], "pool", 3)
    near1 = send_sub(project_out([beside1, across1], out_weight))
    second0, near1 = tie((second0, near1))
    near1 = send_heads(near1)
    far0 = send_heads(send_sub(project_out([second0], out_weight)))
    second1, near1, back0, far0, own = tie((second1, near1, back0, far0, own))
    back_second0 = swap(add_shares(far0), "pool", 2)
    near1 = add_shares(near1)
    back1 = swap(near1[:few], "pool", 1), swap(near1[few:], "pool", 3)
    far1 = send_heads(send_sub(project_out([second1], out_weight)))
    back_second0, back1, far1 = tie((back_second0, back1, far1))
    back_second1 = swap(add_shares(far1), "pool", 2)
    own = add_shares(send_heads(send_sub(own)))
    backs = [(0, 1, back0[0]), (0, 3, back0[1]), (many, 1, back1[0]), (many, 3, back1[1])]
    backs += [(0, 2, back_second0), (0, 0, own), (many, 2, back_second1)]
    output = jnp.zeros((part_rows, pool_size * columns), jnp.bfloat16)
    for row, flip, block in backs:
        output = lax.dynamic_update_slice(output, block, (row, (pool_index ^ flip) * columns))
    return output


def solution(mesh):
    in_specs = (
        P(("groups", "pool"), None, ("heads", "sub")),
        P(("groups", "pool"), None),
        P(None, ("heads", "sub"), None, None),
        P(),
        P(),
        P(("heads", "sub"), "pool"),
        P("groups", None),
        P("groups", None),
        P("groups"),
        P("groups"),
    )
    out_specs = P(("groups", "pool", "heads", "sub"), None)
    return jax.shard_map(
        per_device, mesh=mesh, in_specs=in_specs, out_specs=out_specs, check_vma=False
    )
```

```python
import functools
import math

import jax
import jax.numpy as jnp
from jax import lax
from jax.experimental import pallas as pl
from jax.experimental.pallas import tpu as pltpu
from jax.sharding import PartitionSpec as P

BLK = 128
LIGHT = pl.CostEstimate(flops=1, bytes_accessed=1, transcendentals=0)


def rms_scale(values, gain):
    return values * lax.rsqrt(jnp.mean(values * values, axis=-1, keepdims=True) + 1e-05) * gain


def pair_rank(holders):
    count = holders.shape[1]
    same = holders[:, :, None] == holders[:, None, :]
    earlier = jnp.arange(count)[None, :] < jnp.arange(count)[:, None]
    return jnp.sum((same & earlier[None]).astype(jnp.int32), axis=2)


def swap(values, axis, flip):
    return lax.ppermute(values, axis, [(i, i ^ flip) for i in range(lax.axis_size(axis))])


def second_hop(block, across):
    index = lax.axis_index("pool")
    at_end = (index == 0) | (index == 3)
    passed = jnp.where(at_end, block, across)
    return lax.ppermute(passed, "pool", [(0, 2), (3, 1), (1, 0), (2, 3)])


def project_kernel(block_count, flips, share, *refs):
    blocks, weight, outs = refs[:block_count], refs[block_count], refs[block_count + 1 :]
    picked = []
    for flip in flips:
        for block in blocks:
            part_rows = block.shape[0] // len(flips)
            start = pl.multiple_of((share[0] ^ flip) * part_rows, part_rows)
            picked.append(block[pl.ds(start, part_rows), :])
    product = jnp.dot(
        jnp.concatenate(picked, axis=0), weight[...], preferred_element_type=jnp.float32
    )
    rows = product.shape[0] // len(outs)
    for i, out in enumerate(outs):
        out[...] = product[i * rows : (i + 1) * rows].astype(out.dtype)


def project_out(blocks, out_weight, direct=False):
    axes = ("heads", "sub")
    share_count = lax.axis_size(axes)
    share = lax.axis_index(axes).astype(jnp.int32).reshape(1)
    depth, columns = out_weight.shape
    flips = [*range(0, share_count, 2), *range(1, share_count, 2)]
    count = share_count if direct else 2
    rows = sum(block.shape[0] for block in blocks) // count
    tile = min(columns, 512)
    whole = pl.BlockSpec(memory_space=pltpu.VMEM)
    return pl.pallas_call(
        functools.partial(
            project_kernel, len(blocks), list(range(share_count)) if direct else flips
        ),
        grid=(columns // tile,),
        in_specs=[pl.BlockSpec(memory_space=pltpu.SMEM)]
        + [whole for _ in blocks]
        + [pl.BlockSpec((depth, tile), lambda n: (0, n))],
        out_specs=[pl.BlockSpec((rows, tile), lambda n: (0, n))] * count,
        out_shape=[
            jax.ShapeDtypeStruct((rows, columns), jnp.bfloat16 if i else jnp.float32)
            for i in range(count)
        ],
        compiler_params=pltpu.CompilerParams(vmem_limit_bytes=16 * 1024 * 1024),
        cost_estimate=LIGHT,
    )(share, *blocks, out_weight)


def send_direct(pieces):
    axes = ("heads", "sub")
    return [pieces[0]] + [swap(pieces[flip], axes, flip) for flip in range(1, len(pieces))]


def add_direct(pieces):
    return sum(piece.astype(jnp.float32) for piece in pieces).astype(jnp.bfloat16)


def send_sub(pieces):
    keep, away = pieces
    return keep, swap(away, "sub", 1)


def send_heads(pieces):
    keep, got = pieces
    heads_size = lax.axis_size("heads")
    rows = keep.shape[0] // heads_size
    received = []
    for flip in range(1, heads_size):
        part = slice(flip * rows, (flip + 1) * rows)
        both = keep[part] + got[part].astype(jnp.float32)
        received.append(swap(both.astype(jnp.bfloat16), "heads", flip))
    return keep, got, received


def add_shares(pieces):
    keep, got, received = pieces
    rows = keep.shape[0] // (len(received) + 1)
    total = keep[:rows] + got[:rows].astype(jnp.float32)
    return sum((part.astype(jnp.float32) for part in received), total).astype(jnp.bfloat16)


def find_blocks(place_holder, place_block, serving_request, items):
    pool_size = lax.axis_size("pool")
    pool_index = lax.axis_index("pool")
    capacity = 2 * ((items + pool_size - 1) // pool_size)
    total_requests = serving_request.shape[0]
    request_ids = jnp.arange(total_requests, dtype=jnp.int32)
    selector = (serving_request[:, None] == request_ids[None, :]).astype(jnp.int32)
    holders = jnp.dot(selector, place_holder).reshape(pool_size, items)
    blocks = jnp.dot(selector, place_block).reshape(pool_size, items)
    ranks = pair_rank(holders)
    slot_ids = jnp.arange(capacity, dtype=jnp.int32)
    matched = (holders[:, None, :] == pool_index) & (ranks[:, None, :] == slot_ids[None, :, None])
    send_block = jnp.sum(jnp.where(matched, blocks[:, None, :], 0), axis=2)
    partners = jnp.arange(pool_size, dtype=jnp.int32) ^ pool_index
    wanted = send_block.at[partners].get(mode="promise_in_bounds")
    my_holders = lax.dynamic_index_in_dim(holders, pool_index, 0, keepdims=False)
    my_ranks = lax.dynamic_index_in_dim(ranks, pool_index, 0, keepdims=False)
    return selector, wanted, (my_holders ^ pool_index) * capacity + my_ranks


def fetch_pieces(latent_store, wanted):
    share_count = lax.axis_size(("heads", "sub"))
    share = lax.axis_index(("heads", "sub"))
    rows = BLK // share_count
    store = latent_store.reshape(-1, rows, latent_store.shape[1])
    outgoing = store.at[wanted.reshape(-1) * share_count + share].get(mode="promise_in_bounds")
    outgoing = outgoing.reshape(*wanted.shape, rows, -1)
    arriving = {flip: swap(outgoing[flip], "pool", flip) for flip in (*range(2, len(wanted)), 1)}
    return [outgoing[0]] + [arriving[flip] for flip in range(1, len(wanted))]


def attend_kernel(share_count, scalars, queries, *refs):
    parts, (kv_up, q_gain, k_gain, out, keys, values) = refs[:share_count], refs[share_count:]
    request = pl.program_id(0)
    head_width = q_gain.shape[1]
    text, width = out.shape
    per_group = width // head_width
    part_slots = parts[0].shape[1]
    share_rows = BLK // share_count
    count, share = scalars[1 + request], scalars[0]
    for flip in range(share_count):
        rows = pl.ds(flip * part_slots, part_slots)
        projected = jnp.dot(parts[flip][request], kv_up[...], preferred_element_type=jnp.float32)
        key = rms_scale(projected[:, :head_width], k_gain[...])
        keys[rows, :] = key.astype(jnp.bfloat16)
        slot = lax.broadcasted_iota(jnp.int32, (part_slots, head_width), 0)
        position = (slot // share_rows) * BLK + (share ^ flip) * share_rows + slot % share_rows
        live = jnp.where(position < count, 1.0, 0.0)
        values[rows, :head_width] = (projected[:, head_width:] * live).astype(jnp.bfloat16)
        values[rows, head_width:] = live.astype(jnp.bfloat16)
    scale = math.log2(math.e) / math.sqrt(head_width)
    together = min(per_group, max(1, 256 // text))
    for first in range(0, per_group, together):
        normed = []
        for head in range(first, first + together):
            query = queries[0, :, :, head * head_width : (head + 1) * head_width]
            query = query.reshape(text, head_width).astype(jnp.float32)
            normed.append(rms_scale(query, q_gain[...]).astype(jnp.bfloat16))
        scores = lax.dot_general(
            jnp.concatenate(normed, axis=0),
            keys[...],
            (((1,), (1,)), ((), ())),
            preferred_element_type=jnp.float32,
        )
        expo = jnp.exp2(scores * scale).astype(jnp.bfloat16)
        total = jnp.dot(expo, values[...], preferred_element_type=jnp.float32)
        result = (total[:, :head_width] / total[:, head_width:]).astype(jnp.bfloat16)
        for i in range(together):
            head = first + i
            columns = slice(head * head_width, (head + 1) * head_width)
            out[:, columns] = result[i * text : (i + 1) * text]


def attend(chunk, rows, queries, parts, kv_flat, q_gain, k_gain, scalars):
    requests, request_shares, _, width = queries.shape
    heads_here, rank_width, pair_width = kv_flat.shape
    head_width = q_gain.shape[1]
    slots = len(parts) * parts[0].shape[1]
    text = request_shares * rows
    whole = pl.BlockSpec(memory_space=pltpu.VMEM)
    return pl.pallas_call(
        functools.partial(attend_kernel, len(parts)),
        grid=(requests, heads_here),
        in_specs=[
            pl.BlockSpec(memory_space=pltpu.SMEM),
            pl.BlockSpec(
                (1, request_shares, rows, width // heads_here),
                lambda r, g: (r, 0, chunk, g),
            ),
        ]
        + [whole for _ in parts]
        + [pl.BlockSpec((None, rank_width, pair_width), lambda r, g: (g, 0, 0)), whole, whole],
        out_specs=pl.BlockSpec((text, width // heads_here), lambda r, g: (r, g)),
        out_shape=jax.ShapeDtypeStruct((requests * text, width), jnp.bfloat16),
        scratch_shapes=[
            pltpu.VMEM((slots, head_width), jnp.bfloat16),
            pltpu.VMEM((slots, 2 * head_width), jnp.bfloat16),
        ],
        compiler_params=pltpu.CompilerParams(vmem_limit_bytes=16 * 1024 * 1024),
        cost_estimate=LIGHT,
    )(scalars, queries, *parts, kv_flat, q_gain, k_gain)


def per_device(
    queries,
    latent_store,
    kv_up,
    q_gain,
    k_gain,
    out_weight,
    place_holder,
    place_block,
    image_count,
    serving_request,
):
    pool_size = lax.axis_size("pool")
    pool_index = lax.axis_index("pool")
    heads_size = lax.axis_size("heads")
    sub_size = lax.axis_size("sub")
    share_count = heads_size * sub_size
    share = lax.axis_index(("heads", "sub"))
    requests_here, text_rows, _ = queries.shape
    blocks_each = place_holder.shape[1]
    items = requests_here * blocks_each
    rank_width = latent_store.shape[1]
    tie = lax.optimization_barrier
    selector, wanted, where = find_blocks(place_holder, place_block, serving_request, items)
    kv_flat = jnp.moveaxis(kv_up.reshape(rank_width, kv_up.shape[1], -1), 1, 0)
    gains = q_gain.reshape(1, -1), k_gain.reshape(1, -1)
    count_here = lax.dynamic_slice_in_dim(
        jnp.dot(selector, image_count), pool_index * requests_here, requests_here
    )
    scalars = jnp.concatenate([share.reshape(1), count_here])
    pieces = jnp.concatenate(fetch_pieces(latent_store, wanted), axis=0)
    chosen = pieces.at[where].get(mode="promise_in_bounds")
    chosen, kv_flat, scalars = tie((chosen, kv_flat, scalars))
    chosen = chosen.reshape(requests_here, -1, rank_width)
    over_heads = [chosen] + [swap(chosen, "heads", flip) for flip in range(1, heads_size)]
    parts = []
    for part in over_heads:
        parts += [part] + [swap(part, "sub", flip) for flip in range(1, sub_size)]
    part_rows = requests_here * text_rows // share_count
    shaped = queries.reshape(requests_here, share_count // requests_here, part_rows, -1)
    few = part_rows // 2
    chunk_rows = part_rows - few, few

    def attended(chunk):
        rows = chunk_rows[chunk]
        start = sum(chunk_rows[:chunk]) // rows
        return attend(start, rows, shaped, parts, kv_flat, *gains, scalars)

    columns = out_weight.shape[1]
    if pool_size != 4:
        outputs = []
        for chunk in range(len(chunk_rows)):
            rows = lax.all_gather(attended(chunk), "pool", axis=0)
            mine = add_direct(
                send_direct(
                    project_out([rows[i] for i in range(pool_size)], out_weight, direct=True)
                )
            )
            mine = mine.reshape(pool_size, -1, columns)
            back = lax.all_to_all(mine, "pool", split_axis=0, concat_axis=0, tiled=True)
            outputs.append(jnp.moveaxis(back, 0, 1).reshape(-1, pool_size * columns))
        return jnp.concatenate(outputs, axis=0)

    first = attended(0)
    across0, beside0 = swap(first, "pool", 3), swap(first, "pool", 1)
    last = attended(1)
    across1, beside1 = swap(last, "pool", 3), swap(last, "pool", 1)
    own = project_out([first, last], out_weight)
    across0, beside0, own = tie((across0, beside0, own))
    second0 = second_hop(first, across0)
    near0 = send_direct(project_out([beside0, across0], out_weight, direct=True))
    across1, beside1, near0, own = tie((across1, beside1, near0, own))
    second1 = second_hop(last, across1)
    near1 = send_sub(project_out([beside1, across1], out_weight))
    second0, near1 = tie((second0, near1))
    near1 = send_heads(near1)
    far0 = send_heads(send_sub(project_out([second0], out_weight)))
    near0 = add_direct(near0)
    own = send_heads(send_sub(own))
    second1, near0, near1, far0, own = tie((second1, near0, near1, far0, own))
    many, few = chunk_rows
    near1 = add_shares(near1)
    back_beside = swap(jnp.concatenate([near0[:many], near1[:few]]), "pool", 1)
    back_across = swap(jnp.concatenate([near0[many:], near1[few:]]), "pool", 3)
    back_second0 = swap(add_shares(far0), "pool", 2)
    far1 = send_direct(project_out([second1], out_weight, direct=True))
    back_beside, back_across, back_second0, far1 = tie(
        (back_beside, back_across, back_second0, far1)
    )
    back_second1 = swap(add_direct(far1), "pool", 2)
    backs = [(0, 0, add_shares(own)), (0, 1, back_beside), (0, 3, back_across)]
    backs += [(0, 2, back_second0), (many, 2, back_second1)]
    output = jnp.zeros((part_rows, pool_size * columns), jnp.bfloat16)
    for row, flip, block in backs:
        output = lax.dynamic_update_slice(output, block, (row, (pool_index ^ flip) * columns))
    return output


def solution(mesh):
    in_specs = (
        P(("groups", "pool"), None, ("heads", "sub")),
        P(("groups", "pool"), None),
        P(None, ("heads", "sub"), None, None),
        P(),
        P(),
        P(("heads", "sub"), "pool"),
        P("groups", None),
        P("groups", None),
        P("groups"),
        P("groups"),
    )
    out_specs = P(("groups", "pool", "heads", "sub"), None)
    return jax.shard_map(
        per_device, mesh=mesh, in_specs=in_specs, out_specs=out_specs, check_vma=False
    )
```

```python
import functools
import math

import jax
import jax.numpy as jnp
from jax import lax
from jax.experimental import pallas as pl
from jax.experimental.pallas import tpu as pltpu
from jax.sharding import PartitionSpec as P

BLK = 128
LIGHT = pl.CostEstimate(flops=1, bytes_accessed=1, transcendentals=0)


def rms_scale(values, gain):
    return values * lax.rsqrt(jnp.mean(values * values, axis=-1, keepdims=True) + 1e-05) * gain


def swap(values, axis, flip):
    return lax.ppermute(values, axis, [(i, i ^ flip) for i in range(lax.axis_size(axis))])


def second_hop(block, across):
    index = lax.axis_index("pool")
    at_end = (index == 0) | (index == 3)
    passed = jnp.where(at_end, block, across)
    return lax.ppermute(passed, "pool", [(0, 2), (3, 1), (1, 0), (2, 3)])


def project_kernel(block_count, flips, share, *refs):
    blocks, weight, outs = refs[:block_count], refs[block_count], refs[block_count + 1 :]
    picked = []
    for flip in flips:
        for block in blocks:
            part_rows = block.shape[0] // len(flips)
            start = pl.multiple_of((share[0] ^ flip) * part_rows, part_rows)
            picked.append(block[pl.ds(start, part_rows), :])
    product = jnp.dot(
        jnp.concatenate(picked, axis=0), weight[...], preferred_element_type=jnp.float32
    )
    rows = product.shape[0] // len(outs)
    for i, out in enumerate(outs):
        out[...] = product[i * rows : (i + 1) * rows].astype(out.dtype)


def project_out(blocks, out_weight, direct=False):
    axes = ("heads", "sub")
    share_count = lax.axis_size(axes)
    share = lax.axis_index(axes).astype(jnp.int32).reshape(1)
    depth, columns = out_weight.shape
    flips = [*range(0, share_count, 2), *range(1, share_count, 2)]
    count = share_count if direct else 2
    rows = sum(block.shape[0] for block in blocks) // count
    tile = min(columns, 512)
    whole = pl.BlockSpec(memory_space=pltpu.VMEM)
    return pl.pallas_call(
        functools.partial(
            project_kernel, len(blocks), list(range(share_count)) if direct else flips
        ),
        grid=(columns // tile,),
        in_specs=[pl.BlockSpec(memory_space=pltpu.SMEM)]
        + [whole for _ in blocks]
        + [pl.BlockSpec((depth, tile), lambda n: (0, n))],
        out_specs=[pl.BlockSpec((rows, tile), lambda n: (0, n))] * count,
        out_shape=[
            jax.ShapeDtypeStruct((rows, columns), jnp.bfloat16 if i else jnp.float32)
            for i in range(count)
        ],
        compiler_params=pltpu.CompilerParams(vmem_limit_bytes=16 * 1024 * 1024),
        cost_estimate=LIGHT,
    )(share, *blocks, out_weight)


def send_direct(pieces):
    axes = ("heads", "sub")
    return [pieces[0]] + [swap(pieces[flip], axes, flip) for flip in range(1, len(pieces))]


def add_direct(pieces):
    return sum(piece.astype(jnp.float32) for piece in pieces).astype(jnp.bfloat16)


def send_sub(pieces):
    keep, away = pieces
    return keep, swap(away, "sub", 1)


def send_heads(pieces):
    keep, got = pieces
    heads_size = lax.axis_size("heads")
    rows = keep.shape[0] // heads_size
    received = []
    for flip in range(1, heads_size):
        part = slice(flip * rows, (flip + 1) * rows)
        both = keep[part] + got[part].astype(jnp.float32)
        received.append(swap(both.astype(jnp.bfloat16), "heads", flip))
    return keep, got, received


def add_shares(pieces):
    keep, got, received = pieces
    rows = keep.shape[0] // (len(received) + 1)
    total = keep[:rows] + got[:rows].astype(jnp.float32)
    return sum((part.astype(jnp.float32) for part in received), total).astype(jnp.bfloat16)


def fetch_kernel(
    place, holder, block, serving, counts, store, where, scalars, *refs, pool_size, share_count
):
    pieces, (table, rank_of, sems) = refs[:pool_size], refs[pool_size:]
    pool_index, share = place[0], place[1]
    capacity = pieces[0].shape[0]
    blocks_each = holder.shape[1]
    requests_here = scalars.shape[0] - 1
    spare = pool_size * capacity
    copies = []
    for flip in range(pool_size):
        for slot in range(capacity):
            table[flip * capacity + slot] = 0
        rank = 0
        for i in range(requests_here):
            request = serving[(pool_index ^ flip) * requests_here + i]
            for j in range(blocks_each):
                held = holder[request, j] == pool_index
                table[jnp.where(held, flip * capacity + rank, spare)] = block[request, j]
                rank = rank + held.astype(jnp.int32)
        for slot in range(capacity):
            index = flip * capacity + slot
            source = store.at[table[index] * share_count + share]
            copies.append(pltpu.make_async_copy(source, pieces[flip].at[slot], sems.at[index]))
            copies[-1].start()
    for i in range(pool_size):
        rank_of[i] = 0
    scalars[0] = share
    for i in range(requests_here):
        request = serving[pool_index * requests_here + i]
        scalars[1 + i] = counts[request]
        for j in range(blocks_each):
            held_by = holder[request, j]
            where[0, i * blocks_each + j] = held_by ^ pool_index
            where[1, i * blocks_each + j] = rank_of[held_by]
            rank_of[held_by] = rank_of[held_by] + 1
    for copy in copies:
        copy.wait()


def fetch(latent_store, place_holder, place_block, serving_request, image_count, items):
    pool_size = lax.axis_size("pool")
    share_count = lax.axis_size(("heads", "sub"))
    place = jnp.stack([lax.axis_index("pool"), lax.axis_index(("heads", "sub"))])
    capacity = 2 * ((items + pool_size - 1) // pool_size)
    rows = BLK // share_count
    store = latent_store.reshape(-1, rows, latent_store.shape[1])
    piece = jax.ShapeDtypeStruct((capacity, rows, store.shape[2]), store.dtype)
    requests_here = items // place_holder.shape[1]
    smem = pl.BlockSpec(memory_space=pltpu.SMEM)
    where, scalars, *pieces = pl.pallas_call(
        functools.partial(fetch_kernel, pool_size=pool_size, share_count=share_count),
        in_specs=[smem] * 5 + [pl.BlockSpec(memory_space=pltpu.HBM)],
        out_specs=[smem, smem] + [pl.BlockSpec(memory_space=pltpu.VMEM)] * pool_size,
        out_shape=[
            jax.ShapeDtypeStruct((2, items), jnp.int32),
            jax.ShapeDtypeStruct((1 + requests_here,), jnp.int32),
        ]
        + [piece] * pool_size,
        scratch_shapes=[
            pltpu.SMEM((pool_size * capacity + 1,), jnp.int32),
            pltpu.SMEM((pool_size,), jnp.int32),
            pltpu.SemaphoreType.DMA((pool_size * capacity,)),
        ],
        cost_estimate=LIGHT,
    )(place.astype(jnp.int32), place_holder, place_block, serving_request, image_count, store)
    return where, scalars, pieces


def choose_kernel(where, *refs):
    pieces, out = refs[:-1], refs[-1]
    for i in range(out.shape[0]):
        flip, slot = where[0, i], where[1, i]
        for other, piece in enumerate(pieces):

            @pl.when(flip == other)
            def _(piece=piece):
                out[i] = piece[slot]


def choose(where, pieces):
    whole = pl.BlockSpec(memory_space=pltpu.VMEM)
    return pl.pallas_call(
        choose_kernel,
        in_specs=[pl.BlockSpec(memory_space=pltpu.SMEM)] + [whole] * len(pieces),
        out_specs=whole,
        out_shape=jax.ShapeDtypeStruct((where.shape[1], *pieces[0].shape[1:]), pieces[0].dtype),
        cost_estimate=LIGHT,
    )(where, *pieces)


def attend_kernel(share_count, scalars, queries, *refs):
    parts, (kv_up, q_gain, k_gain, out, keys, values) = refs[:share_count], refs[share_count:]
    request = pl.program_id(0)
    head_width = q_gain.shape[1]
    text, width = out.shape
    per_group = width // head_width
    part_slots = parts[0].shape[1]
    share_rows = BLK // share_count
    count, share = scalars[1 + request], scalars[0]
    for flip in range(share_count):
        rows = pl.ds(flip * part_slots, part_slots)
        projected = jnp.dot(parts[flip][request], kv_up[...], preferred_element_type=jnp.float32)
        key = rms_scale(projected[:, :head_width], k_gain[...])
        keys[rows, :] = key.astype(jnp.bfloat16)
        slot = lax.broadcasted_iota(jnp.int32, (part_slots, head_width), 0)
        position = (slot // share_rows) * BLK + (share ^ flip) * share_rows + slot % share_rows
        live = jnp.where(position < count, 1.0, 0.0)
        values[rows, :head_width] = (projected[:, head_width:] * live).astype(jnp.bfloat16)
        values[rows, head_width:] = live.astype(jnp.bfloat16)
    scale = math.log2(math.e) / math.sqrt(head_width)
    together = min(per_group, max(1, 256 // text))
    for first in range(0, per_group, together):
        normed = []
        for head in range(first, first + together):
            query = queries[0, :, :, head * head_width : (head + 1) * head_width]
            query = query.reshape(text, head_width).astype(jnp.float32)
            normed.append(rms_scale(query, q_gain[...]).astype(jnp.bfloat16))
        scores = lax.dot_general(
            jnp.concatenate(normed, axis=0),
            keys[...],
            (((1,), (1,)), ((), ())),
            preferred_element_type=jnp.float32,
        )
        expo = jnp.exp2(scores * scale).astype(jnp.bfloat16)
        total = jnp.dot(expo, values[...], preferred_element_type=jnp.float32)
        result = (total[:, :head_width] / total[:, head_width:]).astype(jnp.bfloat16)
        for i in range(together):
            head = first + i
            columns = slice(head * head_width, (head + 1) * head_width)
            out[:, columns] = result[i * text : (i + 1) * text]


def attend(chunk, rows, queries, parts, kv_flat, q_gain, k_gain, scalars):
    requests, request_shares, _, width = queries.shape
    heads_here, rank_width, pair_width = kv_flat.shape
    head_width = q_gain.shape[1]
    slots = len(parts) * parts[0].shape[1]
    text = request_shares * rows
    whole = pl.BlockSpec(memory_space=pltpu.VMEM)
    return pl.pallas_call(
        functools.partial(attend_kernel, len(parts)),
        grid=(requests, heads_here),
        in_specs=[
            pl.BlockSpec(memory_space=pltpu.SMEM),
            pl.BlockSpec(
                (1, request_shares, rows, width // heads_here),
                lambda r, g: (r, 0, chunk, g),
            ),
        ]
        + [whole for _ in parts]
        + [pl.BlockSpec((None, rank_width, pair_width), lambda r, g: (g, 0, 0)), whole, whole],
        out_specs=pl.BlockSpec((text, width // heads_here), lambda r, g: (r, g)),
        out_shape=jax.ShapeDtypeStruct((requests * text, width), jnp.bfloat16),
        scratch_shapes=[
            pltpu.VMEM((slots, head_width), jnp.bfloat16),
            pltpu.VMEM((slots, 2 * head_width), jnp.bfloat16),
        ],
        compiler_params=pltpu.CompilerParams(vmem_limit_bytes=16 * 1024 * 1024),
        cost_estimate=LIGHT,
    )(scalars, queries, *parts, kv_flat, q_gain, k_gain)


def per_device(
    queries,
    latent_store,
    kv_up,
    q_gain,
    k_gain,
    out_weight,
    place_holder,
    place_block,
    image_count,
    serving_request,
):
    pool_size = lax.axis_size("pool")
    pool_index = lax.axis_index("pool")
    heads_size = lax.axis_size("heads")
    sub_size = lax.axis_size("sub")
    share_count = heads_size * sub_size
    share = lax.axis_index(("heads", "sub"))
    requests_here, text_rows, _ = queries.shape
    blocks_each = place_holder.shape[1]
    items = requests_here * blocks_each
    rank_width = latent_store.shape[1]
    tie = lax.optimization_barrier
    where, scalars, pieces = fetch(
        latent_store, place_holder, place_block, serving_request, image_count, items
    )
    kv_flat = jnp.moveaxis(kv_up.reshape(rank_width, kv_up.shape[1], -1), 1, 0)
    gains = q_gain.reshape(1, -1), k_gain.reshape(1, -1)
    arriving = [swap(pieces[flip], "pool", flip) for flip in range(1, pool_size)]
    chosen = choose(where, pieces[:1] + arriving)
    chosen, kv_flat, scalars = tie((chosen, kv_flat, scalars))
    chosen = chosen.reshape(requests_here, -1, rank_width)
    over_heads = [chosen] + [swap(chosen, "heads", flip) for flip in range(1, heads_size)]
    parts = []
    for part in over_heads:
        parts += [part] + [swap(part, "sub", flip) for flip in range(1, sub_size)]
    part_rows = requests_here * text_rows // share_count
    shaped = queries.reshape(requests_here, share_count // requests_here, part_rows, -1)
    few = part_rows // 2
    chunk_rows = part_rows - few, few

    def attended(chunk):
        rows = chunk_rows[chunk]
        start = sum(chunk_rows[:chunk]) // rows
        return attend(start, rows, shaped, parts, kv_flat, *gains, scalars)

    columns = out_weight.shape[1]
    if pool_size != 4:
        outputs = []
        for chunk in range(len(chunk_rows)):
            rows = lax.all_gather(attended(chunk), "pool", axis=0)
            mine = add_direct(
                send_direct(
                    project_out([rows[i] for i in range(pool_size)], out_weight, direct=True)
                )
            )
            mine = mine.reshape(pool_size, -1, columns)
            back = lax.all_to_all(mine, "pool", split_axis=0, concat_axis=0, tiled=True)
            outputs.append(jnp.moveaxis(back, 0, 1).reshape(-1, pool_size * columns))
        return jnp.concatenate(outputs, axis=0)

    first = attended(0)
    across0, beside0 = swap(first, "pool", 3), swap(first, "pool", 1)
    last = attended(1)
    across1, beside1 = swap(last, "pool", 3), swap(last, "pool", 1)
    own = project_out([first, last], out_weight)
    across0, beside0, own = tie((across0, beside0, own))
    second0 = second_hop(first, across0)
    near0 = send_direct(project_out([beside0, across0], out_weight, direct=True))
    across1, beside1, near0, own = tie((across1, beside1, near0, own))
    second1 = second_hop(last, across1)
    near1 = send_sub(project_out([beside1, across1], out_weight))
    second0, near1 = tie((second0, near1))
    near1 = send_heads(near1)
    far0 = send_heads(send_sub(project_out([second0], out_weight)))
    near0 = add_direct(near0)
    own = send_heads(send_sub(own))
    second1, near0, near1, far0, own = tie((second1, near0, near1, far0, own))
    many, few = chunk_rows
    near1 = add_shares(near1)
    back_beside = swap(jnp.concatenate([near0[:many], near1[:few]]), "pool", 1)
    back_across = swap(jnp.concatenate([near0[many:], near1[few:]]), "pool", 3)
    back_second0 = swap(add_shares(far0), "pool", 2)
    far1 = send_direct(project_out([second1], out_weight, direct=True))
    back_beside, back_across, back_second0, far1 = tie(
        (back_beside, back_across, back_second0, far1)
    )
    back_second1 = swap(add_direct(far1), "pool", 2)
    backs = [(0, 0, add_shares(own)), (0, 1, back_beside), (0, 3, back_across)]
    backs += [(0, 2, back_second0), (many, 2, back_second1)]
    output = jnp.zeros((part_rows, pool_size * columns), jnp.bfloat16)
    for row, flip, block in backs:
        output = lax.dynamic_update_slice(output, block, (row, (pool_index ^ flip) * columns))
    return output


def solution(mesh):
    in_specs = (
        P(("groups", "pool"), None, ("heads", "sub")),
        P(("groups", "pool"), None),
        P(None, ("heads", "sub"), None, None),
        P(),
        P(),
        P(("heads", "sub"), "pool"),
        P("groups", None),
        P("groups", None),
        P("groups"),
        P("groups"),
    )
    out_specs = P(("groups", "pool", "heads", "sub"), None)
    return jax.shard_map(
        per_device, mesh=mesh, in_specs=in_specs, out_specs=out_specs, check_vma=False
    )
```

```python
import functools
import math

import jax
import jax.numpy as jnp
from jax import lax
from jax.experimental import pallas as pl
from jax.experimental.pallas import tpu as pltpu
from jax.sharding import PartitionSpec as P

BLK = 128
LIGHT = pl.CostEstimate(flops=1, bytes_accessed=1, transcendentals=0)


def rms_scale(values, gain):
    return values * lax.rsqrt(jnp.mean(values * values, axis=-1, keepdims=True) + 1e-05) * gain


def swap(values, axis, flip):
    return lax.ppermute(values, axis, [(i, i ^ flip) for i in range(lax.axis_size(axis))])


def second_hop(block, across):
    index = lax.axis_index("pool")
    at_end = (index == 0) | (index == 3)
    passed = jnp.where(at_end, block, across)
    return lax.ppermute(passed, "pool", [(0, 2), (3, 1), (1, 0), (2, 3)])


def project_kernel(block_count, flips, share, *refs):
    blocks, weight, outs = refs[:block_count], refs[block_count], refs[block_count + 1 :]
    picked = []
    for flip in flips:
        for block in blocks:
            part_rows = block.shape[0] // len(flips)
            start = pl.multiple_of((share[0] ^ flip) * part_rows, part_rows)
            picked.append(block[pl.ds(start, part_rows), :])
    product = jnp.dot(
        jnp.concatenate(picked, axis=0), weight[...], preferred_element_type=jnp.float32
    )
    rows = product.shape[0] // len(outs)
    for i, out in enumerate(outs):
        out[...] = product[i * rows : (i + 1) * rows].astype(out.dtype)


def project_out(blocks, out_weight, direct=False):
    axes = ("heads", "sub")
    share_count = lax.axis_size(axes)
    share = lax.axis_index(axes).astype(jnp.int32).reshape(1)
    depth, columns = out_weight.shape
    flips = [*range(0, share_count, 2), *range(1, share_count, 2)]
    count = share_count if direct else 2
    rows = sum(block.shape[0] for block in blocks) // count
    tile = min(columns, 512)
    whole = pl.BlockSpec(memory_space=pltpu.VMEM)
    return pl.pallas_call(
        functools.partial(
            project_kernel, len(blocks), list(range(share_count)) if direct else flips
        ),
        grid=(columns // tile,),
        in_specs=[pl.BlockSpec(memory_space=pltpu.SMEM)]
        + [whole for _ in blocks]
        + [pl.BlockSpec((depth, tile), lambda n: (0, n))],
        out_specs=[pl.BlockSpec((rows, tile), lambda n: (0, n))] * count,
        out_shape=[
            jax.ShapeDtypeStruct((rows, columns), jnp.bfloat16 if i else jnp.float32)
            for i in range(count)
        ],
        compiler_params=pltpu.CompilerParams(vmem_limit_bytes=16 * 1024 * 1024),
        cost_estimate=LIGHT,
    )(share, *blocks, out_weight)


def send_direct(pieces):
    axes = ("heads", "sub")
    return [pieces[0]] + [swap(pieces[flip], axes, flip) for flip in range(1, len(pieces))]


def add_direct(pieces):
    return sum(piece.astype(jnp.float32) for piece in pieces).astype(jnp.bfloat16)


def send_sub(pieces):
    keep, away = pieces
    return keep, swap(away, "sub", 1)


def send_heads(pieces):
    keep, got = pieces
    heads_size = lax.axis_size("heads")
    rows = keep.shape[0] // heads_size
    received = []
    for flip in range(1, heads_size):
        part = slice(flip * rows, (flip + 1) * rows)
        both = keep[part] + got[part].astype(jnp.float32)
        received.append(swap(both.astype(jnp.bfloat16), "heads", flip))
    return keep, got, received


def add_shares(pieces):
    keep, got, received = pieces
    rows = keep.shape[0] // (len(received) + 1)
    total = keep[:rows] + got[:rows].astype(jnp.float32)
    return sum((part.astype(jnp.float32) for part in received), total).astype(jnp.bfloat16)


def fetch_kernel(
    place, holder, block, serving, store, where, *refs, pool_size, share_count
):
    pieces, (table, rank_of, sems) = refs[:pool_size], refs[pool_size:]
    pool_index, share = place[0], place[1]
    capacity = pieces[0].shape[0]
    blocks_each = holder.shape[1]
    requests_here = where.shape[1] // blocks_each
    spare = pool_size * capacity
    copies = []
    for flip in range(pool_size):
        for slot in range(capacity):
            table[flip * capacity + slot] = 0
        rank = 0
        for i in range(requests_here):
            request = serving[(pool_index ^ flip) * requests_here + i]
            for j in range(blocks_each):
                held = holder[request, j] == pool_index
                table[jnp.where(held, flip * capacity + rank, spare)] = block[request, j]
                rank = rank + held.astype(jnp.int32)
        for slot in range(capacity):
            index = flip * capacity + slot
            source = store.at[table[index] * share_count + share]
            copies.append(pltpu.make_async_copy(source, pieces[flip].at[slot], sems.at[index]))
            copies[-1].start()
    for i in range(pool_size):
        rank_of[i] = 0
    for i in range(requests_here):
        request = serving[pool_index * requests_here + i]
        for j in range(blocks_each):
            held_by = holder[request, j]
            where[0, i * blocks_each + j] = held_by ^ pool_index
            where[1, i * blocks_each + j] = rank_of[held_by]
            rank_of[held_by] = rank_of[held_by] + 1
    for copy in copies:
        copy.wait()


def fetch(place, latent_store, place_holder, place_block, serving_request, items):
    pool_size = lax.axis_size("pool")
    share_count = lax.axis_size(("heads", "sub"))
    capacity = 2 * ((items + pool_size - 1) // pool_size)
    rows = BLK // share_count
    store = latent_store.reshape(-1, rows, latent_store.shape[1])
    piece = jax.ShapeDtypeStruct((capacity, rows, store.shape[2]), store.dtype)
    smem = pl.BlockSpec(memory_space=pltpu.SMEM)
    where, *pieces = pl.pallas_call(
        functools.partial(fetch_kernel, pool_size=pool_size, share_count=share_count),
        in_specs=[smem] * 4 + [pl.BlockSpec(memory_space=pltpu.HBM)],
        out_specs=[smem] + [pl.BlockSpec(memory_space=pltpu.VMEM)] * pool_size,
        out_shape=[jax.ShapeDtypeStruct((2, items), jnp.int32)] + [piece] * pool_size,
        scratch_shapes=[
            pltpu.SMEM((pool_size * capacity + 1,), jnp.int32),
            pltpu.SMEM((pool_size,), jnp.int32),
            pltpu.SemaphoreType.DMA((pool_size * capacity,)),
        ],
        cost_estimate=LIGHT,
    )(place, place_holder, place_block, serving_request, store)
    return where, pieces


def choose_kernel(where, *refs):
    pieces, out = refs[:-1], refs[-1]
    for i in range(out.shape[0]):
        flip, slot = where[0, i], where[1, i]
        for other, piece in enumerate(pieces):

            @pl.when(flip == other)
            def _(piece=piece):
                out[i] = piece[slot]


def choose(where, pieces):
    whole = pl.BlockSpec(memory_space=pltpu.VMEM)
    return pl.pallas_call(
        choose_kernel,
        in_specs=[pl.BlockSpec(memory_space=pltpu.SMEM)] + [whole] * len(pieces),
        out_specs=whole,
        out_shape=jax.ShapeDtypeStruct((where.shape[1], *pieces[0].shape[1:]), pieces[0].dtype),
        compiler_params=pltpu.CompilerParams(vmem_limit_bytes=8 * 1024 * 1024),
        cost_estimate=LIGHT,
    )(where, *pieces)


def attend_kernel(share_count, scalars, queries, *refs):
    parts, (kv_up, gains, out, keys, values) = refs[:share_count], refs[share_count:]
    request = pl.program_id(0)
    q_gain, k_gain = gains[0:1, :], gains[1:2, :]
    head_width = gains.shape[1]
    text, width = out.shape
    per_group = width // head_width
    part_slots = parts[0].shape[1]
    share_rows = BLK // share_count
    share, count = scalars[0], scalars[1 + request]
    for flip in range(share_count):
        rows = pl.ds(flip * part_slots, part_slots)
        projected = jnp.dot(parts[flip][request], kv_up[...], preferred_element_type=jnp.float32)
        key = rms_scale(projected[:, :head_width], k_gain)
        keys[rows, :] = key.astype(jnp.bfloat16)
        slot = lax.broadcasted_iota(jnp.int32, (part_slots, head_width), 0)
        position = (slot // share_rows) * BLK + (share ^ flip) * share_rows + slot % share_rows
        live = jnp.where(position < count, 1.0, 0.0)
        values[rows, :head_width] = (projected[:, head_width:] * live).astype(jnp.bfloat16)
        values[rows, head_width:] = live.astype(jnp.bfloat16)
    scale = math.log2(math.e) / math.sqrt(head_width)
    together = min(per_group, max(1, 256 // text))
    for first in range(0, per_group, together):
        normed = []
        for head in range(first, first + together):
            query = queries[0, :, :, head * head_width : (head + 1) * head_width]
            query = query.reshape(text, head_width).astype(jnp.float32)
            normed.append(rms_scale(query, q_gain).astype(jnp.bfloat16))
        scores = lax.dot_general(
            jnp.concatenate(normed, axis=0),
            keys[...],
            (((1,), (1,)), ((), ())),
            preferred_element_type=jnp.float32,
        )
        expo = jnp.exp2(scores * scale).astype(jnp.bfloat16)
        total = jnp.dot(expo, values[...], preferred_element_type=jnp.float32)
        result = (total[:, :head_width] / total[:, head_width:]).astype(jnp.bfloat16)
        for i in range(together):
            head = first + i
            columns = slice(head * head_width, (head + 1) * head_width)
            out[:, columns] = result[i * text : (i + 1) * text]


def attend(chunk, rows, queries, parts, kv_flat, gains, scalars):
    requests, request_shares, _, width = queries.shape
    heads_here, rank_width, pair_width = kv_flat.shape
    head_width = gains.shape[1]
    slots = len(parts) * parts[0].shape[1]
    text = request_shares * rows
    whole = pl.BlockSpec(memory_space=pltpu.VMEM)
    return pl.pallas_call(
        functools.partial(attend_kernel, len(parts)),
        grid=(requests, heads_here),
        in_specs=[
            pl.BlockSpec(memory_space=pltpu.SMEM),
            pl.BlockSpec(
                (1, request_shares, rows, width // heads_here),
                lambda r, g: (r, 0, chunk, g),
            ),
        ]
        + [whole for _ in parts]
        + [pl.BlockSpec((None, rank_width, pair_width), lambda r, g: (g, 0, 0)), whole],
        out_specs=pl.BlockSpec((text, width // heads_here), lambda r, g: (r, g)),
        out_shape=jax.ShapeDtypeStruct((requests * text, width), jnp.bfloat16),
        scratch_shapes=[
            pltpu.VMEM((slots, head_width), jnp.bfloat16),
            pltpu.VMEM((slots, 2 * head_width), jnp.bfloat16),
        ],
        compiler_params=pltpu.CompilerParams(vmem_limit_bytes=16 * 1024 * 1024),
        cost_estimate=LIGHT,
    )(scalars, queries, *parts, kv_flat, gains)


def per_device(
    queries,
    latent_store,
    kv_up,
    q_gain,
    k_gain,
    out_weight,
    place_holder,
    place_block,
    image_count,
    serving_request,
):
    pool_size = lax.axis_size("pool")
    pool_index = lax.axis_index("pool")
    heads_size = lax.axis_size("heads")
    sub_size = lax.axis_size("sub")
    share_count = heads_size * sub_size
    share = lax.axis_index(("heads", "sub"))
    requests_here, text_rows, _ = queries.shape
    blocks_each = place_holder.shape[1]
    items = requests_here * blocks_each
    rank_width = latent_store.shape[1]
    tie = lax.optimization_barrier
    place = jnp.stack([pool_index, share]).astype(jnp.int32)
    where, pieces = fetch(place, latent_store, place_holder, place_block, serving_request, items)
    kv_flat = jnp.moveaxis(kv_up.reshape(rank_width, kv_up.shape[1], -1), 1, 0)
    gains = jnp.stack([q_gain, k_gain])
    request_ids = jnp.arange(serving_request.shape[0], dtype=jnp.int32)
    served_here = lax.dynamic_slice_in_dim(
        serving_request, pool_index * requests_here, requests_here
    )
    count_here = jnp.sum(
        jnp.where(served_here[:, None] == request_ids[None, :], image_count[None, :], 0), axis=1
    )
    scalars = jnp.concatenate([share.reshape(1), count_here])
    arriving = [swap(pieces[flip], "pool", flip) for flip in range(1, pool_size)]
    chosen = choose(where, pieces[:1] + arriving)
    chosen, kv_flat, gains, scalars = tie((chosen, kv_flat, gains, scalars))
    chosen = chosen.reshape(requests_here, -1, rank_width)
    over_heads = [chosen] + [swap(chosen, "heads", flip) for flip in range(1, heads_size)]
    parts = []
    for part in over_heads:
        parts += [part] + [swap(part, "sub", flip) for flip in range(1, sub_size)]
    part_rows = requests_here * text_rows // share_count
    shaped = queries.reshape(requests_here, share_count // requests_here, part_rows, -1)
    few = part_rows // 2
    chunk_rows = part_rows - few, few

    def attended(chunk):
        rows = chunk_rows[chunk]
        start = sum(chunk_rows[:chunk]) // rows
        return attend(start, rows, shaped, parts, kv_flat, gains, scalars)

    columns = out_weight.shape[1]
    if pool_size != 4:
        outputs = []
        for chunk in range(len(chunk_rows)):
            rows = lax.all_gather(attended(chunk), "pool", axis=0)
            mine = add_direct(
                send_direct(
                    project_out([rows[i] for i in range(pool_size)], out_weight, direct=True)
                )
            )
            mine = mine.reshape(pool_size, -1, columns)
            back = lax.all_to_all(mine, "pool", split_axis=0, concat_axis=0, tiled=True)
            outputs.append(jnp.moveaxis(back, 0, 1).reshape(-1, pool_size * columns))
        return jnp.concatenate(outputs, axis=0)

    first = attended(0)
    across0, beside0 = swap(first, "pool", 3), swap(first, "pool", 1)
    last = attended(1)
    across1, beside1 = swap(last, "pool", 3), swap(last, "pool", 1)
    own = project_out([first, last], out_weight)
    across0, beside0, own = tie((across0, beside0, own))
    second0 = second_hop(first, across0)
    near0 = send_direct(project_out([beside0, across0], out_weight, direct=True))
    across1, beside1, near0, own = tie((across1, beside1, near0, own))
    second1 = second_hop(last, across1)
    near1 = send_sub(project_out([beside1, across1], out_weight))
    second0, near1 = tie((second0, near1))
    near1 = send_heads(near1)
    far0 = send_heads(send_sub(project_out([second0], out_weight)))
    near0 = add_direct(near0)
    own = send_heads(send_sub(own))
    second1, near0, near1, far0, own = tie((second1, near0, near1, far0, own))
    many, few = chunk_rows
    near1 = add_shares(near1)
    back_beside = swap(jnp.concatenate([near0[:many], near1[:few]]), "pool", 1)
    back_across = swap(jnp.concatenate([near0[many:], near1[few:]]), "pool", 3)
    back_second0 = swap(add_shares(far0), "pool", 2)
    far1 = send_direct(project_out([second1], out_weight, direct=True))
    back_beside, back_across, back_second0, far1 = tie(
        (back_beside, back_across, back_second0, far1)
    )
    back_second1 = swap(add_direct(far1), "pool", 2)
    backs = [(0, 0, add_shares(own)), (0, 1, back_beside), (0, 3, back_across)]
    backs += [(0, 2, back_second0), (many, 2, back_second1)]
    output = jnp.zeros((part_rows, pool_size * columns), jnp.bfloat16)
    for row, flip, block in backs:
        output = lax.dynamic_update_slice(output, block, (row, (pool_index ^ flip) * columns))
    return output


def solution(mesh):
    in_specs = (
        P(("groups", "pool"), None, ("heads", "sub")),
        P(("groups", "pool"), None),
        P(None, ("heads", "sub"), None, None),
        P(),
        P(),
        P(("heads", "sub"), "pool"),
        P("groups", None),
        P("groups", None),
        P("groups"),
        P("groups"),
    )
    out_specs = P(("groups", "pool", "heads", "sub"), None)
    return jax.shard_map(
        per_device, mesh=mesh, in_specs=in_specs, out_specs=out_specs, check_vma=False
    )
```

```python
import functools
import math

import jax
import jax.numpy as jnp
from jax import lax
from jax.experimental import pallas as pl
from jax.experimental.pallas import tpu as pltpu
from jax.sharding import PartitionSpec as P

BLK = 128
LIGHT = pl.CostEstimate(flops=1, bytes_accessed=1, transcendentals=0)


def rms_scale(values, gain):
    return values * lax.rsqrt(jnp.mean(values * values, axis=-1, keepdims=True) + 1e-05) * gain


def swap(values, axis, flip):
    return lax.ppermute(values, axis, [(i, i ^ flip) for i in range(lax.axis_size(axis))])


def second_hop(block, across):
    index = lax.axis_index("pool")
    at_end = (index == 0) | (index == 3)
    passed = jnp.where(at_end, block, across)
    return lax.ppermute(passed, "pool", [(0, 2), (3, 1), (1, 0), (2, 3)])


def project_kernel(block_count, flips, share, *refs):
    blocks, weight, outs = refs[:block_count], refs[block_count], refs[block_count + 1 :]
    picked = []
    for flip in flips:
        for block in blocks:
            part_rows = block.shape[0] // len(flips)
            start = pl.multiple_of((share[0] ^ flip) * part_rows, part_rows)
            picked.append(block[pl.ds(start, part_rows), :])
    product = jnp.dot(
        jnp.concatenate(picked, axis=0), weight[...], preferred_element_type=jnp.float32
    )
    rows = product.shape[0] // len(outs)
    for i, out in enumerate(outs):
        out[...] = product[i * rows : (i + 1) * rows].astype(out.dtype)


def project_out(blocks, out_weight, direct=False):
    axes = ("heads", "sub")
    share_count = lax.axis_size(axes)
    share = lax.axis_index(axes).astype(jnp.int32).reshape(1)
    depth, columns = out_weight.shape
    flips = [*range(0, share_count, 2), *range(1, share_count, 2)]
    count = share_count if direct else 2
    rows = sum(block.shape[0] for block in blocks) // count
    tile = min(columns, 512)
    whole = pl.BlockSpec(memory_space=pltpu.VMEM)
    return pl.pallas_call(
        functools.partial(
            project_kernel, len(blocks), list(range(share_count)) if direct else flips
        ),
        grid=(columns // tile,),
        in_specs=[pl.BlockSpec(memory_space=pltpu.SMEM)]
        + [whole for _ in blocks]
        + [pl.BlockSpec((depth, tile), lambda n: (0, n))],
        out_specs=[pl.BlockSpec((rows, tile), lambda n: (0, n))] * count,
        out_shape=[
            jax.ShapeDtypeStruct((rows, columns), jnp.bfloat16 if i else jnp.float32)
            for i in range(count)
        ],
        compiler_params=pltpu.CompilerParams(vmem_limit_bytes=16 * 1024 * 1024),
        cost_estimate=LIGHT,
    )(share, *blocks, out_weight)


def send_direct(pieces):
    axes = ("heads", "sub")
    return [pieces[0]] + [swap(pieces[flip], axes, flip) for flip in range(1, len(pieces))]


def add_direct(pieces):
    return sum(piece.astype(jnp.float32) for piece in pieces).astype(jnp.bfloat16)


def send_sub(pieces):
    keep, away = pieces
    return keep, swap(away, "sub", 1)


def send_heads(pieces):
    keep, got = pieces
    heads_size = lax.axis_size("heads")
    rows = keep.shape[0] // heads_size
    received = []
    for flip in range(1, heads_size):
        part = slice(flip * rows, (flip + 1) * rows)
        both = keep[part] + got[part].astype(jnp.float32)
        received.append(swap(both.astype(jnp.bfloat16), "heads", flip))
    return keep, got, received


def add_shares(pieces):
    keep, got, received = pieces
    rows = keep.shape[0] // (len(received) + 1)
    total = keep[:rows] + got[:rows].astype(jnp.float32)
    return sum((part.astype(jnp.float32) for part in received), total).astype(jnp.bfloat16)


def fetch_kernel(
    place, holder, block, serving, store, where, *refs, pool_size, share_count
):
    pieces, (table, rank_of, sems) = refs[:pool_size], refs[pool_size:]
    pool_index, share = place[0], place[1]
    capacity = pieces[0].shape[0]
    blocks_each = holder.shape[1]
    requests_here = where.shape[1] // blocks_each
    spare = pool_size * capacity
    copies = []
    for flip in range(pool_size):
        for slot in range(capacity):
            table[flip * capacity + slot] = 0
        rank = 0
        for i in range(requests_here):
            request = serving[(pool_index ^ flip) * requests_here + i]
            for j in range(blocks_each):
                held = holder[request, j] == pool_index
                table[jnp.where(held, flip * capacity + rank, spare)] = block[request, j]
                rank = rank + held.astype(jnp.int32)
        for slot in range(capacity):
            index = flip * capacity + slot
            source = store.at[table[index] * share_count + share]
            copies.append(pltpu.make_async_copy(source, pieces[flip].at[slot], sems.at[index]))
            copies[-1].start()
    for i in range(pool_size):
        rank_of[i] = 0
    for i in range(requests_here):
        request = serving[pool_index * requests_here + i]
        for j in range(blocks_each):
            held_by = holder[request, j]
            where[0, i * blocks_each + j] = held_by ^ pool_index
            where[1, i * blocks_each + j] = rank_of[held_by]
            rank_of[held_by] = rank_of[held_by] + 1
    for copy in copies:
        copy.wait()


def fetch(place, latent_store, place_holder, place_block, serving_request, items):
    pool_size = lax.axis_size("pool")
    share_count = lax.axis_size(("heads", "sub"))
    capacity = 2 * ((items + pool_size - 1) // pool_size)
    rows = BLK // share_count
    store = latent_store.reshape(-1, rows, latent_store.shape[1])
    piece = jax.ShapeDtypeStruct((capacity, rows, store.shape[2]), store.dtype)
    smem = pl.BlockSpec(memory_space=pltpu.SMEM)
    where, *pieces = pl.pallas_call(
        functools.partial(fetch_kernel, pool_size=pool_size, share_count=share_count),
        in_specs=[smem] * 4 + [pl.BlockSpec(memory_space=pltpu.HBM)],
        out_specs=[smem] + [pl.BlockSpec(memory_space=pltpu.VMEM)] * pool_size,
        out_shape=[jax.ShapeDtypeStruct((2, items), jnp.int32)] + [piece] * pool_size,
        scratch_shapes=[
            pltpu.SMEM((pool_size * capacity + 1,), jnp.int32),
            pltpu.SMEM((pool_size,), jnp.int32),
            pltpu.SemaphoreType.DMA((pool_size * capacity,)),
        ],
        cost_estimate=LIGHT,
    )(place, place_holder, place_block, serving_request, store)
    return where, pieces


def choose_kernel(where, *refs):
    pieces, out = refs[:-1], refs[-1]
    for i in range(out.shape[0]):
        flip, slot = where[0, i], where[1, i]
        for other, piece in enumerate(pieces):

            @pl.when(flip == other)
            def _(piece=piece):
                out[i] = piece[slot]


def choose(where, pieces):
    whole = pl.BlockSpec(memory_space=pltpu.VMEM)
    return pl.pallas_call(
        choose_kernel,
        in_specs=[pl.BlockSpec(memory_space=pltpu.SMEM)] + [whole] * len(pieces),
        out_specs=whole,
        out_shape=jax.ShapeDtypeStruct((where.shape[1], *pieces[0].shape[1:]), pieces[0].dtype),
        compiler_params=pltpu.CompilerParams(vmem_limit_bytes=8 * 1024 * 1024),
        cost_estimate=LIGHT,
    )(where, *pieces)


def attend_kernel(share_count, scalars, queries, *refs):
    parts, (kv_up, gains, out, keys, values) = refs[:share_count], refs[share_count:]
    request = pl.program_id(0)
    q_gain, k_gain = gains[0:1, :], gains[1:2, :]
    head_width = gains.shape[1]
    text, width = out.shape
    per_group = width // head_width
    part_slots = parts[0].shape[1]
    share_rows = BLK // share_count
    share, count = scalars[0], scalars[1 + request]
    for flip in range(share_count):
        rows = pl.ds(flip * part_slots, part_slots)
        projected = jnp.dot(parts[flip][request], kv_up[...], preferred_element_type=jnp.float32)
        key = rms_scale(projected[:, :head_width], k_gain)
        keys[rows, :] = key.astype(jnp.bfloat16)
        slot = lax.broadcasted_iota(jnp.int32, (part_slots, head_width), 0)
        position = (slot // share_rows) * BLK + (share ^ flip) * share_rows + slot % share_rows
        live = jnp.where(position < count, 1.0, 0.0)
        values[rows, :head_width] = (projected[:, head_width:] * live).astype(jnp.bfloat16)
        values[rows, head_width:] = live.astype(jnp.bfloat16)
    scale = math.log2(math.e) / math.sqrt(head_width)
    together = min(per_group, max(1, 256 // text))
    for first in range(0, per_group, together):
        normed = []
        for head in range(first, first + together):
            query = queries[0, :, :, head * head_width : (head + 1) * head_width]
            query = query.reshape(text, head_width).astype(jnp.float32)
            normed.append(rms_scale(query, q_gain).astype(jnp.bfloat16))
        scores = lax.dot_general(
            jnp.concatenate(normed, axis=0),
            keys[...],
            (((1,), (1,)), ((), ())),
            preferred_element_type=jnp.float32,
        )
        expo = jnp.exp2(scores * scale).astype(jnp.bfloat16)
        total = jnp.dot(expo, values[...], preferred_element_type=jnp.float32)
        result = (total[:, :head_width] / total[:, head_width:]).astype(jnp.bfloat16)
        for i in range(together):
            head = first + i
            columns = slice(head * head_width, (head + 1) * head_width)
            out[:, columns] = result[i * text : (i + 1) * text]


def attend(chunk, rows, queries, parts, kv_flat, gains, scalars):
    requests, request_shares, _, width = queries.shape
    heads_here, rank_width, pair_width = kv_flat.shape
    head_width = gains.shape[1]
    slots = len(parts) * parts[0].shape[1]
    text = request_shares * rows
    whole = pl.BlockSpec(memory_space=pltpu.VMEM)
    return pl.pallas_call(
        functools.partial(attend_kernel, len(parts)),
        grid=(requests, heads_here),
        in_specs=[
            pl.BlockSpec(memory_space=pltpu.SMEM),
            pl.BlockSpec(
                (1, request_shares, rows, width // heads_here),
                lambda r, g: (r, 0, chunk, g),
            ),
        ]
        + [whole for _ in parts]
        + [pl.BlockSpec((None, rank_width, pair_width), lambda r, g: (g, 0, 0)), whole],
        out_specs=pl.BlockSpec((text, width // heads_here), lambda r, g: (r, g)),
        out_shape=jax.ShapeDtypeStruct((requests * text, width), jnp.bfloat16),
        scratch_shapes=[
            pltpu.VMEM((slots, head_width), jnp.bfloat16),
            pltpu.VMEM((slots, 2 * head_width), jnp.bfloat16),
        ],
        compiler_params=pltpu.CompilerParams(vmem_limit_bytes=16 * 1024 * 1024),
        cost_estimate=LIGHT,
    )(scalars, queries, *parts, kv_flat, gains)


def per_device(
    queries,
    latent_store,
    kv_up,
    q_gain,
    k_gain,
    out_weight,
    place_holder,
    place_block,
    image_count,
    serving_request,
):
    pool_size = lax.axis_size("pool")
    pool_index = lax.axis_index("pool")
    heads_size = lax.axis_size("heads")
    sub_size = lax.axis_size("sub")
    share_count = heads_size * sub_size
    share = lax.axis_index(("heads", "sub"))
    requests_here, text_rows, _ = queries.shape
    blocks_each = place_holder.shape[1]
    items = requests_here * blocks_each
    rank_width = latent_store.shape[1]
    tie = lax.optimization_barrier
    place = jnp.stack([pool_index, share]).astype(jnp.int32)
    where, pieces = fetch(place, latent_store, place_holder, place_block, serving_request, items)
    kv_flat = jnp.moveaxis(kv_up.reshape(rank_width, kv_up.shape[1], -1), 1, 0)
    gains = jnp.stack([q_gain, k_gain])
    request_ids = jnp.arange(serving_request.shape[0], dtype=jnp.int32)
    served_here = lax.dynamic_slice_in_dim(
        serving_request, pool_index * requests_here, requests_here
    )
    count_here = jnp.sum(
        jnp.where(served_here[:, None] == request_ids[None, :], image_count[None, :], 0), axis=1
    )
    scalars = jnp.concatenate([share.reshape(1), count_here])
    arriving = [swap(pieces[flip], "pool", flip) for flip in range(1, pool_size)]
    chosen = choose(where, pieces[:1] + arriving)
    chosen, kv_flat, gains, scalars = tie((chosen, kv_flat, gains, scalars))
    chosen = chosen.reshape(requests_here, -1, rank_width)
    over_heads = [chosen] + [swap(chosen, "heads", flip) for flip in range(1, heads_size)]
    parts = []
    for part in over_heads:
        parts += [part] + [swap(part, "sub", flip) for flip in range(1, sub_size)]
    part_rows = requests_here * text_rows // share_count
    shaped = queries.reshape(requests_here, share_count // requests_here, part_rows, -1)
    few = part_rows // 2
    chunk_rows = part_rows - few, few

    def attended(chunk):
        rows = chunk_rows[chunk]
        start = sum(chunk_rows[:chunk]) // rows
        return attend(start, rows, shaped, parts, kv_flat, gains, scalars)

    columns = out_weight.shape[1]
    if pool_size != 4:
        outputs = []
        for chunk in range(len(chunk_rows)):
            rows = lax.all_gather(attended(chunk), "pool", axis=0)
            mine = add_direct(
                send_direct(
                    project_out([rows[i] for i in range(pool_size)], out_weight, direct=True)
                )
            )
            mine = mine.reshape(pool_size, -1, columns)
            back = lax.all_to_all(mine, "pool", split_axis=0, concat_axis=0, tiled=True)
            outputs.append(jnp.moveaxis(back, 0, 1).reshape(-1, pool_size * columns))
        return jnp.concatenate(outputs, axis=0)

    first = attended(0)
    across0, beside0 = swap(first, "pool", 3), swap(first, "pool", 1)
    last = attended(1)
    across1, beside1 = swap(last, "pool", 3), swap(last, "pool", 1)
    own = project_out([first, last], out_weight)
    across0, beside0, own = tie((across0, beside0, own))
    second0 = second_hop(first, across0)
    near0 = send_direct(project_out([beside0, across0], out_weight, direct=True))
    across1, beside1, near0, own = tie((across1, beside1, near0, own))
    second1 = second_hop(last, across1)
    many, few = chunk_rows
    near0 = add_direct(near0)
    back0 = swap(near0[:many], "pool", 1), swap(near0[many:], "pool", 3)
    near1 = send_sub(project_out([beside1, across1], out_weight))
    second0, near1 = tie((second0, near1))
    near1 = send_heads(near1)
    far0 = send_heads(send_sub(project_out([second0], out_weight)))
    far1 = project_out([second1], out_weight)
    back0, near1, far0, far1, own = tie((back0, near1, far0, far1, own))
    near1 = add_shares(near1)
    back1 = swap(near1[:few], "pool", 1), swap(near1[few:], "pool", 3)
    back_second0 = swap(add_shares(far0), "pool", 2)
    far1 = send_heads(send_sub(far1))
    back1, back_second0, far1 = tie((back1, back_second0, far1))
    back_second1 = swap(add_shares(far1), "pool", 2)
    own = add_shares(send_heads(send_sub(own)))
    backs = [(0, 1, back0[0]), (0, 3, back0[1]), (many, 1, back1[0]), (many, 3, back1[1])]
    backs += [(0, 2, back_second0), (0, 0, own), (many, 2, back_second1)]
    output = jnp.zeros((part_rows, pool_size * columns), jnp.bfloat16)
    for row, flip, block in backs:
        output = lax.dynamic_update_slice(output, block, (row, (pool_index ^ flip) * columns))
    return output


def solution(mesh):
    in_specs = (
        P(("groups", "pool"), None, ("heads", "sub")),
        P(("groups", "pool"), None),
        P(None, ("heads", "sub"), None, None),
        P(),
        P(),
        P(("heads", "sub"), "pool"),
        P("groups", None),
        P("groups", None),
        P("groups"),
        P("groups"),
    )
    out_specs = P(("groups", "pool", "heads", "sub"), None)
    return jax.shard_map(
        per_device, mesh=mesh, in_specs=in_specs, out_specs=out_specs, check_vma=False
    )
```

```python
import functools
import math

import jax
import jax.numpy as jnp
from jax import lax
from jax.experimental import pallas as pl
from jax.experimental.pallas import tpu as pltpu
from jax.sharding import PartitionSpec as P

BLK = 128
LIGHT = pl.CostEstimate(flops=1, bytes_accessed=1, transcendentals=0)


def rms_scale(values, gain):
    return values * lax.rsqrt(jnp.mean(values * values, axis=-1, keepdims=True) + 1e-05) * gain


def swap(values, axis, flip):
    return lax.ppermute(values, axis, [(i, i ^ flip) for i in range(lax.axis_size(axis))])


def second_hop(block, across):
    index = lax.axis_index("pool")
    at_end = (index == 0) | (index == 3)
    passed = jnp.where(at_end, block, across)
    return lax.ppermute(passed, "pool", [(0, 2), (3, 1), (1, 0), (2, 3)])


def project_kernel(block_count, flips, share, *refs):
    blocks, weight, outs = refs[:block_count], refs[block_count], refs[block_count + 1 :]
    picked = []
    for flip in flips:
        for block in blocks:
            part_rows = block.shape[0] // len(flips)
            start = pl.multiple_of((share[0] ^ flip) * part_rows, part_rows)
            picked.append(block[pl.ds(start, part_rows), :])
    product = jnp.dot(
        jnp.concatenate(picked, axis=0), weight[...], preferred_element_type=jnp.float32
    )
    rows = product.shape[0] // len(outs)
    for i, out in enumerate(outs):
        out[...] = product[i * rows : (i + 1) * rows].astype(out.dtype)


def project_out(blocks, out_weight, direct=False):
    axes = ("heads", "sub")
    share_count = lax.axis_size(axes)
    share = lax.axis_index(axes).astype(jnp.int32).reshape(1)
    depth, columns = out_weight.shape
    flips = [*range(0, share_count, 2), *range(1, share_count, 2)]
    count = share_count if direct else 2
    rows = sum(block.shape[0] for block in blocks) // count
    tile = min(columns, 512)
    whole = pl.BlockSpec(memory_space=pltpu.VMEM)
    return pl.pallas_call(
        functools.partial(
            project_kernel, len(blocks), list(range(share_count)) if direct else flips
        ),
        grid=(columns // tile,),
        in_specs=[pl.BlockSpec(memory_space=pltpu.SMEM)]
        + [whole for _ in blocks]
        + [pl.BlockSpec((depth, tile), lambda n: (0, n))],
        out_specs=[pl.BlockSpec((rows, tile), lambda n: (0, n))] * count,
        out_shape=[
            jax.ShapeDtypeStruct((rows, columns), jnp.bfloat16 if i else jnp.float32)
            for i in range(count)
        ],
        compiler_params=pltpu.CompilerParams(vmem_limit_bytes=16 * 1024 * 1024),
        cost_estimate=LIGHT,
    )(share, *blocks, out_weight)


def send_direct(pieces):
    axes = ("heads", "sub")
    return [pieces[0]] + [swap(pieces[flip], axes, flip) for flip in range(1, len(pieces))]


def add_direct(pieces):
    return sum(piece.astype(jnp.float32) for piece in pieces).astype(jnp.bfloat16)


def send_sub(pieces):
    keep, away = pieces
    return keep, swap(away, "sub", 1)


def send_heads(pieces):
    keep, got = pieces
    heads_size = lax.axis_size("heads")
    rows = keep.shape[0] // heads_size
    received = []
    for flip in range(1, heads_size):
        part = slice(flip * rows, (flip + 1) * rows)
        both = keep[part] + got[part].astype(jnp.float32)
        received.append(swap(both.astype(jnp.bfloat16), "heads", flip))
    return keep, got, received


def add_shares(pieces):
    keep, got, received = pieces
    rows = keep.shape[0] // (len(received) + 1)
    total = keep[:rows] + got[:rows].astype(jnp.float32)
    return sum((part.astype(jnp.float32) for part in received), total).astype(jnp.bfloat16)


def fetch_kernel(
    place, holder, block, serving, store, where, *refs, pool_size, share_count
):
    pieces, (table, rank_of, sems) = refs[:pool_size], refs[pool_size:]
    pool_index, share = place[0], place[1]
    capacity = pieces[0].shape[0]
    blocks_each = holder.shape[1]
    requests_here = where.shape[1] // blocks_each
    spare = pool_size * capacity
    copies = []
    for flip in range(pool_size):
        for slot in range(capacity):
            table[flip * capacity + slot] = 0
        rank = 0
        for i in range(requests_here):
            request = serving[(pool_index ^ flip) * requests_here + i]
            for j in range(blocks_each):
                held = holder[request, j] == pool_index
                table[jnp.where(held, flip * capacity + rank, spare)] = block[request, j]
                rank = rank + held.astype(jnp.int32)
        for slot in range(capacity):
            index = flip * capacity + slot
            source = store.at[table[index] * share_count + share]
            copies.append(pltpu.make_async_copy(source, pieces[flip].at[slot], sems.at[index]))
            copies[-1].start()
    for i in range(pool_size):
        rank_of[i] = 0
    for i in range(requests_here):
        request = serving[pool_index * requests_here + i]
        for j in range(blocks_each):
            held_by = holder[request, j]
            where[0, i * blocks_each + j] = held_by ^ pool_index
            where[1, i * blocks_each + j] = rank_of[held_by]
            rank_of[held_by] = rank_of[held_by] + 1
    for copy in copies:
        copy.wait()


def fetch(place, latent_store, place_holder, place_block, serving_request, items):
    pool_size = lax.axis_size("pool")
    share_count = lax.axis_size(("heads", "sub"))
    capacity = 2 * ((items + pool_size - 1) // pool_size)
    rows = BLK // share_count
    store = latent_store.reshape(-1, rows, latent_store.shape[1])
    piece = jax.ShapeDtypeStruct((capacity, rows, store.shape[2]), store.dtype)
    smem = pl.BlockSpec(memory_space=pltpu.SMEM)
    where, *pieces = pl.pallas_call(
        functools.partial(fetch_kernel, pool_size=pool_size, share_count=share_count),
        in_specs=[smem] * 4 + [pl.BlockSpec(memory_space=pltpu.HBM)],
        out_specs=[smem] + [pl.BlockSpec(memory_space=pltpu.VMEM)] * pool_size,
        out_shape=[jax.ShapeDtypeStruct((2, items), jnp.int32)] + [piece] * pool_size,
        scratch_shapes=[
            pltpu.SMEM((pool_size * capacity + 1,), jnp.int32),
            pltpu.SMEM((pool_size,), jnp.int32),
            pltpu.SemaphoreType.DMA((pool_size * capacity,)),
        ],
        cost_estimate=LIGHT,
    )(place, place_holder, place_block, serving_request, store)
    return where, pieces


def choose_kernel(order, where, *refs):
    pieces, out = refs[:-1], refs[-1]
    for i in range(out.shape[0]):
        flip, slot = where[0, i], where[1, i]
        for other, piece in zip(order, pieces):

            @pl.when(flip == other)
            def _(piece=piece):
                out[i] = piece[slot]


def choose(where, pieces):
    order = [0, *range(2, len(pieces)), 1]
    whole = pl.BlockSpec(memory_space=pltpu.VMEM)
    return pl.pallas_call(
        functools.partial(choose_kernel, order),
        in_specs=[pl.BlockSpec(memory_space=pltpu.SMEM)] + [whole] * len(pieces),
        out_specs=whole,
        out_shape=jax.ShapeDtypeStruct((where.shape[1], *pieces[0].shape[1:]), pieces[0].dtype),
        compiler_params=pltpu.CompilerParams(vmem_limit_bytes=8 * 1024 * 1024),
        cost_estimate=LIGHT,
    )(where, *[pieces[flip] for flip in order])


def attend_kernel(share_count, scalars, queries, *refs):
    parts, (kv_up, gains, out, keys, values) = refs[:share_count], refs[share_count:]
    request = pl.program_id(0)
    q_gain, k_gain = gains[0:1, :], gains[1:2, :]
    head_width = gains.shape[1]
    text, width = out.shape
    per_group = width // head_width
    part_slots = parts[0].shape[1]
    share_rows = BLK // share_count
    share, count = scalars[0], scalars[1 + request]
    for flip in range(share_count):
        rows = pl.ds(flip * part_slots, part_slots)
        projected = jnp.dot(parts[flip][request], kv_up[...], preferred_element_type=jnp.float32)
        key = rms_scale(projected[:, :head_width], k_gain)
        keys[rows, :] = key.astype(jnp.bfloat16)
        slot = lax.broadcasted_iota(jnp.int32, (part_slots, head_width), 0)
        position = (slot // share_rows) * BLK + (share ^ flip) * share_rows + slot % share_rows
        live = jnp.where(position < count, 1.0, 0.0)
        values[rows, :head_width] = (projected[:, head_width:] * live).astype(jnp.bfloat16)
        values[rows, head_width:] = live.astype(jnp.bfloat16)
    scale = math.log2(math.e) / math.sqrt(head_width)
    together = min(per_group, max(1, 256 // text))
    for first in range(0, per_group, together):
        normed = []
        for head in range(first, first + together):
            query = queries[0, :, :, head * head_width : (head + 1) * head_width]
            query = query.reshape(text, head_width).astype(jnp.float32)
            normed.append(rms_scale(query, q_gain).astype(jnp.bfloat16))
        scores = lax.dot_general(
            jnp.concatenate(normed, axis=0),
            keys[...],
            (((1,), (1,)), ((), ())),
            preferred_element_type=jnp.float32,
        )
        expo = jnp.exp2(scores * scale).astype(jnp.bfloat16)
        total = jnp.dot(expo, values[...], preferred_element_type=jnp.float32)
        result = (total[:, :head_width] / total[:, head_width:]).astype(jnp.bfloat16)
        for i in range(together):
            head = first + i
            columns = slice(head * head_width, (head + 1) * head_width)
            out[:, columns] = result[i * text : (i + 1) * text]


def attend(chunk, rows, queries, parts, kv_flat, gains, scalars):
    requests, request_shares, _, width = queries.shape
    heads_here, rank_width, pair_width = kv_flat.shape
    head_width = gains.shape[1]
    slots = len(parts) * parts[0].shape[1]
    text = request_shares * rows
    whole = pl.BlockSpec(memory_space=pltpu.VMEM)
    return pl.pallas_call(
        functools.partial(attend_kernel, len(parts)),
        grid=(requests, heads_here),
        in_specs=[
            pl.BlockSpec(memory_space=pltpu.SMEM),
            pl.BlockSpec(
                (1, request_shares, rows, width // heads_here),
                lambda r, g: (r, 0, chunk, g),
            ),
        ]
        + [whole for _ in parts]
        + [pl.BlockSpec((None, rank_width, pair_width), lambda r, g: (g, 0, 0)), whole],
        out_specs=pl.BlockSpec((text, width // heads_here), lambda r, g: (r, g)),
        out_shape=jax.ShapeDtypeStruct((requests * text, width), jnp.bfloat16),
        scratch_shapes=[
            pltpu.VMEM((slots, head_width), jnp.bfloat16),
            pltpu.VMEM((slots, 2 * head_width), jnp.bfloat16),
        ],
        compiler_params=pltpu.CompilerParams(vmem_limit_bytes=16 * 1024 * 1024),
        cost_estimate=LIGHT,
    )(scalars, queries, *parts, kv_flat, gains)


def per_device(
    queries,
    latent_store,
    kv_up,
    q_gain,
    k_gain,
    out_weight,
    place_holder,
    place_block,
    image_count,
    serving_request,
):
    pool_size = lax.axis_size("pool")
    pool_index = lax.axis_index("pool")
    heads_size = lax.axis_size("heads")
    sub_size = lax.axis_size("sub")
    share_count = heads_size * sub_size
    share = lax.axis_index(("heads", "sub"))
    requests_here, text_rows, _ = queries.shape
    blocks_each = place_holder.shape[1]
    items = requests_here * blocks_each
    rank_width = latent_store.shape[1]
    tie = lax.optimization_barrier
    place = jnp.stack([pool_index, share]).astype(jnp.int32)
    where, pieces = fetch(place, latent_store, place_holder, place_block, serving_request, items)
    kv_flat = jnp.moveaxis(kv_up.reshape(rank_width, kv_up.shape[1], -1), 1, 0)
    gains = jnp.stack([q_gain, k_gain])
    request_ids = jnp.arange(serving_request.shape[0], dtype=jnp.int32)
    served_here = lax.dynamic_slice_in_dim(
        serving_request, pool_index * requests_here, requests_here
    )
    count_here = jnp.sum(
        jnp.where(served_here[:, None] == request_ids[None, :], image_count[None, :], 0), axis=1
    )
    scalars = jnp.concatenate([share.reshape(1), count_here])
    for flip in [*range(2, pool_size), 1]:
        pieces[flip] = swap(pieces[flip], "pool", flip)
    capacity = pieces[0].shape[0]
    pieces[0] = jnp.roll(pieces[0], 1, axis=0)
    local = jnp.where(where[0] == 0, 1, 0)
    where = jnp.stack([where[0], (where[1] + local) % capacity])
    chosen = choose(where, pieces)
    chosen, kv_flat, gains, scalars = tie((chosen, kv_flat, gains, scalars))
    chosen = chosen.reshape(requests_here, -1, rank_width)
    over_heads = [chosen] + [swap(chosen, "heads", flip) for flip in range(1, heads_size)]
    parts = []
    for part in over_heads:
        parts += [part] + [swap(part, "sub", flip) for flip in range(1, sub_size)]
    part_rows = requests_here * text_rows // share_count
    shaped = queries.reshape(requests_here, share_count // requests_here, part_rows, -1)
    few = part_rows // 2
    chunk_rows = part_rows - few, few

    def attended(chunk):
        rows = chunk_rows[chunk]
        start = sum(chunk_rows[:chunk]) // rows
        return attend(start, rows, shaped, parts, kv_flat, gains, scalars)

    columns = out_weight.shape[1]
    if pool_size != 4:
        outputs = []
        for chunk in range(len(chunk_rows)):
            rows = lax.all_gather(attended(chunk), "pool", axis=0)
            mine = add_direct(
                send_direct(
                    project_out([rows[i] for i in range(pool_size)], out_weight, direct=True)
                )
            )
            mine = mine.reshape(pool_size, -1, columns)
            back = lax.all_to_all(mine, "pool", split_axis=0, concat_axis=0, tiled=True)
            outputs.append(jnp.moveaxis(back, 0, 1).reshape(-1, pool_size * columns))
        return jnp.concatenate(outputs, axis=0)

    first = attended(0)
    across0, beside0 = swap(first, "pool", 3), swap(first, "pool", 1)
    last = attended(1)
    across1, beside1 = swap(last, "pool", 3), swap(last, "pool", 1)
    own = project_out([first, last], out_weight)
    across0, beside0, own = tie((across0, beside0, own))
    second0 = second_hop(first, across0)
    near0 = send_direct(project_out([beside0, across0], out_weight, direct=True))
    across1, beside1, near0, own = tie((across1, beside1, near0, own))
    second1 = second_hop(last, across1)
    many, few = chunk_rows
    near0 = add_direct(near0)
    back0 = swap(near0[:many], "pool", 1), swap(near0[many:], "pool", 3)
    near1 = send_sub(project_out([beside1, across1], out_weight))
    second0, near1 = tie((second0, near1))
    near1 = send_heads(near1)
    far0 = send_heads(send_sub(project_out([second0], out_weight)))
    far1 = project_out([second1], out_weight)
    back0, near1, far0, far1, own = tie((back0, near1, far0, far1, own))
    near1 = add_shares(near1)
    back1 = swap(near1[:few], "pool", 1), swap(near1[few:], "pool", 3)
    back_second0 = swap(add_shares(far0), "pool", 2)
    far1 = send_heads(send_sub(far1))
    own = send_heads(send_sub(own))
    back1, back_second0, far1, own = tie((back1, back_second0, far1, own))
    back_second1 = swap(add_shares(far1), "pool", 2)
    own = add_shares(own)
    backs = [(0, 1, back0[0]), (0, 3, back0[1]), (many, 1, back1[0]), (many, 3, back1[1])]
    backs += [(0, 2, back_second0), (0, 0, own), (many, 2, back_second1)]
    output = jnp.zeros((part_rows, pool_size * columns), jnp.bfloat16)
    for row, flip, block in backs:
        output = lax.dynamic_update_slice(output, block, (row, (pool_index ^ flip) * columns))
    return output


def solution(mesh):
    in_specs = (
        P(("groups", "pool"), None, ("heads", "sub")),
        P(("groups", "pool"), None),
        P(None, ("heads", "sub"), None, None),
        P(),
        P(),
        P(("heads", "sub"), "pool"),
        P("groups", None),
        P("groups", None),
        P("groups"),
        P("groups"),
    )
    out_specs = P(("groups", "pool", "heads", "sub"), None)
    return jax.shard_map(
        per_device, mesh=mesh, in_specs=in_specs, out_specs=out_specs, check_vma=False
    )
```

```python
import functools
import math

import jax
import jax.numpy as jnp
from jax import lax
from jax.experimental import pallas as pl
from jax.experimental.pallas import tpu as pltpu
from jax.sharding import PartitionSpec as P

BLK = 128
LIGHT = pl.CostEstimate(flops=1, bytes_accessed=1, transcendentals=0)


def rms_scale(values, gain):
    return values * lax.rsqrt(jnp.mean(values * values, axis=-1, keepdims=True) + 1e-05) * gain


def swap(values, axis, flip):
    return lax.ppermute(values, axis, [(i, i ^ flip) for i in range(lax.axis_size(axis))])


def second_hop(block, across):
    index = lax.axis_index("pool")
    at_end = (index == 0) | (index == 3)
    passed = jnp.where(at_end, block, across)
    return lax.ppermute(passed, "pool", [(0, 2), (3, 1), (1, 0), (2, 3)])


def project_kernel(block_count, flips, share, *refs):
    blocks, weight, outs = refs[:block_count], refs[block_count], refs[block_count + 1 :]
    picked = []
    for flip in flips:
        for block in blocks:
            part_rows = block.shape[0] // len(flips)
            start = pl.multiple_of((share[0] ^ flip) * part_rows, part_rows)
            picked.append(block[pl.ds(start, part_rows), :])
    product = jnp.dot(
        jnp.concatenate(picked, axis=0), weight[...], preferred_element_type=jnp.float32
    )
    rows = product.shape[0] // len(outs)
    for i, out in enumerate(outs):
        out[...] = product[i * rows : (i + 1) * rows].astype(out.dtype)


def project_out(blocks, out_weight, direct=False):
    axes = ("heads", "sub")
    share_count = lax.axis_size(axes)
    share = lax.axis_index(axes).astype(jnp.int32).reshape(1)
    depth, columns = out_weight.shape
    flips = [*range(0, share_count, 2), *range(1, share_count, 2)]
    count = share_count if direct else 2
    rows = sum(block.shape[0] for block in blocks) // count
    tile = min(columns, 512)
    whole = pl.BlockSpec(memory_space=pltpu.VMEM)
    return pl.pallas_call(
        functools.partial(
            project_kernel, len(blocks), list(range(share_count)) if direct else flips
        ),
        grid=(columns // tile,),
        in_specs=[pl.BlockSpec(memory_space=pltpu.SMEM)]
        + [whole for _ in blocks]
        + [pl.BlockSpec((depth, tile), lambda n: (0, n))],
        out_specs=[pl.BlockSpec((rows, tile), lambda n: (0, n))] * count,
        out_shape=[
            jax.ShapeDtypeStruct((rows, columns), jnp.bfloat16 if i else jnp.float32)
            for i in range(count)
        ],
        compiler_params=pltpu.CompilerParams(vmem_limit_bytes=10 * 1024 * 1024),
        cost_estimate=LIGHT,
    )(share, *blocks, out_weight)


def send_direct(pieces):
    axes = ("heads", "sub")
    return [pieces[0]] + [swap(pieces[flip], axes, flip) for flip in range(1, len(pieces))]


def add_direct(pieces):
    return sum(piece.astype(jnp.float32) for piece in pieces).astype(jnp.bfloat16)


def send_sub(pieces):
    keep, away = pieces
    return keep, swap(away, "sub", 1)


def send_heads(pieces):
    keep, got = pieces
    heads_size = lax.axis_size("heads")
    rows = keep.shape[0] // heads_size
    received = []
    for flip in range(1, heads_size):
        part = slice(flip * rows, (flip + 1) * rows)
        both = keep[part] + got[part].astype(jnp.float32)
        received.append(swap(both.astype(jnp.bfloat16), "heads", flip))
    return keep, got, received


def add_shares(pieces):
    keep, got, received = pieces
    rows = keep.shape[0] // (len(received) + 1)
    total = keep[:rows] + got[:rows].astype(jnp.float32)
    return sum((part.astype(jnp.float32) for part in received), total).astype(jnp.bfloat16)


def fetch_kernel(
    place, holder, block, serving, store, where, *refs, pool_size, share_count
):
    pieces, (table, rank_of, sems) = refs[:pool_size], refs[pool_size:]
    pool_index, share = place[0], place[1]
    capacity = pieces[0].shape[0]
    blocks_each = holder.shape[1]
    requests_here = where.shape[1] // blocks_each
    spare = pool_size * capacity
    copies = []
    for flip in range(pool_size):
        for slot in range(capacity):
            table[flip * capacity + slot] = 0
        rank = 0
        for i in range(requests_here):
            request = serving[(pool_index ^ flip) * requests_here + i]
            for j in range(blocks_each):
                held = holder[request, j] == pool_index
                table[jnp.where(held, flip * capacity + rank, spare)] = block[request, j]
                rank = rank + held.astype(jnp.int32)
        for slot in range(capacity):
            index = flip * capacity + slot
            source = store.at[table[index] * share_count + share]
            copies.append(pltpu.make_async_copy(source, pieces[flip].at[slot], sems.at[index]))
            copies[-1].start()
    for i in range(pool_size):
        rank_of[i] = 0
    for i in range(requests_here):
        request = serving[pool_index * requests_here + i]
        for j in range(blocks_each):
            held_by = holder[request, j]
            where[0, i * blocks_each + j] = held_by ^ pool_index
            where[1, i * blocks_each + j] = rank_of[held_by]
            rank_of[held_by] = rank_of[held_by] + 1
    for copy in copies:
        copy.wait()


def fetch(place, latent_store, place_holder, place_block, serving_request, items):
    pool_size = lax.axis_size("pool")
    share_count = lax.axis_size(("heads", "sub"))
    capacity = 2 * ((items + pool_size - 1) // pool_size)
    rows = BLK // share_count
    store = latent_store.reshape(-1, rows, latent_store.shape[1])
    piece = jax.ShapeDtypeStruct((capacity, rows, store.shape[2]), store.dtype)
    smem = pl.BlockSpec(memory_space=pltpu.SMEM)
    where, *pieces = pl.pallas_call(
        functools.partial(fetch_kernel, pool_size=pool_size, share_count=share_count),
        in_specs=[smem] * 4 + [pl.BlockSpec(memory_space=pltpu.HBM)],
        out_specs=[smem] + [pl.BlockSpec(memory_space=pltpu.VMEM)] * pool_size,
        out_shape=[jax.ShapeDtypeStruct((2, items), jnp.int32)] + [piece] * pool_size,
        scratch_shapes=[
            pltpu.SMEM((pool_size * capacity + 1,), jnp.int32),
            pltpu.SMEM((pool_size,), jnp.int32),
            pltpu.SemaphoreType.DMA((pool_size * capacity,)),
        ],
        cost_estimate=LIGHT,
    )(place, place_holder, place_block, serving_request, store)
    return where, pieces


def choose_kernel(order, where, *refs):
    pieces, out = refs[:-1], refs[-1]
    for i in range(out.shape[0]):
        flip, slot = where[0, i], where[1, i]
        for other, piece in zip(order, pieces):

            @pl.when(flip == other)
            def _(piece=piece):
                out[i] = piece[slot]


def choose(where, pieces):
    order = [0, *range(2, len(pieces)), 1]
    whole = pl.BlockSpec(memory_space=pltpu.VMEM)
    return pl.pallas_call(
        functools.partial(choose_kernel, order),
        in_specs=[pl.BlockSpec(memory_space=pltpu.SMEM)] + [whole] * len(pieces),
        out_specs=whole,
        out_shape=jax.ShapeDtypeStruct((where.shape[1], *pieces[0].shape[1:]), pieces[0].dtype),
        compiler_params=pltpu.CompilerParams(vmem_limit_bytes=8 * 1024 * 1024),
        cost_estimate=LIGHT,
    )(where, *[pieces[flip] for flip in order])


def attend_kernel(share_count, scalars, queries, *refs):
    parts, (kv_up, gains, out, keys, values) = refs[:share_count], refs[share_count:]
    request = pl.program_id(0)
    q_gain, k_gain = gains[0:1, :], gains[1:2, :]
    head_width = gains.shape[1]
    text, width = out.shape
    per_group = width // head_width
    part_slots = parts[0].shape[1]
    share_rows = BLK // share_count
    share, count = scalars[0], scalars[1 + request]
    slot = lax.broadcasted_iota(jnp.int32, (part_slots, head_width), 0)
    position = (slot // share_rows) * BLK + slot % share_rows
    for flip in range(share_count):
        rows = pl.ds(flip * part_slots, part_slots)
        projected = jnp.dot(parts[flip][request], kv_up[...], preferred_element_type=jnp.float32)
        key = rms_scale(projected[:, :head_width], k_gain)
        keys[rows, :] = key.astype(jnp.bfloat16)
        live = jnp.where(position < count - (share ^ flip) * share_rows, 1.0, 0.0)
        values[rows, :head_width] = (projected[:, head_width:] * live).astype(jnp.bfloat16)
        values[rows, head_width:] = live.astype(jnp.bfloat16)
    scale = math.log2(math.e) / math.sqrt(head_width)
    together = min(per_group, max(1, 256 // text))
    for first in range(0, per_group, together):
        normed = []
        for head in range(first, first + together):
            query = queries[0, :, :, head * head_width : (head + 1) * head_width]
            query = query.reshape(text, head_width).astype(jnp.float32)
            normed.append(rms_scale(query, q_gain).astype(jnp.bfloat16))
        scores = lax.dot_general(
            jnp.concatenate(normed, axis=0),
            keys[...],
            (((1,), (1,)), ((), ())),
            preferred_element_type=jnp.float32,
        )
        expo = jnp.exp2(scores * scale).astype(jnp.bfloat16)
        total = jnp.dot(expo, values[...], preferred_element_type=jnp.float32)
        result = (total[:, :head_width] / total[:, head_width:]).astype(jnp.bfloat16)
        for i in range(together):
            head = first + i
            columns = slice(head * head_width, (head + 1) * head_width)
            out[:, columns] = result[i * text : (i + 1) * text]


def attend(chunk, rows, queries, parts, kv_flat, gains, scalars):
    requests, request_shares, _, width = queries.shape
    heads_here, rank_width, pair_width = kv_flat.shape
    head_width = gains.shape[1]
    slots = len(parts) * parts[0].shape[1]
    text = request_shares * rows
    whole = pl.BlockSpec(memory_space=pltpu.VMEM)
    return pl.pallas_call(
        functools.partial(attend_kernel, len(parts)),
        grid=(requests, heads_here),
        in_specs=[
            pl.BlockSpec(memory_space=pltpu.SMEM),
            pl.BlockSpec(
                (1, request_shares, rows, width // heads_here),
                lambda r, g: (r, 0, chunk, g),
            ),
        ]
        + [whole for _ in parts]
        + [pl.BlockSpec((None, rank_width, pair_width), lambda r, g: (g, 0, 0)), whole],
        out_specs=pl.BlockSpec((text, width // heads_here), lambda r, g: (r, g)),
        out_shape=jax.ShapeDtypeStruct((requests * text, width), jnp.bfloat16),
        scratch_shapes=[
            pltpu.VMEM((slots, head_width), jnp.bfloat16),
            pltpu.VMEM((slots, 2 * head_width), jnp.bfloat16),
        ],
        compiler_params=pltpu.CompilerParams(vmem_limit_bytes=12 * 1024 * 1024),
        cost_estimate=LIGHT,
    )(scalars, queries, *parts, kv_flat, gains)


def per_device(
    queries,
    latent_store,
    kv_up,
    q_gain,
    k_gain,
    out_weight,
    place_holder,
    place_block,
    image_count,
    serving_request,
):
    pool_size = lax.axis_size("pool")
    pool_index = lax.axis_index("pool")
    heads_size = lax.axis_size("heads")
    sub_size = lax.axis_size("sub")
    share_count = heads_size * sub_size
    share = lax.axis_index(("heads", "sub"))
    requests_here, text_rows, _ = queries.shape
    blocks_each = place_holder.shape[1]
    items = requests_here * blocks_each
    rank_width = latent_store.shape[1]
    tie = lax.optimization_barrier
    place = jnp.stack([pool_index, share]).astype(jnp.int32)
    where, pieces = fetch(place, latent_store, place_holder, place_block, serving_request, items)
    kv_flat = jnp.moveaxis(kv_up.reshape(rank_width, kv_up.shape[1], -1), 1, 0)
    gains = jnp.stack([q_gain, k_gain])
    request_ids = jnp.arange(serving_request.shape[0], dtype=jnp.int32)
    served_here = lax.dynamic_slice_in_dim(
        serving_request, pool_index * requests_here, requests_here
    )
    count_here = jnp.sum(
        jnp.where(served_here[:, None] == request_ids[None, :], image_count[None, :], 0), axis=1
    )
    scalars = jnp.concatenate([share.reshape(1), count_here])
    for flip in [*range(2, pool_size), 1]:
        pieces[flip] = swap(pieces[flip], "pool", flip)
    capacity = pieces[0].shape[0]
    pieces[0] = jnp.roll(pieces[0], 1, axis=0)
    local = jnp.where(where[0] == 0, 1, 0)
    where = jnp.stack([where[0], (where[1] + local) % capacity])
    chosen = choose(where, pieces)
    chosen, kv_flat, gains, scalars = tie((chosen, kv_flat, gains, scalars))
    chosen = chosen.reshape(requests_here, -1, rank_width)
    over_heads = [chosen] + [swap(chosen, "heads", flip) for flip in range(1, heads_size)]
    parts = []
    for part in over_heads:
        parts += [part] + [swap(part, "sub", flip) for flip in range(1, sub_size)]
    part_rows = requests_here * text_rows // share_count
    shaped = queries.reshape(requests_here, share_count // requests_here, part_rows, -1)
    few = part_rows // 2
    chunk_rows = part_rows - few, few

    def attended(chunk):
        rows = chunk_rows[chunk]
        start = sum(chunk_rows[:chunk]) // rows
        return attend(start, rows, shaped, parts, kv_flat, gains, scalars)

    columns = out_weight.shape[1]
    if pool_size != 4:
        outputs = []
        for chunk in range(len(chunk_rows)):
            rows = lax.all_gather(attended(chunk), "pool", axis=0)
            mine = add_direct(
                send_direct(
                    project_out([rows[i] for i in range(pool_size)], out_weight, direct=True)
                )
            )
            mine = mine.reshape(pool_size, -1, columns)
            back = lax.all_to_all(mine, "pool", split_axis=0, concat_axis=0, tiled=True)
            outputs.append(jnp.moveaxis(back, 0, 1).reshape(-1, pool_size * columns))
        return jnp.concatenate(outputs, axis=0)

    first = attended(0)
    across0, beside0 = swap(first, "pool", 3), swap(first, "pool", 1)
    last = attended(1)
    across1, beside1 = swap(last, "pool", 3), swap(last, "pool", 1)
    own = project_out([first, last], out_weight)
    across0, beside0, own = tie((across0, beside0, own))
    second0 = second_hop(first, across0)
    near0 = send_direct(project_out([beside0, across0], out_weight, direct=True))
    across1, beside1, near0, own = tie((across1, beside1, near0, own))
    second1 = second_hop(last, across1)
    many, few = chunk_rows
    near0 = add_direct(near0)
    back0 = swap(near0[:many], "pool", 1), swap(near0[many:], "pool", 3)
    near1 = send_sub(project_out([beside1, across1], out_weight))
    second0, near1 = tie((second0, near1))
    near1 = send_heads(near1)
    far0 = send_heads(send_sub(project_out([second0], out_weight)))
    far1 = project_out([second1], out_weight)
    back0, near1, far0, far1, own = tie((back0, near1, far0, far1, own))
    near1 = add_shares(near1)
    back1 = swap(near1[:few], "pool", 1), swap(near1[few:], "pool", 3)
    back_second0 = swap(add_shares(far0), "pool", 2)
    far1 = send_heads(send_sub(far1))
    own = send_heads(send_sub(own))
    back1, back_second0, far1, own = tie((back1, back_second0, far1, own))
    back_second1 = swap(add_shares(far1), "pool", 2)
    own = add_shares(own)
    backs = [(0, 1, back0[0]), (0, 3, back0[1]), (many, 1, back1[0]), (many, 3, back1[1])]
    backs += [(0, 2, back_second0), (0, 0, own), (many, 2, back_second1)]
    output = jnp.zeros((part_rows, pool_size * columns), jnp.bfloat16)
    for row, flip, block in backs:
        output = lax.dynamic_update_slice(output, block, (row, (pool_index ^ flip) * columns))
    return output


def solution(mesh):
    in_specs = (
        P(("groups", "pool"), None, ("heads", "sub")),
        P(("groups", "pool"), None),
        P(None, ("heads", "sub"), None, None),
        P(),
        P(),
        P(("heads", "sub"), "pool"),
        P("groups", None),
        P("groups", None),
        P("groups"),
        P("groups"),
    )
    out_specs = P(("groups", "pool", "heads", "sub"), None)
    return jax.shard_map(
        per_device, mesh=mesh, in_specs=in_specs, out_specs=out_specs, check_vma=False
    )
```

```python
import functools
import math

import jax
import jax.numpy as jnp
from jax import lax
from jax.experimental import pallas as pl
from jax.experimental.pallas import tpu as pltpu
from jax.sharding import PartitionSpec as P

BLK = 128
LIGHT = pl.CostEstimate(flops=1, bytes_accessed=1, transcendentals=0)


def rms_scale(values, gain):
    return values * lax.rsqrt(jnp.mean(values * values, axis=-1, keepdims=True) + 1e-05) * gain


def swap(values, axis, flip):
    return lax.ppermute(values, axis, [(i, i ^ flip) for i in range(lax.axis_size(axis))])


def second_hop(block, across):
    index = lax.axis_index("pool")
    at_end = (index == 0) | (index == 3)
    passed = jnp.where(at_end, block, across)
    return lax.ppermute(passed, "pool", [(0, 2), (3, 1), (1, 0), (2, 3)])


def project_kernel(block_count, flips, share, *refs):
    blocks, weight, outs = refs[:block_count], refs[block_count], refs[block_count + 1 :]
    picked = []
    for flip in flips:
        for block in blocks:
            part_rows = block.shape[0] // len(flips)
            start = pl.multiple_of((share[0] ^ flip) * part_rows, part_rows)
            picked.append(block[pl.ds(start, part_rows), :])
    product = jnp.dot(
        jnp.concatenate(picked, axis=0), weight[...], preferred_element_type=jnp.float32
    )
    rows = product.shape[0] // len(outs)
    for i, out in enumerate(outs):
        out[...] = product[i * rows : (i + 1) * rows].astype(out.dtype)


def project_out(blocks, out_weight, direct=False):
    axes = ("heads", "sub")
    share_count = lax.axis_size(axes)
    share = lax.axis_index(axes).astype(jnp.int32).reshape(1)
    depth, columns = out_weight.shape
    flips = [*range(0, share_count, 2), *range(1, share_count, 2)]
    count = share_count if direct else 2
    rows = sum(block.shape[0] for block in blocks) // count
    tile = min(columns, 512)
    whole = pl.BlockSpec(memory_space=pltpu.VMEM)
    return pl.pallas_call(
        functools.partial(
            project_kernel, len(blocks), list(range(share_count)) if direct else flips
        ),
        grid=(columns // tile,),
        in_specs=[pl.BlockSpec(memory_space=pltpu.SMEM)]
        + [whole for _ in blocks]
        + [pl.BlockSpec((depth, tile), lambda n: (0, n))],
        out_specs=[pl.BlockSpec((rows, tile), lambda n: (0, n))] * count,
        out_shape=[
            jax.ShapeDtypeStruct((rows, columns), jnp.bfloat16 if i else jnp.float32)
            for i in range(count)
        ],
        compiler_params=pltpu.CompilerParams(vmem_limit_bytes=10 * 1024 * 1024),
        cost_estimate=LIGHT,
    )(share, *blocks, out_weight)


def send_direct(pieces):
    axes = ("heads", "sub")
    return [pieces[0]] + [swap(pieces[flip], axes, flip) for flip in range(1, len(pieces))]


def add_direct(pieces):
    return sum(piece.astype(jnp.float32) for piece in pieces).astype(jnp.bfloat16)


def send_sub(pieces):
    keep, away = pieces
    return keep, swap(away, "sub", 1)


def send_heads(pieces):
    keep, got = pieces
    heads_size = lax.axis_size("heads")
    rows = keep.shape[0] // heads_size
    received = []
    for flip in range(1, heads_size):
        part = slice(flip * rows, (flip + 1) * rows)
        both = keep[part] + got[part].astype(jnp.float32)
        received.append(swap(both.astype(jnp.bfloat16), "heads", flip))
    return keep, got, received


def add_shares(pieces):
    keep, got, received = pieces
    rows = keep.shape[0] // (len(received) + 1)
    total = keep[:rows] + got[:rows].astype(jnp.float32)
    return sum((part.astype(jnp.float32) for part in received), total).astype(jnp.bfloat16)


def fetch_kernel(
    place, holder, block, serving, store, where, *refs, pool_size, share_count
):
    pieces, (table, rank_of, sems) = refs[:pool_size], refs[pool_size:]
    pool_index, share = place[0], place[1]
    capacity = pieces[0].shape[0]
    blocks_each = holder.shape[1]
    requests_here = where.shape[1] // blocks_each
    spare = pool_size * capacity
    copies = []
    for flip in range(pool_size):
        for slot in range(capacity):
            table[flip * capacity + slot] = 0
        rank = 0
        for i in range(requests_here):
            request = serving[(pool_index ^ flip) * requests_here + i]
            for j in range(blocks_each):
                held = holder[request, j] == pool_index
                table[jnp.where(held, flip * capacity + rank, spare)] = block[request, j]
                rank = rank + held.astype(jnp.int32)
        for slot in range(capacity):
            index = flip * capacity + slot
            source = store.at[table[index] * share_count + share]
            copies.append(pltpu.make_async_copy(source, pieces[flip].at[slot], sems.at[index]))
            copies[-1].start()
    for i in range(pool_size):
        rank_of[i] = 0
    for i in range(requests_here):
        request = serving[pool_index * requests_here + i]
        for j in range(blocks_each):
            held_by = holder[request, j]
            where[0, i * blocks_each + j] = held_by ^ pool_index
            where[1, i * blocks_each + j] = rank_of[held_by]
            rank_of[held_by] = rank_of[held_by] + 1
    for copy in copies:
        copy.wait()


def fetch(place, latent_store, place_holder, place_block, serving_request, items):
    pool_size = lax.axis_size("pool")
    share_count = lax.axis_size(("heads", "sub"))
    capacity = 2 * ((items + pool_size - 1) // pool_size)
    rows = BLK // share_count
    store = latent_store.reshape(-1, rows, latent_store.shape[1])
    piece = jax.ShapeDtypeStruct((capacity, rows, store.shape[2]), store.dtype)
    smem = pl.BlockSpec(memory_space=pltpu.SMEM)
    where, *pieces = pl.pallas_call(
        functools.partial(fetch_kernel, pool_size=pool_size, share_count=share_count),
        in_specs=[smem] * 4 + [pl.BlockSpec(memory_space=pltpu.HBM)],
        out_specs=[smem] + [pl.BlockSpec(memory_space=pltpu.VMEM)] * pool_size,
        out_shape=[jax.ShapeDtypeStruct((2, items), jnp.int32)] + [piece] * pool_size,
        scratch_shapes=[
            pltpu.SMEM((pool_size * capacity + 1,), jnp.int32),
            pltpu.SMEM((pool_size,), jnp.int32),
            pltpu.SemaphoreType.DMA((pool_size * capacity,)),
        ],
        cost_estimate=LIGHT,
    )(place, place_holder, place_block, serving_request, store)
    return where, pieces


def choose_kernel(order, where, *refs):
    pieces, out = refs[:-1], refs[-1]
    for i in range(out.shape[0]):
        flip, slot = where[0, i], where[1, i]
        for other, piece in zip(order, pieces):

            @pl.when(flip == other)
            def _(piece=piece):
                out[i] = piece[slot]


def choose(where, pieces):
    order = [0, *range(2, len(pieces)), 1]
    whole = pl.BlockSpec(memory_space=pltpu.VMEM)
    return pl.pallas_call(
        functools.partial(choose_kernel, order),
        in_specs=[pl.BlockSpec(memory_space=pltpu.SMEM)] + [whole] * len(pieces),
        out_specs=whole,
        out_shape=jax.ShapeDtypeStruct((where.shape[1], *pieces[0].shape[1:]), pieces[0].dtype),
        compiler_params=pltpu.CompilerParams(vmem_limit_bytes=8 * 1024 * 1024),
        cost_estimate=LIGHT,
    )(where, *[pieces[flip] for flip in order])


def attend_kernel(start, rows, share_count, scalars, queries, *refs):
    parts, (kv_up, gains, out, keys, values) = refs[:share_count], refs[share_count:]
    q_gain, k_gain = gains[0:1, :], gains[1:2, :]
    requests, request_shares, _, width = queries.shape
    heads_here = kv_up.shape[0]
    head_width = gains.shape[1]
    text = request_shares * rows
    per_group = width // heads_here // head_width
    part_slots = parts[0].shape[1]
    share_rows = BLK // share_count
    share = scalars[0]
    slot = lax.broadcasted_iota(jnp.int32, (part_slots, head_width), 0)
    position = (slot // share_rows) * BLK + slot % share_rows
    scale = math.log2(math.e) / math.sqrt(head_width)
    together = min(per_group, max(1, 256 // text))
    for request in range(requests):
        count = scalars[1 + request]
        for flip in range(share_count):
            run = pl.ds(flip * part_slots, part_slots)
            live = jnp.where(position < count - (share ^ flip) * share_rows, 1.0, 0.0)
            for group in range(heads_here):
                pair = request * heads_here + group
                projected = jnp.dot(
                    parts[flip][request], kv_up[group], preferred_element_type=jnp.float32
                )
                key = rms_scale(projected[:, :head_width], k_gain)
                keys[pair, run, :] = key.astype(jnp.bfloat16)
                value = projected[:, head_width:] * live
                values[pair, run, :head_width] = value.astype(jnp.bfloat16)
                values[pair, run, head_width:] = live.astype(jnp.bfloat16)
        for group in range(heads_here):
            pair = request * heads_here + group
            for first in range(group * per_group, (group + 1) * per_group, together):
                normed = []
                for head in range(first, first + together):
                    columns = slice(head * head_width, (head + 1) * head_width)
                    query = queries[request, :, start : start + rows, columns]
                    query = query.reshape(text, head_width).astype(jnp.float32)
                    normed.append(rms_scale(query, q_gain).astype(jnp.bfloat16))
                scores = lax.dot_general(
                    jnp.concatenate(normed, axis=0),
                    keys[pair],
                    (((1,), (1,)), ((), ())),
                    preferred_element_type=jnp.float32,
                )
                expo = jnp.exp2(scores * scale).astype(jnp.bfloat16)
                total = jnp.dot(expo, values[pair], preferred_element_type=jnp.float32)
                result = (total[:, :head_width] / total[:, head_width:]).astype(jnp.bfloat16)
                for i in range(together):
                    head = first + i
                    columns = slice(head * head_width, (head + 1) * head_width)
                    out[request * text : (request + 1) * text, columns] = result[
                        i * text : (i + 1) * text
                    ]


def attend(start, rows, queries, parts, kv_flat, gains, scalars):
    requests, request_shares, _, width = queries.shape
    heads_here = kv_flat.shape[0]
    head_width = gains.shape[1]
    slots = len(parts) * parts[0].shape[1]
    whole = pl.BlockSpec(memory_space=pltpu.VMEM)
    return pl.pallas_call(
        functools.partial(attend_kernel, start, rows, len(parts)),
        in_specs=[pl.BlockSpec(memory_space=pltpu.SMEM)] + [whole] * (len(parts) + 3),
        out_specs=whole,
        out_shape=jax.ShapeDtypeStruct((requests * request_shares * rows, width), jnp.bfloat16),
        scratch_shapes=[
            pltpu.VMEM((requests * heads_here, slots, head_width), jnp.bfloat16),
            pltpu.VMEM((requests * heads_here, slots, 2 * head_width), jnp.bfloat16),
        ],
        compiler_params=pltpu.CompilerParams(vmem_limit_bytes=20 * 1024 * 1024),
        cost_estimate=LIGHT,
    )(scalars, queries, *parts, kv_flat, gains)


def per_device(
    queries,
    latent_store,
    kv_up,
    q_gain,
    k_gain,
    out_weight,
    place_holder,
    place_block,
    image_count,
    serving_request,
):
    pool_size = lax.axis_size("pool")
    pool_index = lax.axis_index("pool")
    heads_size = lax.axis_size("heads")
    sub_size = lax.axis_size("sub")
    share_count = heads_size * sub_size
    share = lax.axis_index(("heads", "sub"))
    requests_here, text_rows, _ = queries.shape
    blocks_each = place_holder.shape[1]
    items = requests_here * blocks_each
    rank_width = latent_store.shape[1]
    tie = lax.optimization_barrier
    place = jnp.stack([pool_index, share]).astype(jnp.int32)
    where, pieces = fetch(place, latent_store, place_holder, place_block, serving_request, items)
    kv_flat = jnp.moveaxis(kv_up.reshape(rank_width, kv_up.shape[1], -1), 1, 0)
    gains = jnp.stack([q_gain, k_gain])
    request_ids = jnp.arange(serving_request.shape[0], dtype=jnp.int32)
    served_here = lax.dynamic_slice_in_dim(
        serving_request, pool_index * requests_here, requests_here
    )
    count_here = jnp.sum(
        jnp.where(served_here[:, None] == request_ids[None, :], image_count[None, :], 0), axis=1
    )
    scalars = jnp.concatenate([share.reshape(1), count_here])
    for flip in [*range(2, pool_size), 1]:
        pieces[flip] = swap(pieces[flip], "pool", flip)
    capacity = pieces[0].shape[0]
    pieces[0] = jnp.roll(pieces[0], 1, axis=0)
    local = jnp.where(where[0] == 0, 1, 0)
    where = jnp.stack([where[0], (where[1] + local) % capacity])
    chosen = choose(where, pieces)
    chosen, kv_flat, gains, scalars = tie((chosen, kv_flat, gains, scalars))
    chosen = chosen.reshape(requests_here, -1, rank_width)
    over_heads = [chosen] + [swap(chosen, "heads", flip) for flip in range(1, heads_size)]
    parts = []
    for part in over_heads:
        parts += [part] + [swap(part, "sub", flip) for flip in range(1, sub_size)]
    part_rows = requests_here * text_rows // share_count
    shaped = queries.reshape(requests_here, share_count // requests_here, part_rows, -1)
    few = part_rows // 2
    chunk_rows = part_rows - few, few

    def attended(chunk):
        rows = chunk_rows[chunk]
        start = sum(chunk_rows[:chunk])
        return attend(start, rows, shaped, parts, kv_flat, gains, scalars)

    columns = out_weight.shape[1]
    if pool_size != 4:
        outputs = []
        for chunk in range(len(chunk_rows)):
            rows = lax.all_gather(attended(chunk), "pool", axis=0)
            mine = add_direct(
                send_direct(
                    project_out([rows[i] for i in range(pool_size)], out_weight, direct=True)
                )
            )
            mine = mine.reshape(pool_size, -1, columns)
            back = lax.all_to_all(mine, "pool", split_axis=0, concat_axis=0, tiled=True)
            outputs.append(jnp.moveaxis(back, 0, 1).reshape(-1, pool_size * columns))
        return jnp.concatenate(outputs, axis=0)

    first = attended(0)
    across0, beside0 = swap(first, "pool", 3), swap(first, "pool", 1)
    last = attended(1)
    across1, beside1 = swap(last, "pool", 3), swap(last, "pool", 1)
    own = project_out([first, last], out_weight)
    across0, beside0, own = tie((across0, beside0, own))
    second0 = second_hop(first, across0)
    near0 = send_direct(project_out([beside0, across0], out_weight, direct=True))
    across1, beside1, near0, own = tie((across1, beside1, near0, own))
    second1 = second_hop(last, across1)
    many, few = chunk_rows
    near0 = add_direct(near0)
    back0 = swap(near0[:many], "pool", 1), swap(near0[many:], "pool", 3)
    near1 = send_sub(project_out([beside1, across1], out_weight))
    second0, near1 = tie((second0, near1))
    near1 = send_heads(near1)
    far0 = send_heads(send_sub(project_out([second0], out_weight)))
    far1 = project_out([second1], out_weight)
    back0, near1, far0, far1, own = tie((back0, near1, far0, far1, own))
    near1 = add_shares(near1)
    back1 = swap(near1[:few], "pool", 1), swap(near1[few:], "pool", 3)
    back_second0 = swap(add_shares(far0), "pool", 2)
    far1 = send_heads(send_sub(far1))
    own = send_heads(send_sub(own))
    back1, back_second0, far1, own = tie((back1, back_second0, far1, own))
    back_second1 = swap(add_shares(far1), "pool", 2)
    own = add_shares(own)
    backs = [(0, 1, back0[0]), (0, 3, back0[1]), (many, 1, back1[0]), (many, 3, back1[1])]
    backs += [(0, 2, back_second0), (0, 0, own), (many, 2, back_second1)]
    output = jnp.zeros((part_rows, pool_size * columns), jnp.bfloat16)
    for row, flip, block in backs:
        output = lax.dynamic_update_slice(output, block, (row, (pool_index ^ flip) * columns))
    return output


def solution(mesh):
    in_specs = (
        P(("groups", "pool"), None, ("heads", "sub")),
        P(("groups", "pool"), None),
        P(None, ("heads", "sub"), None, None),
        P(),
        P(),
        P(("heads", "sub"), "pool"),
        P("groups", None),
        P("groups", None),
        P("groups"),
        P("groups"),
    )
    out_specs = P(("groups", "pool", "heads", "sub"), None)
    return jax.shard_map(
        per_device, mesh=mesh, in_specs=in_specs, out_specs=out_specs, check_vma=False
    )
```

```python
import functools
import math

import jax
import jax.numpy as jnp
from jax import lax
from jax.experimental import pallas as pl
from jax.experimental.pallas import tpu as pltpu
from jax.sharding import PartitionSpec as P

BLK = 128
LIGHT = pl.CostEstimate(flops=1, bytes_accessed=1, transcendentals=0)


def rms_scale(values, gain):
    return values * lax.rsqrt(jnp.mean(values * values, axis=-1, keepdims=True) + 1e-05) * gain


def swap(values, axis, flip):
    return lax.ppermute(values, axis, [(i, i ^ flip) for i in range(lax.axis_size(axis))])


def second_hop(block, across):
    index = lax.axis_index("pool")
    at_end = (index == 0) | (index == 3)
    passed = jnp.where(at_end, block, across)
    return lax.ppermute(passed, "pool", [(0, 2), (3, 1), (1, 0), (2, 3)])


def project_kernel(block_count, flips, share, *refs):
    blocks, weight, outs = refs[:block_count], refs[block_count], refs[block_count + 1 :]
    picked = []
    for flip in flips:
        for block in blocks:
            part_rows = block.shape[0] // len(flips)
            start = pl.multiple_of((share[0] ^ flip) * part_rows, part_rows)
            picked.append(block[pl.ds(start, part_rows), :])
    product = jnp.dot(
        jnp.concatenate(picked, axis=0), weight[...], preferred_element_type=jnp.float32
    )
    rows = product.shape[0] // len(outs)
    for i, out in enumerate(outs):
        out[...] = product[i * rows : (i + 1) * rows].astype(out.dtype)


def project_out(blocks, out_weight, direct=False):
    axes = ("heads", "sub")
    share_count = lax.axis_size(axes)
    share = lax.axis_index(axes).astype(jnp.int32).reshape(1)
    depth, columns = out_weight.shape
    flips = [*range(0, share_count, 2), *range(1, share_count, 2)]
    count = share_count if direct else 2
    rows = sum(block.shape[0] for block in blocks) // count
    tile = min(columns, 512)
    whole = pl.BlockSpec(memory_space=pltpu.VMEM)
    return pl.pallas_call(
        functools.partial(
            project_kernel, len(blocks), list(range(share_count)) if direct else flips
        ),
        grid=(columns // tile,),
        in_specs=[pl.BlockSpec(memory_space=pltpu.SMEM)]
        + [whole for _ in blocks]
        + [pl.BlockSpec((depth, tile), lambda n: (0, n))],
        out_specs=[pl.BlockSpec((rows, tile), lambda n: (0, n))] * count,
        out_shape=[
            jax.ShapeDtypeStruct((rows, columns), jnp.bfloat16 if i else jnp.float32)
            for i in range(count)
        ],
        compiler_params=pltpu.CompilerParams(vmem_limit_bytes=10 * 1024 * 1024),
        cost_estimate=LIGHT,
    )(share, *blocks, out_weight)


def send_direct(pieces):
    axes = ("heads", "sub")
    return [pieces[0]] + [swap(pieces[flip], axes, flip) for flip in range(1, len(pieces))]


def add_direct(pieces):
    return sum(piece.astype(jnp.float32) for piece in pieces).astype(jnp.bfloat16)


def send_sub(pieces):
    keep, away = pieces
    return keep, swap(away, "sub", 1)


def send_heads(pieces, start=0, stop=None):
    keep, got = pieces
    heads_size = lax.axis_size("heads")
    rows = keep.shape[0] // heads_size
    stop = rows if stop is None else stop
    received = []
    for flip in range(1, heads_size):
        part = slice(flip * rows + start, flip * rows + stop)
        both = keep[part] + got[part].astype(jnp.float32)
        received.append(swap(both.astype(jnp.bfloat16), "heads", flip))
    return keep, got, received


def add_shares(pieces, start=0):
    keep, got, received = pieces
    part = slice(start, start + received[0].shape[0])
    total = keep[part] + got[part].astype(jnp.float32)
    return sum((piece.astype(jnp.float32) for piece in received), total).astype(jnp.bfloat16)


def fetch_kernel(
    place, holder, block, serving, store, where, *refs, pool_size, share_count
):
    pieces, (table, rank_of, sems) = refs[:pool_size], refs[pool_size:]
    pool_index, share = place[0], place[1]
    capacity = pieces[0].shape[0]
    blocks_each = holder.shape[1]
    requests_here = where.shape[1] // blocks_each
    spare = pool_size * capacity
    copies = []
    for flip in range(pool_size):
        for slot in range(capacity):
            table[flip * capacity + slot] = 0
        rank = 0
        for i in range(requests_here):
            request = serving[(pool_index ^ flip) * requests_here + i]
            for j in range(blocks_each):
                held = holder[request, j] == pool_index
                table[jnp.where(held, flip * capacity + rank, spare)] = block[request, j]
                rank = rank + held.astype(jnp.int32)
        for slot in range(capacity):
            index = flip * capacity + slot
            source = store.at[table[index] * share_count + share]
            copies.append(pltpu.make_async_copy(source, pieces[flip].at[slot], sems.at[index]))
            copies[-1].start()
    for i in range(pool_size):
        rank_of[i] = 0
    for i in range(requests_here):
        request = serving[pool_index * requests_here + i]
        for j in range(blocks_each):
            held_by = holder[request, j]
            where[0, i * blocks_each + j] = held_by ^ pool_index
            where[1, i * blocks_each + j] = rank_of[held_by]
            rank_of[held_by] = rank_of[held_by] + 1
    for copy in copies:
        copy.wait()


def fetch(place, latent_store, place_holder, place_block, serving_request, items):
    pool_size = lax.axis_size("pool")
    share_count = lax.axis_size(("heads", "sub"))
    capacity = 2 * ((items + pool_size - 1) // pool_size)
    rows = BLK // share_count
    store = latent_store.reshape(-1, rows, latent_store.shape[1])
    piece = jax.ShapeDtypeStruct((capacity, rows, store.shape[2]), store.dtype)
    smem = pl.BlockSpec(memory_space=pltpu.SMEM)
    where, *pieces = pl.pallas_call(
        functools.partial(fetch_kernel, pool_size=pool_size, share_count=share_count),
        in_specs=[smem] * 4 + [pl.BlockSpec(memory_space=pltpu.HBM)],
        out_specs=[smem] + [pl.BlockSpec(memory_space=pltpu.VMEM)] * pool_size,
        out_shape=[jax.ShapeDtypeStruct((2, items), jnp.int32)] + [piece] * pool_size,
        scratch_shapes=[
            pltpu.SMEM((pool_size * capacity + 1,), jnp.int32),
            pltpu.SMEM((pool_size,), jnp.int32),
            pltpu.SemaphoreType.DMA((pool_size * capacity,)),
        ],
        cost_estimate=LIGHT,
    )(place, place_holder, place_block, serving_request, store)
    return where, pieces


def choose_kernel(order, where, *refs):
    pieces, out = refs[:-1], refs[-1]
    for i in range(out.shape[0]):
        flip, slot = where[0, i], where[1, i]
        for other, piece in zip(order, pieces):

            @pl.when(flip == other)
            def _(piece=piece):
                out[i] = piece[slot]


def choose(where, pieces):
    order = [0, *range(2, len(pieces)), 1]
    whole = pl.BlockSpec(memory_space=pltpu.VMEM)
    return pl.pallas_call(
        functools.partial(choose_kernel, order),
        in_specs=[pl.BlockSpec(memory_space=pltpu.SMEM)] + [whole] * len(pieces),
        out_specs=whole,
        out_shape=jax.ShapeDtypeStruct((where.shape[1], *pieces[0].shape[1:]), pieces[0].dtype),
        compiler_params=pltpu.CompilerParams(vmem_limit_bytes=8 * 1024 * 1024),
        cost_estimate=LIGHT,
    )(where, *[pieces[flip] for flip in order])


def attend_kernel(start, rows, share_count, scalars, queries, *refs):
    parts, (kv_up, gains, out, keys, values) = refs[:share_count], refs[share_count:]
    q_gain, k_gain = gains[0:1, :], gains[1:2, :]
    requests, request_shares, _, width = queries.shape
    heads_here = kv_up.shape[0]
    head_width = gains.shape[1]
    text = request_shares * rows
    per_group = width // heads_here // head_width
    part_slots = parts[0].shape[1]
    share_rows = BLK // share_count
    share = scalars[0]
    slot = lax.broadcasted_iota(jnp.int32, (part_slots, head_width), 0)
    position = (slot // share_rows) * BLK + slot % share_rows
    scale = math.log2(math.e) / math.sqrt(head_width)
    together = min(per_group, max(1, 256 // text))
    for request in range(requests):
        count = scalars[1 + request]
        for flip in range(share_count):
            run = pl.ds(flip * part_slots, part_slots)
            live = jnp.where(position < count - (share ^ flip) * share_rows, 1.0, 0.0)
            for group in range(heads_here):
                pair = request * heads_here + group
                projected = jnp.dot(
                    parts[flip][request], kv_up[group], preferred_element_type=jnp.float32
                )
                key = rms_scale(projected[:, :head_width], k_gain)
                keys[pair, run, :] = key.astype(jnp.bfloat16)
                value = projected[:, head_width:] * live
                values[pair, run, :head_width] = value.astype(jnp.bfloat16)
                values[pair, run, head_width:] = live.astype(jnp.bfloat16)
        for group in range(heads_here):
            pair = request * heads_here + group
            for first in range(group * per_group, (group + 1) * per_group, together):
                normed = []
                for head in range(first, first + together):
                    columns = slice(head * head_width, (head + 1) * head_width)
                    query = queries[request, :, start : start + rows, columns]
                    query = query.reshape(text, head_width).astype(jnp.float32)
                    normed.append(rms_scale(query, q_gain).astype(jnp.bfloat16))
                scores = lax.dot_general(
                    jnp.concatenate(normed, axis=0),
                    keys[pair],
                    (((1,), (1,)), ((), ())),
                    preferred_element_type=jnp.float32,
                )
                expo = jnp.exp2(scores * scale).astype(jnp.bfloat16)
                total = jnp.dot(expo, values[pair], preferred_element_type=jnp.float32)
                result = (total[:, :head_width] / total[:, head_width:]).astype(jnp.bfloat16)
                for i in range(together):
                    head = first + i
                    columns = slice(head * head_width, (head + 1) * head_width)
                    out[request * text : (request + 1) * text, columns] = result[
                        i * text : (i + 1) * text
                    ]


def attend(start, rows, queries, parts, kv_flat, gains, scalars):
    requests, request_shares, _, width = queries.shape
    heads_here = kv_flat.shape[0]
    head_width = gains.shape[1]
    slots = len(parts) * parts[0].shape[1]
    whole = pl.BlockSpec(memory_space=pltpu.VMEM)
    return pl.pallas_call(
        functools.partial(attend_kernel, start, rows, len(parts)),
        in_specs=[pl.BlockSpec(memory_space=pltpu.SMEM)] + [whole] * (len(parts) + 3),
        out_specs=whole,
        out_shape=jax.ShapeDtypeStruct((requests * request_shares * rows, width), jnp.bfloat16),
        scratch_shapes=[
            pltpu.VMEM((requests * heads_here, slots, head_width), jnp.bfloat16),
            pltpu.VMEM((requests * heads_here, slots, 2 * head_width), jnp.bfloat16),
        ],
        compiler_params=pltpu.CompilerParams(vmem_limit_bytes=20 * 1024 * 1024),
        cost_estimate=LIGHT,
    )(scalars, queries, *parts, kv_flat, gains)


def per_device(
    queries,
    latent_store,
    kv_up,
    q_gain,
    k_gain,
    out_weight,
    place_holder,
    place_block,
    image_count,
    serving_request,
):
    pool_size = lax.axis_size("pool")
    pool_index = lax.axis_index("pool")
    heads_size = lax.axis_size("heads")
    sub_size = lax.axis_size("sub")
    share_count = heads_size * sub_size
    share = lax.axis_index(("heads", "sub"))
    requests_here, text_rows, _ = queries.shape
    blocks_each = place_holder.shape[1]
    items = requests_here * blocks_each
    rank_width = latent_store.shape[1]
    tie = lax.optimization_barrier
    place = jnp.stack([pool_index, share]).astype(jnp.int32)
    where, pieces = fetch(place, latent_store, place_holder, place_block, serving_request, items)
    kv_flat = jnp.moveaxis(kv_up.reshape(rank_width, kv_up.shape[1], -1), 1, 0)
    gains = jnp.stack([q_gain, k_gain])
    request_ids = jnp.arange(serving_request.shape[0], dtype=jnp.int32)
    served_here = lax.dynamic_slice_in_dim(
        serving_request, pool_index * requests_here, requests_here
    )
    count_here = jnp.sum(
        jnp.where(served_here[:, None] == request_ids[None, :], image_count[None, :], 0), axis=1
    )
    scalars = jnp.concatenate([share.reshape(1), count_here])
    for flip in [*range(2, pool_size), 1]:
        pieces[flip] = swap(pieces[flip], "pool", flip)
    capacity = pieces[0].shape[0]
    pieces[0] = jnp.roll(pieces[0], 1, axis=0)
    local = jnp.where(where[0] == 0, 1, 0)
    where = jnp.stack([where[0], (where[1] + local) % capacity])
    chosen = choose(where, pieces)
    chosen, kv_flat, gains, scalars = tie((chosen, kv_flat, gains, scalars))
    chosen = chosen.reshape(requests_here, -1, rank_width)
    over_heads = [chosen] + [swap(chosen, "heads", flip) for flip in range(1, heads_size)]
    parts = []
    for part in over_heads:
        parts += [part] + [swap(part, "sub", flip) for flip in range(1, sub_size)]
    part_rows = requests_here * text_rows // share_count
    shaped = queries.reshape(requests_here, share_count // requests_here, part_rows, -1)
    few = part_rows // 2
    chunk_rows = part_rows - few, few

    def attended(chunk):
        rows = chunk_rows[chunk]
        start = sum(chunk_rows[:chunk])
        return attend(start, rows, shaped, parts, kv_flat, gains, scalars)

    columns = out_weight.shape[1]
    if pool_size != 4:
        outputs = []
        for chunk in range(len(chunk_rows)):
            rows = lax.all_gather(attended(chunk), "pool", axis=0)
            mine = add_direct(
                send_direct(
                    project_out([rows[i] for i in range(pool_size)], out_weight, direct=True)
                )
            )
            mine = mine.reshape(pool_size, -1, columns)
            back = lax.all_to_all(mine, "pool", split_axis=0, concat_axis=0, tiled=True)
            outputs.append(jnp.moveaxis(back, 0, 1).reshape(-1, pool_size * columns))
        return jnp.concatenate(outputs, axis=0)

    first = attended(0)
    across0, beside0 = swap(first, "pool", 3), swap(first, "pool", 1)
    last = attended(1)
    across1, beside1 = swap(last, "pool", 3), swap(last, "pool", 1)
    own = project_out([first, last], out_weight)
    across0, beside0, own = tie((across0, beside0, own))
    second0 = second_hop(first, across0)
    near0 = send_direct(project_out([beside0, across0], out_weight, direct=True))
    across1, beside1, near0, own = tie((across1, beside1, near0, own))
    second1 = second_hop(last, across1)
    many, few = chunk_rows
    near0 = add_direct(near0)
    back0 = swap(near0[:many], "pool", 1), swap(near0[many:], "pool", 3)
    near1 = send_sub(project_out([beside1, across1], out_weight))
    second0, near1 = tie((second0, near1))
    near1 = send_heads(near1)
    far0 = send_heads(send_sub(project_out([second0], out_weight)))
    far1 = project_out([second1], out_weight)
    back0, near1, far0, far1, own = tie((back0, near1, far0, far1, own))
    near1 = add_shares(near1)
    back1 = swap(near1[:few], "pool", 1), swap(near1[few:], "pool", 3)
    back_second0 = swap(add_shares(far0), "pool", 2)
    far1 = send_heads(send_sub(far1))
    own = send_sub(own)
    own0, own1 = send_heads(own, 0, many), send_heads(own, many, many + few)
    back1, back_second0, far1, own0 = tie((back1, back_second0, far1, own0))
    back_second1 = swap(add_shares(far1), "pool", 2)
    own0, own1 = add_shares(own0), add_shares(own1, many)
    backs = [(0, 1, back0[0]), (0, 3, back0[1]), (many, 1, back1[0]), (many, 3, back1[1])]
    backs += [(0, 2, back_second0), (0, 0, own0), (many, 0, own1), (many, 2, back_second1)]
    output = jnp.zeros((part_rows, pool_size * columns), jnp.bfloat16)
    for row, flip, block in backs:
        output = lax.dynamic_update_slice(output, block, (row, (pool_index ^ flip) * columns))
    return output


def solution(mesh):
    in_specs = (
        P(("groups", "pool"), None, ("heads", "sub")),
        P(("groups", "pool"), None),
        P(None, ("heads", "sub"), None, None),
        P(),
        P(),
        P(("heads", "sub"), "pool"),
        P("groups", None),
        P("groups", None),
        P("groups"),
        P("groups"),
    )
    out_specs = P(("groups", "pool", "heads", "sub"), None)
    return jax.shard_map(
        per_device, mesh=mesh, in_specs=in_specs, out_specs=out_specs, check_vma=False
    )
```

```python
import functools
import math

import jax
import jax.numpy as jnp
from jax import lax
from jax.experimental import pallas as pl
from jax.experimental.pallas import tpu as pltpu
from jax.sharding import PartitionSpec as P

BLK = 128
LIGHT = pl.CostEstimate(flops=1, bytes_accessed=1, transcendentals=0)


def rms_scale(values, gain):
    return values * lax.rsqrt(jnp.mean(values * values, axis=-1, keepdims=True) + 1e-05) * gain


def swap(values, axis, flip):
    return lax.ppermute(values, axis, [(i, i ^ flip) for i in range(lax.axis_size(axis))])


def second_hop(block, across):
    index = lax.axis_index("pool")
    at_end = (index == 0) | (index == 3)
    passed = jnp.where(at_end, block, across)
    return lax.ppermute(passed, "pool", [(0, 2), (3, 1), (1, 0), (2, 3)])


def project_kernel(block_count, flips, share, *refs):
    blocks, weight, outs = refs[:block_count], refs[block_count], refs[block_count + 1 :]
    picked = []
    for flip in flips:
        for block in blocks:
            part_rows = block.shape[0] // len(flips)
            start = pl.multiple_of((share[0] ^ flip) * part_rows, part_rows)
            picked.append(block[pl.ds(start, part_rows), :])
    product = jnp.dot(
        jnp.concatenate(picked, axis=0), weight[...], preferred_element_type=jnp.float32
    )
    rows = product.shape[0] // len(outs)
    for i, out in enumerate(outs):
        out[...] = product[i * rows : (i + 1) * rows].astype(out.dtype)


def project_out(blocks, out_weight, direct=False, vmem=10):
    axes = ("heads", "sub")
    share_count = lax.axis_size(axes)
    share = lax.axis_index(axes).astype(jnp.int32).reshape(1)
    depth, columns = out_weight.shape
    flips = [*range(0, share_count, 2), *range(1, share_count, 2)]
    count = share_count if direct else 2
    rows = sum(block.shape[0] for block in blocks) // count
    tile = min(columns, 512)
    whole = pl.BlockSpec(memory_space=pltpu.VMEM)
    return pl.pallas_call(
        functools.partial(
            project_kernel, len(blocks), list(range(share_count)) if direct else flips
        ),
        grid=(columns // tile,),
        in_specs=[pl.BlockSpec(memory_space=pltpu.SMEM)]
        + [whole for _ in blocks]
        + [pl.BlockSpec((depth, tile), lambda n: (0, n))],
        out_specs=[pl.BlockSpec((rows, tile), lambda n: (0, n))] * count,
        out_shape=[
            jax.ShapeDtypeStruct((rows, columns), jnp.bfloat16 if i else jnp.float32)
            for i in range(count)
        ],
        compiler_params=pltpu.CompilerParams(vmem_limit_bytes=vmem * 1024 * 1024),
        cost_estimate=LIGHT,
    )(share, *blocks, out_weight)


def send_direct(pieces):
    axes = ("heads", "sub")
    return [pieces[0]] + [swap(pieces[flip], axes, flip) for flip in range(1, len(pieces))]


def add_direct(pieces):
    return sum(piece.astype(jnp.float32) for piece in pieces).astype(jnp.bfloat16)


def send_sub(pieces):
    keep, away = pieces
    return keep, swap(away, "sub", 1)


def send_heads(pieces, start=0, stop=None):
    keep, got = pieces
    heads_size = lax.axis_size("heads")
    rows = keep.shape[0] // heads_size
    stop = rows if stop is None else stop
    received = []
    for flip in range(1, heads_size):
        part = slice(flip * rows + start, flip * rows + stop)
        both = keep[part] + got[part].astype(jnp.float32)
        received.append(swap(both.astype(jnp.bfloat16), "heads", flip))
    return keep, got, received


def add_shares(pieces, start=0):
    keep, got, received = pieces
    part = slice(start, start + received[0].shape[0])
    total = keep[part] + got[part].astype(jnp.float32)
    return sum((piece.astype(jnp.float32) for piece in received), total).astype(jnp.bfloat16)


def fetch_kernel(
    place, holder, block, serving, store, where, *refs, pool_size, share_count
):
    pieces, (table, rank_of, sems) = refs[:pool_size], refs[pool_size:]
    pool_index, share = place[0], place[1]
    capacity = pieces[0].shape[0]
    blocks_each = holder.shape[1]
    requests_here = where.shape[1] // blocks_each
    spare = pool_size * capacity
    copies = []
    for flip in range(pool_size):
        for slot in range(capacity):
            table[flip * capacity + slot] = 0
        rank = 0
        for i in range(requests_here):
            request = serving[(pool_index ^ flip) * requests_here + i]
            for j in range(blocks_each):
                held = holder[request, j] == pool_index
                table[jnp.where(held, flip * capacity + rank, spare)] = block[request, j]
                rank = rank + held.astype(jnp.int32)
        for slot in range(capacity):
            index = flip * capacity + slot
            source = store.at[table[index] * share_count + share]
            copies.append(pltpu.make_async_copy(source, pieces[flip].at[slot], sems.at[index]))
            copies[-1].start()
    for i in range(pool_size):
        rank_of[i] = 0
    for i in range(requests_here):
        request = serving[pool_index * requests_here + i]
        for j in range(blocks_each):
            held_by = holder[request, j]
            where[0, i * blocks_each + j] = held_by ^ pool_index
            where[1, i * blocks_each + j] = rank_of[held_by]
            rank_of[held_by] = rank_of[held_by] + 1
    for copy in copies:
        copy.wait()


def fetch(place, latent_store, place_holder, place_block, serving_request, items):
    pool_size = lax.axis_size("pool")
    share_count = lax.axis_size(("heads", "sub"))
    capacity = 2 * ((items + pool_size - 1) // pool_size)
    rows = BLK // share_count
    store = latent_store.reshape(-1, rows, latent_store.shape[1])
    piece = jax.ShapeDtypeStruct((capacity, rows, store.shape[2]), store.dtype)
    smem = pl.BlockSpec(memory_space=pltpu.SMEM)
    where, *pieces = pl.pallas_call(
        functools.partial(fetch_kernel, pool_size=pool_size, share_count=share_count),
        in_specs=[smem] * 4 + [pl.BlockSpec(memory_space=pltpu.HBM)],
        out_specs=[smem] + [pl.BlockSpec(memory_space=pltpu.VMEM)] * pool_size,
        out_shape=[jax.ShapeDtypeStruct((2, items), jnp.int32)] + [piece] * pool_size,
        scratch_shapes=[
            pltpu.SMEM((pool_size * capacity + 1,), jnp.int32),
            pltpu.SMEM((pool_size,), jnp.int32),
            pltpu.SemaphoreType.DMA((pool_size * capacity,)),
        ],
        cost_estimate=LIGHT,
    )(place, place_holder, place_block, serving_request, store)
    return where, pieces


def choose_kernel(order, where, *refs):
    pieces, out = refs[:-1], refs[-1]
    for i in range(out.shape[0]):
        flip, slot = where[0, i], where[1, i]
        for other, piece in zip(order, pieces):

            @pl.when(flip == other)
            def _(piece=piece):
                out[i] = piece[slot]


def choose(where, pieces):
    order = [0, *range(2, len(pieces)), 1]
    whole = pl.BlockSpec(memory_space=pltpu.VMEM)
    return pl.pallas_call(
        functools.partial(choose_kernel, order),
        in_specs=[pl.BlockSpec(memory_space=pltpu.SMEM)] + [whole] * len(pieces),
        out_specs=whole,
        out_shape=jax.ShapeDtypeStruct((where.shape[1], *pieces[0].shape[1:]), pieces[0].dtype),
        compiler_params=pltpu.CompilerParams(vmem_limit_bytes=8 * 1024 * 1024),
        cost_estimate=LIGHT,
    )(where, *[pieces[flip] for flip in order])


def attend_kernel(start, rows, share_count, scalars, queries, *refs):
    parts, (kv_up, gains, out, keys, values) = refs[:share_count], refs[share_count:]
    q_gain, k_gain = gains[0:1, :], gains[1:2, :]
    requests, request_shares, _, width = queries.shape
    heads_here = kv_up.shape[0]
    head_width = gains.shape[1]
    text = request_shares * rows
    per_group = width // heads_here // head_width
    part_slots = parts[0].shape[1]
    share_rows = BLK // share_count
    share = scalars[0]
    slot = lax.broadcasted_iota(jnp.int32, (part_slots, head_width), 0)
    position = (slot // share_rows) * BLK + slot % share_rows
    scale = math.log2(math.e) / math.sqrt(head_width)
    together = min(per_group, max(1, 256 // text))
    for request in range(requests):
        count = scalars[1 + request]
        for flip in range(share_count):
            run = pl.ds(flip * part_slots, part_slots)
            live = jnp.where(position < count - (share ^ flip) * share_rows, 1.0, 0.0)
            for group in range(heads_here):
                pair = request * heads_here + group
                projected = jnp.dot(
                    parts[flip][request], kv_up[group], preferred_element_type=jnp.float32
                )
                key = rms_scale(projected[:, :head_width], k_gain)
                keys[pair, run, :] = key.astype(jnp.bfloat16)
                value = projected[:, head_width:] * live
                values[pair, run, :head_width] = value.astype(jnp.bfloat16)
                values[pair, run, head_width:] = live.astype(jnp.bfloat16)
        for group in range(heads_here):
            pair = request * heads_here + group
            for first in range(group * per_group, (group + 1) * per_group, together):
                normed = []
                for head in range(first, first + together):
                    columns = slice(head * head_width, (head + 1) * head_width)
                    query = queries[request, :, start : start + rows, columns]
                    query = query.reshape(text, head_width).astype(jnp.float32)
                    normed.append(rms_scale(query, q_gain).astype(jnp.bfloat16))
                scores = lax.dot_general(
                    jnp.concatenate(normed, axis=0),
                    keys[pair],
                    (((1,), (1,)), ((), ())),
                    preferred_element_type=jnp.float32,
                )
                expo = jnp.exp2(scores * scale).astype(jnp.bfloat16)
                total = jnp.dot(expo, values[pair], preferred_element_type=jnp.float32)
                result = (total[:, :head_width] / total[:, head_width:]).astype(jnp.bfloat16)
                for i in range(together):
                    head = first + i
                    columns = slice(head * head_width, (head + 1) * head_width)
                    out[request * text : (request + 1) * text, columns] = result[
                        i * text : (i + 1) * text
                    ]


def attend(start, rows, queries, parts, kv_flat, gains, scalars):
    requests, request_shares, _, width = queries.shape
    heads_here = kv_flat.shape[0]
    head_width = gains.shape[1]
    slots = len(parts) * parts[0].shape[1]
    whole = pl.BlockSpec(memory_space=pltpu.VMEM)
    return pl.pallas_call(
        functools.partial(attend_kernel, start, rows, len(parts)),
        in_specs=[pl.BlockSpec(memory_space=pltpu.SMEM)] + [whole] * (len(parts) + 3),
        out_specs=whole,
        out_shape=jax.ShapeDtypeStruct((requests * request_shares * rows, width), jnp.bfloat16),
        scratch_shapes=[
            pltpu.VMEM((requests * heads_here, slots, head_width), jnp.bfloat16),
            pltpu.VMEM((requests * heads_here, slots, 2 * head_width), jnp.bfloat16),
        ],
        compiler_params=pltpu.CompilerParams(vmem_limit_bytes=20 * 1024 * 1024),
        cost_estimate=LIGHT,
    )(scalars, queries, *parts, kv_flat, gains)


def per_device(
    queries,
    latent_store,
    kv_up,
    q_gain,
    k_gain,
    out_weight,
    place_holder,
    place_block,
    image_count,
    serving_request,
):
    pool_size = lax.axis_size("pool")
    pool_index = lax.axis_index("pool")
    heads_size = lax.axis_size("heads")
    sub_size = lax.axis_size("sub")
    share_count = heads_size * sub_size
    share = lax.axis_index(("heads", "sub"))
    requests_here, text_rows, _ = queries.shape
    blocks_each = place_holder.shape[1]
    items = requests_here * blocks_each
    rank_width = latent_store.shape[1]
    tie = lax.optimization_barrier
    place = jnp.stack([pool_index, share]).astype(jnp.int32)
    where, pieces = fetch(place, latent_store, place_holder, place_block, serving_request, items)
    kv_flat = jnp.moveaxis(kv_up.reshape(rank_width, kv_up.shape[1], -1), 1, 0)
    gains = jnp.stack([q_gain, k_gain])
    request_ids = jnp.arange(serving_request.shape[0], dtype=jnp.int32)
    served_here = lax.dynamic_slice_in_dim(
        serving_request, pool_index * requests_here, requests_here
    )
    count_here = jnp.sum(
        jnp.where(served_here[:, None] == request_ids[None, :], image_count[None, :], 0), axis=1
    )
    scalars = jnp.concatenate([share.reshape(1), count_here])
    for flip in [*range(2, pool_size), 1]:
        pieces[flip] = swap(pieces[flip], "pool", flip)
    capacity = pieces[0].shape[0]
    pieces[0] = jnp.roll(pieces[0], 1, axis=0)
    local = jnp.where(where[0] == 0, 1, 0)
    where = jnp.stack([where[0], (where[1] + local) % capacity])
    chosen = choose(where, pieces)
    chosen, kv_flat, gains, scalars = tie((chosen, kv_flat, gains, scalars))
    chosen = chosen.reshape(requests_here, -1, rank_width)
    over_heads = [chosen] + [swap(chosen, "heads", flip) for flip in range(1, heads_size)]
    parts = []
    for part in over_heads:
        parts += [part] + [swap(part, "sub", flip) for flip in range(1, sub_size)]
    part_rows = requests_here * text_rows // share_count
    shaped = queries.reshape(requests_here, share_count // requests_here, part_rows, -1)
    few = part_rows // 2
    chunk_rows = part_rows - few, few

    def attended(chunk):
        rows = chunk_rows[chunk]
        start = sum(chunk_rows[:chunk])
        return attend(start, rows, shaped, parts, kv_flat, gains, scalars)

    columns = out_weight.shape[1]
    if pool_size != 4:
        outputs = []
        for chunk in range(len(chunk_rows)):
            rows = lax.all_gather(attended(chunk), "pool", axis=0)
            mine = add_direct(
                send_direct(
                    project_out([rows[i] for i in range(pool_size)], out_weight, direct=True)
                )
            )
            mine = mine.reshape(pool_size, -1, columns)
            back = lax.all_to_all(mine, "pool", split_axis=0, concat_axis=0, tiled=True)
            outputs.append(jnp.moveaxis(back, 0, 1).reshape(-1, pool_size * columns))
        return jnp.concatenate(outputs, axis=0)

    first = attended(0)
    across0, beside0 = swap(first, "pool", 3), swap(first, "pool", 1)
    last = attended(1)
    across1, beside1 = swap(last, "pool", 3), swap(last, "pool", 1)
    own = project_out([first, last], out_weight)
    across0, beside0, own = tie((across0, beside0, own))
    second0 = second_hop(first, across0)
    near0 = send_direct(project_out([beside0, across0], out_weight, direct=True))
    across1, beside1, near0, own = tie((across1, beside1, near0, own))
    second1 = second_hop(last, across1)
    many, few = chunk_rows
    near0 = add_direct(near0)
    back0 = swap(near0[:many], "pool", 1), swap(near0[many:], "pool", 3)
    near1 = send_sub(project_out([beside1, across1], out_weight))
    second0, near1 = tie((second0, near1))
    near1 = send_heads(near1)
    far0 = send_heads(send_sub(project_out([second0], out_weight)))
    far1 = project_out([second1], out_weight, vmem=54)
    back0, near1, far0, far1, own = tie((back0, near1, far0, far1, own))
    near1 = add_shares(near1)
    back1 = swap(near1[:few], "pool", 1), swap(near1[few:], "pool", 3)
    back_second0 = swap(add_shares(far0), "pool", 2)
    far1 = send_heads(send_sub(far1))
    own = send_sub(own)
    own0, own1 = send_heads(own, 0, many), send_heads(own, many, many + few)
    back1, back_second0, far1, own0 = tie((back1, back_second0, far1, own0))
    back_second1 = swap(add_shares(far1), "pool", 2)
    own0, own1 = add_shares(own0), add_shares(own1, many)
    backs = [(0, 1, back0[0]), (0, 3, back0[1]), (many, 1, back1[0]), (many, 3, back1[1])]
    backs += [(0, 2, back_second0), (0, 0, own0), (many, 0, own1), (many, 2, back_second1)]
    output = jnp.zeros((part_rows, pool_size * columns), jnp.bfloat16)
    for row, flip, block in backs:
        output = lax.dynamic_update_slice(output, block, (row, (pool_index ^ flip) * columns))
    return output


def solution(mesh):
    in_specs = (
        P(("groups", "pool"), None, ("heads", "sub")),
        P(("groups", "pool"), None),
        P(None, ("heads", "sub"), None, None),
        P(),
        P(),
        P(("heads", "sub"), "pool"),
        P("groups", None),
        P("groups", None),
        P("groups"),
        P("groups"),
    )
    out_specs = P(("groups", "pool", "heads", "sub"), None)
    return jax.shard_map(
        per_device, mesh=mesh, in_specs=in_specs, out_specs=out_specs, check_vma=False
    )
```

```python
import functools
import math

import jax
import jax.numpy as jnp
from jax import lax
from jax.experimental import pallas as pl
from jax.experimental.pallas import tpu as pltpu
from jax.sharding import PartitionSpec as P

BLK = 128
LIGHT = pl.CostEstimate(flops=1, bytes_accessed=1, transcendentals=0)


def rms_scale(values, gain):
    return values * lax.rsqrt(jnp.mean(values * values, axis=-1, keepdims=True) + 1e-05) * gain


def swap(values, axis, flip):
    return lax.ppermute(values, axis, [(i, i ^ flip) for i in range(lax.axis_size(axis))])


def second_hop(block, across):
    index = lax.axis_index("pool")
    at_end = (index == 0) | (index == 3)
    passed = jnp.where(at_end, block, across)
    return lax.ppermute(passed, "pool", [(0, 2), (3, 1), (1, 0), (2, 3)])


def project_kernel(block_count, flips, share, *refs):
    blocks, weight = refs[:block_count], refs[block_count]
    outs, rows = refs[block_count + 1 : -1], refs[-1]
    done = 0
    for flip in flips:
        for block in blocks:
            part_rows = block.shape[0] // len(flips)
            start = pl.multiple_of((share[0] ^ flip) * part_rows, part_rows)
            rows[done : done + part_rows, :] = block[pl.ds(start, part_rows), :]
            done += part_rows
    columns = weight.shape[1]
    tile = min(columns, 512)
    each = rows.shape[0] // len(outs)
    for n in range(0, columns, tile):
        product = jnp.dot(
            rows[...], weight[:, n : n + tile], preferred_element_type=jnp.float32
        )
        for i, out in enumerate(outs):
            out[:, n : n + tile] = product[i * each : (i + 1) * each].astype(out.dtype)


def project_out(blocks, out_weight, direct=False):
    axes = ("heads", "sub")
    share_count = lax.axis_size(axes)
    share = lax.axis_index(axes).astype(jnp.int32).reshape(1)
    depth, columns = out_weight.shape
    flips = [*range(0, share_count, 2), *range(1, share_count, 2)]
    count = share_count if direct else 2
    rows = sum(block.shape[0] for block in blocks) // count
    whole = pl.BlockSpec(memory_space=pltpu.VMEM)
    return pl.pallas_call(
        functools.partial(
            project_kernel, len(blocks), list(range(share_count)) if direct else flips
        ),
        in_specs=[pl.BlockSpec(memory_space=pltpu.SMEM)] + [whole] * (len(blocks) + 1),
        out_specs=[whole] * count,
        out_shape=[
            jax.ShapeDtypeStruct((rows, columns), jnp.bfloat16 if i else jnp.float32)
            for i in range(count)
        ],
        scratch_shapes=[pltpu.VMEM((rows * count, depth), jnp.bfloat16)],
        compiler_params=pltpu.CompilerParams(vmem_limit_bytes=24 * 1024 * 1024),
        cost_estimate=LIGHT,
    )(share, *blocks, out_weight)


def send_direct(pieces):
    axes = ("heads", "sub")
    return [pieces[0]] + [swap(pieces[flip], axes, flip) for flip in range(1, len(pieces))]


def add_direct(pieces):
    return sum(piece.astype(jnp.float32) for piece in pieces).astype(jnp.bfloat16)


def send_sub(pieces):
    keep, away = pieces
    return keep, swap(away, "sub", 1)


def send_heads(pieces, start=0, stop=None):
    keep, got = pieces
    heads_size = lax.axis_size("heads")
    rows = keep.shape[0] // heads_size
    stop = rows if stop is None else stop
    received = []
    for flip in range(1, heads_size):
        part = slice(flip * rows + start, flip * rows + stop)
        both = keep[part] + got[part].astype(jnp.float32)
        received.append(swap(both.astype(jnp.bfloat16), "heads", flip))
    return keep, got, received


def add_shares(pieces, start=0):
    keep, got, received = pieces
    part = slice(start, start + received[0].shape[0])
    total = keep[part] + got[part].astype(jnp.float32)
    return sum((piece.astype(jnp.float32) for piece in received), total).astype(jnp.bfloat16)


def fetch_kernel(
    place, holder, block, serving, store, where, *refs, pool_size, share_count
):
    pieces, (table, rank_of, sems) = refs[:pool_size], refs[pool_size:]
    pool_index, share = place[0], place[1]
    capacity = pieces[0].shape[0]
    blocks_each = holder.shape[1]
    requests_here = where.shape[1] // blocks_each
    spare = pool_size * capacity
    copies = []
    for flip in range(pool_size):
        for slot in range(capacity):
            table[flip * capacity + slot] = 0
        rank = 0
        for i in range(requests_here):
            request = serving[(pool_index ^ flip) * requests_here + i]
            for j in range(blocks_each):
                held = holder[request, j] == pool_index
                table[jnp.where(held, flip * capacity + rank, spare)] = block[request, j]
                rank = rank + held.astype(jnp.int32)
        for slot in range(capacity):
            index = flip * capacity + slot
            source = store.at[table[index] * share_count + share]
            copies.append(pltpu.make_async_copy(source, pieces[flip].at[slot], sems.at[index]))
            copies[-1].start()
    for i in range(pool_size):
        rank_of[i] = 0
    for i in range(requests_here):
        request = serving[pool_index * requests_here + i]
        for j in range(blocks_each):
            held_by = holder[request, j]
            where[0, i * blocks_each + j] = held_by ^ pool_index
            where[1, i * blocks_each + j] = rank_of[held_by]
            rank_of[held_by] = rank_of[held_by] + 1
    for copy in copies:
        copy.wait()


def fetch(place, latent_store, place_holder, place_block, serving_request, items):
    pool_size = lax.axis_size("pool")
    share_count = lax.axis_size(("heads", "sub"))
    capacity = 2 * ((items + pool_size - 1) // pool_size)
    rows = BLK // share_count
    store = latent_store.reshape(-1, rows, latent_store.shape[1])
    piece = jax.ShapeDtypeStruct((capacity, rows, store.shape[2]), store.dtype)
    smem = pl.BlockSpec(memory_space=pltpu.SMEM)
    where, *pieces = pl.pallas_call(
        functools.partial(fetch_kernel, pool_size=pool_size, share_count=share_count),
        in_specs=[smem] * 4 + [pl.BlockSpec(memory_space=pltpu.HBM)],
        out_specs=[smem] + [pl.BlockSpec(memory_space=pltpu.VMEM)] * pool_size,
        out_shape=[jax.ShapeDtypeStruct((2, items), jnp.int32)] + [piece] * pool_size,
        scratch_shapes=[
            pltpu.SMEM((pool_size * capacity + 1,), jnp.int32),
            pltpu.SMEM((pool_size,), jnp.int32),
            pltpu.SemaphoreType.DMA((pool_size * capacity,)),
        ],
        cost_estimate=LIGHT,
    )(place, place_holder, place_block, serving_request, store)
    return where, pieces


def choose_kernel(order, where, *refs):
    pieces, out = refs[:-1], refs[-1]
    for i in range(out.shape[0]):
        flip, slot = where[0, i], where[1, i]
        for other, piece in zip(order, pieces):

            @pl.when(flip == other)
            def _(piece=piece):
                out[i] = piece[slot]


def choose(where, pieces):
    order = [0, *range(2, len(pieces)), 1]
    whole = pl.BlockSpec(memory_space=pltpu.VMEM)
    return pl.pallas_call(
        functools.partial(choose_kernel, order),
        in_specs=[pl.BlockSpec(memory_space=pltpu.SMEM)] + [whole] * len(pieces),
        out_specs=whole,
        out_shape=jax.ShapeDtypeStruct((where.shape[1], *pieces[0].shape[1:]), pieces[0].dtype),
        compiler_params=pltpu.CompilerParams(vmem_limit_bytes=8 * 1024 * 1024),
        cost_estimate=LIGHT,
    )(where, *[pieces[flip] for flip in order])


def attend_kernel(start, rows, share_count, scalars, queries, *refs):
    parts, (kv_up, gains, out, keys, values) = refs[:share_count], refs[share_count:]
    q_gain, k_gain = gains[0:1, :], gains[1:2, :]
    requests, request_shares, _, width = queries.shape
    heads_here = kv_up.shape[0]
    head_width = gains.shape[1]
    text = request_shares * rows
    per_group = width // heads_here // head_width
    part_slots = parts[0].shape[1]
    share_rows = BLK // share_count
    share = scalars[0]
    slot = lax.broadcasted_iota(jnp.int32, (part_slots, head_width), 0)
    position = (slot // share_rows) * BLK + slot % share_rows
    scale = math.log2(math.e) / math.sqrt(head_width)
    together = min(per_group, max(1, 256 // text))
    for request in range(requests):
        count = scalars[1 + request]
        for flip in range(share_count):
            run = pl.ds(flip * part_slots, part_slots)
            live = jnp.where(position < count - (share ^ flip) * share_rows, 1.0, 0.0)
            for group in range(heads_here):
                pair = request * heads_here + group
                projected = jnp.dot(
                    parts[flip][request], kv_up[group], preferred_element_type=jnp.float32
                )
                key = rms_scale(projected[:, :head_width], k_gain)
                keys[pair, run, :] = key.astype(jnp.bfloat16)
                value = projected[:, head_width:] * live
                values[pair, run, :head_width] = value.astype(jnp.bfloat16)
                values[pair, run, head_width:] = live.astype(jnp.bfloat16)
        for group in range(heads_here):
            pair = request * heads_here + group
            for first in range(group * per_group, (group + 1) * per_group, together):
                normed = []
                for head in range(first, first + together):
                    columns = slice(head * head_width, (head + 1) * head_width)
                    query = queries[request, :, start : start + rows, columns]
                    query = query.reshape(text, head_width).astype(jnp.float32)
                    normed.append(rms_scale(query, q_gain).astype(jnp.bfloat16))
                scores = lax.dot_general(
                    jnp.concatenate(normed, axis=0),
                    keys[pair],
                    (((1,), (1,)), ((), ())),
                    preferred_element_type=jnp.float32,
                )
                expo = jnp.exp2(scores * scale).astype(jnp.bfloat16)
                total = jnp.dot(expo, values[pair], preferred_element_type=jnp.float32)
                result = (total[:, :head_width] / total[:, head_width:]).astype(jnp.bfloat16)
                for i in range(together):
                    head = first + i
                    columns = slice(head * head_width, (head + 1) * head_width)
                    out[request * text : (request + 1) * text, columns] = result[
                        i * text : (i + 1) * text
                    ]


def attend(start, rows, queries, parts, kv_flat, gains, scalars):
    requests, request_shares, _, width = queries.shape
    heads_here = kv_flat.shape[0]
    head_width = gains.shape[1]
    slots = len(parts) * parts[0].shape[1]
    whole = pl.BlockSpec(memory_space=pltpu.VMEM)
    return pl.pallas_call(
        functools.partial(attend_kernel, start, rows, len(parts)),
        in_specs=[pl.BlockSpec(memory_space=pltpu.SMEM)] + [whole] * (len(parts) + 3),
        out_specs=whole,
        out_shape=jax.ShapeDtypeStruct((requests * request_shares * rows, width), jnp.bfloat16),
        scratch_shapes=[
            pltpu.VMEM((requests * heads_here, slots, head_width), jnp.bfloat16),
            pltpu.VMEM((requests * heads_here, slots, 2 * head_width), jnp.bfloat16),
        ],
        compiler_params=pltpu.CompilerParams(vmem_limit_bytes=20 * 1024 * 1024),
        cost_estimate=LIGHT,
    )(scalars, queries, *parts, kv_flat, gains)


def per_device(
    queries,
    latent_store,
    kv_up,
    q_gain,
    k_gain,
    out_weight,
    place_holder,
    place_block,
    image_count,
    serving_request,
):
    pool_size = lax.axis_size("pool")
    pool_index = lax.axis_index("pool")
    heads_size = lax.axis_size("heads")
    sub_size = lax.axis_size("sub")
    share_count = heads_size * sub_size
    share = lax.axis_index(("heads", "sub"))
    requests_here, text_rows, _ = queries.shape
    blocks_each = place_holder.shape[1]
    items = requests_here * blocks_each
    rank_width = latent_store.shape[1]
    tie = lax.optimization_barrier
    place = jnp.stack([pool_index, share]).astype(jnp.int32)
    where, pieces = fetch(place, latent_store, place_holder, place_block, serving_request, items)
    kv_flat = jnp.moveaxis(kv_up.reshape(rank_width, kv_up.shape[1], -1), 1, 0)
    gains = jnp.stack([q_gain, k_gain])
    request_ids = jnp.arange(serving_request.shape[0], dtype=jnp.int32)
    served_here = lax.dynamic_slice_in_dim(
        serving_request, pool_index * requests_here, requests_here
    )
    count_here = jnp.sum(
        jnp.where(served_here[:, None] == request_ids[None, :], image_count[None, :], 0), axis=1
    )
    scalars = jnp.concatenate([share.reshape(1), count_here])
    for flip in [*range(2, pool_size), 1]:
        pieces[flip] = swap(pieces[flip], "pool", flip)
    capacity = pieces[0].shape[0]
    pieces[0] = jnp.roll(pieces[0], 1, axis=0)
    local = jnp.where(where[0] == 0, 1, 0)
    where = jnp.stack([where[0], (where[1] + local) % capacity])
    chosen = choose(where, pieces)
    chosen, kv_flat, gains, scalars = tie((chosen, kv_flat, gains, scalars))
    chosen = chosen.reshape(requests_here, -1, rank_width)
    over_heads = [chosen] + [swap(chosen, "heads", flip) for flip in range(1, heads_size)]
    parts = []
    for part in over_heads:
        parts += [part] + [swap(part, "sub", flip) for flip in range(1, sub_size)]
    part_rows = requests_here * text_rows // share_count
    shaped = queries.reshape(requests_here, share_count // requests_here, part_rows, -1)
    few = part_rows // 2
    chunk_rows = part_rows - few, few

    def attended(chunk):
        rows = chunk_rows[chunk]
        start = sum(chunk_rows[:chunk])
        return attend(start, rows, shaped, parts, kv_flat, gains, scalars)

    columns = out_weight.shape[1]
    if pool_size != 4:
        outputs = []
        for chunk in range(len(chunk_rows)):
            rows = lax.all_gather(attended(chunk), "pool", axis=0)
            mine = add_direct(
                send_direct(
                    project_out([rows[i] for i in range(pool_size)], out_weight, direct=True)
                )
            )
            mine = mine.reshape(pool_size, -1, columns)
            back = lax.all_to_all(mine, "pool", split_axis=0, concat_axis=0, tiled=True)
            outputs.append(jnp.moveaxis(back, 0, 1).reshape(-1, pool_size * columns))
        return jnp.concatenate(outputs, axis=0)

    first = attended(0)
    across0, beside0 = swap(first, "pool", 3), swap(first, "pool", 1)
    last = attended(1)
    across1, beside1 = swap(last, "pool", 3), swap(last, "pool", 1)
    own = project_out([first, last], out_weight)
    across0, beside0, own = tie((across0, beside0, own))
    second0 = second_hop(first, across0)
    near0 = send_direct(project_out([beside0, across0], out_weight, direct=True))
    across1, beside1, near0, own = tie((across1, beside1, near0, own))
    second1 = second_hop(last, across1)
    many, few = chunk_rows
    near0 = add_direct(near0)
    back0 = swap(near0[:many], "pool", 1), swap(near0[many:], "pool", 3)
    near1 = send_sub(project_out([beside1, across1], out_weight))
    second0, near1 = tie((second0, near1))
    near1 = send_heads(near1)
    far0 = send_heads(send_sub(project_out([second0], out_weight)))
    far1 = project_out([second1], out_weight)
    back0, near1, far0, far1, own = tie((back0, near1, far0, far1, own))
    near1 = add_shares(near1)
    back1 = swap(near1[:few], "pool", 1), swap(near1[few:], "pool", 3)
    back_second0 = swap(add_shares(far0), "pool", 2)
    far1 = send_heads(send_sub(far1))
    own = send_sub(own)
    own0, own1 = send_heads(own, 0, many), send_heads(own, many, many + few)
    back1, back_second0, far1, own0 = tie((back1, back_second0, far1, own0))
    back_second1 = swap(add_shares(far1), "pool", 2)
    own0, own1 = add_shares(own0), add_shares(own1, many)
    backs = [(0, 1, back0[0]), (0, 3, back0[1]), (many, 1, back1[0]), (many, 3, back1[1])]
    backs += [(0, 2, back_second0), (0, 0, own0), (many, 0, own1), (many, 2, back_second1)]
    output = jnp.zeros((part_rows, pool_size * columns), jnp.bfloat16)
    for row, flip, block in backs:
        output = lax.dynamic_update_slice(output, block, (row, (pool_index ^ flip) * columns))
    return output


def solution(mesh):
    in_specs = (
        P(("groups", "pool"), None, ("heads", "sub")),
        P(("groups", "pool"), None),
        P(None, ("heads", "sub"), None, None),
        P(),
        P(),
        P(("heads", "sub"), "pool"),
        P("groups", None),
        P("groups", None),
        P("groups"),
        P("groups"),
    )
    out_specs = P(("groups", "pool", "heads", "sub"), None)
    return jax.shard_map(
        per_device, mesh=mesh, in_specs=in_specs, out_specs=out_specs, check_vma=False
    )
```

```python
import functools
import math

import jax
import jax.numpy as jnp
from jax import lax
from jax.experimental import pallas as pl
from jax.experimental.pallas import tpu as pltpu
from jax.sharding import PartitionSpec as P

BLK = 128
LIGHT = pl.CostEstimate(flops=1, bytes_accessed=1, transcendentals=0)


def rms_scale(values, gain):
    return values * lax.rsqrt(jnp.mean(values * values, axis=-1, keepdims=True) + 1e-05) * gain


def swap(values, axis, flip):
    return lax.ppermute(values, axis, [(i, i ^ flip) for i in range(lax.axis_size(axis))])


def second_hop(block, across):
    index = lax.axis_index("pool")
    at_end = (index == 0) | (index == 3)
    passed = jnp.where(at_end, block, across)
    return lax.ppermute(passed, "pool", [(0, 2), (3, 1), (1, 0), (2, 3)])


def project_kernel(block_count, flips, share, *refs):
    blocks, weight = refs[:block_count], refs[block_count]
    outs, rows = refs[block_count + 1 : -1], refs[-1]
    done = 0
    for flip in flips:
        for block in blocks:
            part_rows = block.shape[0] // len(flips)
            start = pl.multiple_of((share[0] ^ flip) * part_rows, part_rows)
            rows[done : done + part_rows, :] = block[pl.ds(start, part_rows), :]
            done += part_rows
    columns = weight.shape[1]
    tile = min(columns, 512)
    each = rows.shape[0] // len(outs)
    for n in range(0, columns, tile):
        product = jnp.dot(
            rows[...], weight[:, n : n + tile], preferred_element_type=jnp.float32
        )
        for i, out in enumerate(outs):
            out[:, n : n + tile] = product[i * each : (i + 1) * each].astype(out.dtype)


def project_out(blocks, out_weight, direct=False):
    axes = ("heads", "sub")
    share_count = lax.axis_size(axes)
    share = lax.axis_index(axes).astype(jnp.int32).reshape(1)
    depth, columns = out_weight.shape
    flips = [*range(0, share_count, 2), *range(1, share_count, 2)]
    count = share_count if direct else 2
    rows = sum(block.shape[0] for block in blocks) // count
    whole = pl.BlockSpec(memory_space=pltpu.VMEM)
    return pl.pallas_call(
        functools.partial(
            project_kernel, len(blocks), list(range(share_count)) if direct else flips
        ),
        in_specs=[pl.BlockSpec(memory_space=pltpu.SMEM)] + [whole] * (len(blocks) + 1),
        out_specs=[whole] * count,
        out_shape=[
            jax.ShapeDtypeStruct((rows, columns), jnp.bfloat16 if i else jnp.float32)
            for i in range(count)
        ],
        scratch_shapes=[pltpu.VMEM((rows * count, depth), jnp.bfloat16)],
        compiler_params=pltpu.CompilerParams(vmem_limit_bytes=24 * 1024 * 1024),
        cost_estimate=LIGHT,
    )(share, *blocks, out_weight)


def send_direct(pieces):
    axes = ("heads", "sub")
    return [pieces[0]] + [swap(pieces[flip], axes, flip) for flip in range(1, len(pieces))]


def add_direct(pieces):
    return sum(piece.astype(jnp.float32) for piece in pieces).astype(jnp.bfloat16)


def send_sub(pieces):
    keep, away = pieces
    return keep, swap(away, "sub", 1)


def send_heads(pieces, start=0, stop=None):
    keep, got = pieces
    heads_size = lax.axis_size("heads")
    rows = keep.shape[0] // heads_size
    stop = rows if stop is None else stop
    received = []
    for flip in range(1, heads_size):
        part = slice(flip * rows + start, flip * rows + stop)
        both = keep[part] + got[part].astype(jnp.float32)
        received.append(swap(both.astype(jnp.bfloat16), "heads", flip))
    return keep, got, received


def add_shares(pieces, start=0):
    keep, got, received = pieces
    part = slice(start, start + received[0].shape[0])
    total = keep[part] + got[part].astype(jnp.float32)
    return sum((piece.astype(jnp.float32) for piece in received), total).astype(jnp.bfloat16)


def fetch_kernel(
    place, holder, block, serving, store, where, *refs, pool_size, share_count
):
    pieces, (table, rank_of, sems) = refs[:pool_size], refs[pool_size:]
    pool_index, share = place[0], place[1]
    capacity = pieces[0].shape[0]
    blocks_each = holder.shape[1]
    requests_here = where.shape[1] // blocks_each
    spare = pool_size * capacity
    copies = []
    for flip in range(pool_size):
        for slot in range(capacity):
            table[flip * capacity + slot] = 0
        rank = 0
        for i in range(requests_here):
            request = serving[(pool_index ^ flip) * requests_here + i]
            for j in range(blocks_each):
                held = holder[request, j] == pool_index
                table[jnp.where(held, flip * capacity + rank, spare)] = block[request, j]
                rank = rank + held.astype(jnp.int32)
        for slot in range(capacity):
            index = flip * capacity + slot
            source = store.at[table[index] * share_count + share]
            copies.append(pltpu.make_async_copy(source, pieces[flip].at[slot], sems.at[index]))
            copies[-1].start()
    for i in range(pool_size):
        rank_of[i] = 0
    for i in range(requests_here):
        request = serving[pool_index * requests_here + i]
        for j in range(blocks_each):
            held_by = holder[request, j]
            where[0, i * blocks_each + j] = held_by ^ pool_index
            where[1, i * blocks_each + j] = rank_of[held_by]
            rank_of[held_by] = rank_of[held_by] + 1
    for copy in copies:
        copy.wait()


def fetch(place, latent_store, place_holder, place_block, serving_request, items):
    pool_size = lax.axis_size("pool")
    share_count = lax.axis_size(("heads", "sub"))
    capacity = 2 * ((items + pool_size - 1) // pool_size)
    rows = BLK // share_count
    store = latent_store.reshape(-1, rows, latent_store.shape[1])
    piece = jax.ShapeDtypeStruct((capacity, rows, store.shape[2]), store.dtype)
    smem = pl.BlockSpec(memory_space=pltpu.SMEM)
    where, *pieces = pl.pallas_call(
        functools.partial(fetch_kernel, pool_size=pool_size, share_count=share_count),
        in_specs=[smem] * 4 + [pl.BlockSpec(memory_space=pltpu.HBM)],
        out_specs=[smem] + [pl.BlockSpec(memory_space=pltpu.VMEM)] * pool_size,
        out_shape=[jax.ShapeDtypeStruct((2, items), jnp.int32)] + [piece] * pool_size,
        scratch_shapes=[
            pltpu.SMEM((pool_size * capacity + 1,), jnp.int32),
            pltpu.SMEM((pool_size,), jnp.int32),
            pltpu.SemaphoreType.DMA((pool_size * capacity,)),
        ],
        cost_estimate=LIGHT,
    )(place, place_holder, place_block, serving_request, store)
    return where, pieces


def choose_kernel(order, where, *refs):
    pieces, out = refs[:-1], refs[-1]
    for i in range(out.shape[0]):
        flip, slot = where[0, i], where[1, i]
        for other, piece in zip(order, pieces):

            @pl.when(flip == other)
            def _(piece=piece):
                out[i] = piece[slot]


def choose(where, pieces):
    order = [0, *range(2, len(pieces)), 1]
    whole = pl.BlockSpec(memory_space=pltpu.VMEM)
    return pl.pallas_call(
        functools.partial(choose_kernel, order),
        in_specs=[pl.BlockSpec(memory_space=pltpu.SMEM)] + [whole] * len(pieces),
        out_specs=whole,
        out_shape=jax.ShapeDtypeStruct((where.shape[1], *pieces[0].shape[1:]), pieces[0].dtype),
        compiler_params=pltpu.CompilerParams(vmem_limit_bytes=8 * 1024 * 1024),
        cost_estimate=LIGHT,
    )(where, *[pieces[flip] for flip in order])


def attend_kernel(start, rows, share_count, scalars, queries, *refs):
    parts, (kv_up, gains, out, keys, values) = refs[:share_count], refs[share_count:]
    q_gain, k_gain = gains[0:1, :], gains[1:2, :]
    requests, request_shares, _, width = queries.shape
    heads_here = kv_up.shape[0]
    head_width = gains.shape[1]
    text = request_shares * rows
    per_group = width // heads_here // head_width
    part_slots = parts[0].shape[1]
    share_rows = BLK // share_count
    share = scalars[0]
    slot = lax.broadcasted_iota(jnp.int32, (part_slots, head_width), 0)
    position = (slot // share_rows) * BLK + slot % share_rows
    scale = math.log2(math.e) / math.sqrt(head_width)
    together = min(per_group, max(1, 256 // text))
    for request in range(requests):
        count = scalars[1 + request]
        for flip in range(share_count):
            run = pl.ds(flip * part_slots, part_slots)
            live = jnp.where(position < count - (share ^ flip) * share_rows, 1.0, 0.0)
            for group in range(heads_here):
                pair = request * heads_here + group
                projected = jnp.dot(
                    parts[flip][request], kv_up[group], preferred_element_type=jnp.float32
                )
                key = rms_scale(projected[:, :head_width], k_gain)
                keys[pair, run, :] = key.astype(jnp.bfloat16)
                value = projected[:, head_width:] * live
                values[pair, run, :head_width] = value.astype(jnp.bfloat16)
                values[pair, run, head_width:] = live.astype(jnp.bfloat16)
        for group in range(heads_here):
            pair = request * heads_here + group
            for first in range(group * per_group, (group + 1) * per_group, together):
                normed = []
                for head in range(first, first + together):
                    columns = slice(head * head_width, (head + 1) * head_width)
                    query = queries[request, :, start : start + rows, columns]
                    query = query.reshape(text, head_width).astype(jnp.float32)
                    normed.append(rms_scale(query, q_gain).astype(jnp.bfloat16))
                scores = lax.dot_general(
                    jnp.concatenate(normed, axis=0),
                    keys[pair],
                    (((1,), (1,)), ((), ())),
                    preferred_element_type=jnp.float32,
                )
                expo = jnp.exp2(scores * scale).astype(jnp.bfloat16)
                total = jnp.dot(expo, values[pair], preferred_element_type=jnp.float32)
                result = (total[:, :head_width] / total[:, head_width:]).astype(jnp.bfloat16)
                for i in range(together):
                    head = first + i
                    columns = slice(head * head_width, (head + 1) * head_width)
                    out[request * text : (request + 1) * text, columns] = result[
                        i * text : (i + 1) * text
                    ]


def attend(start, rows, queries, parts, kv_flat, gains, scalars):
    requests, request_shares, _, width = queries.shape
    heads_here = kv_flat.shape[0]
    head_width = gains.shape[1]
    slots = len(parts) * parts[0].shape[1]
    whole = pl.BlockSpec(memory_space=pltpu.VMEM)
    return pl.pallas_call(
        functools.partial(attend_kernel, start, rows, len(parts)),
        in_specs=[pl.BlockSpec(memory_space=pltpu.SMEM)] + [whole] * (len(parts) + 3),
        out_specs=whole,
        out_shape=jax.ShapeDtypeStruct((requests * request_shares * rows, width), jnp.bfloat16),
        scratch_shapes=[
            pltpu.VMEM((requests * heads_here, slots, head_width), jnp.bfloat16),
            pltpu.VMEM((requests * heads_here, slots, 2 * head_width), jnp.bfloat16),
        ],
        compiler_params=pltpu.CompilerParams(vmem_limit_bytes=20 * 1024 * 1024),
        cost_estimate=LIGHT,
    )(scalars, queries, *parts, kv_flat, gains)


def per_device(
    queries,
    latent_store,
    kv_up,
    q_gain,
    k_gain,
    out_weight,
    place_holder,
    place_block,
    image_count,
    serving_request,
):
    pool_size = lax.axis_size("pool")
    pool_index = lax.axis_index("pool")
    heads_size = lax.axis_size("heads")
    sub_size = lax.axis_size("sub")
    share_count = heads_size * sub_size
    share = lax.axis_index(("heads", "sub"))
    requests_here, text_rows, _ = queries.shape
    blocks_each = place_holder.shape[1]
    items = requests_here * blocks_each
    rank_width = latent_store.shape[1]
    tie = lax.optimization_barrier
    place = jnp.stack([pool_index, share]).astype(jnp.int32)
    where, pieces = fetch(place, latent_store, place_holder, place_block, serving_request, items)
    kv_flat = jnp.moveaxis(kv_up.reshape(rank_width, kv_up.shape[1], -1), 1, 0)
    gains = jnp.stack([q_gain, k_gain])
    request_ids = jnp.arange(serving_request.shape[0], dtype=jnp.int32)
    served_here = lax.dynamic_slice_in_dim(
        serving_request, pool_index * requests_here, requests_here
    )
    count_here = jnp.sum(
        jnp.where(served_here[:, None] == request_ids[None, :], image_count[None, :], 0), axis=1
    )
    scalars = jnp.concatenate([share.reshape(1), count_here])
    for flip in [*range(2, pool_size), 1]:
        pieces[flip] = swap(pieces[flip], "pool", flip)
    capacity = pieces[0].shape[0]
    pieces[0] = jnp.roll(pieces[0], 1, axis=0)
    local = jnp.where(where[0] == 0, 1, 0)
    where = jnp.stack([where[0], (where[1] + local) % capacity])
    chosen = choose(where, pieces)
    chosen, kv_flat, gains, scalars = tie((chosen, kv_flat, gains, scalars))
    chosen = chosen.reshape(requests_here, -1, rank_width)
    over_heads = [chosen] + [swap(chosen, "heads", flip) for flip in range(1, heads_size)]
    parts = []
    for part in over_heads:
        parts += [part] + [swap(part, "sub", flip) for flip in range(1, sub_size)]
    part_rows = requests_here * text_rows // share_count
    shaped = queries.reshape(requests_here, share_count // requests_here, part_rows, -1)
    few = part_rows // 2
    chunk_rows = part_rows - few, few

    def attended(chunk):
        rows = chunk_rows[chunk]
        start = sum(chunk_rows[:chunk])
        return attend(start, rows, shaped, parts, kv_flat, gains, scalars)

    columns = out_weight.shape[1]
    if pool_size != 4:
        outputs = []
        for chunk in range(len(chunk_rows)):
            rows = lax.all_gather(attended(chunk), "pool", axis=0)
            mine = add_direct(
                send_direct(
                    project_out([rows[i] for i in range(pool_size)], out_weight, direct=True)
                )
            )
            mine = mine.reshape(pool_size, -1, columns)
            back = lax.all_to_all(mine, "pool", split_axis=0, concat_axis=0, tiled=True)
            outputs.append(jnp.moveaxis(back, 0, 1).reshape(-1, pool_size * columns))
        return jnp.concatenate(outputs, axis=0)

    first = attended(0)
    across0, beside0 = swap(first, "pool", 3), swap(first, "pool", 1)
    last = attended(1)
    across1, beside1 = swap(last, "pool", 3), swap(last, "pool", 1)
    own = project_out([first, last], out_weight)
    across0, beside0, own = tie((across0, beside0, own))
    second0 = second_hop(first, across0)
    near0 = send_direct(project_out([beside0, across0], out_weight, direct=True))
    across1, beside1, near0, own = tie((across1, beside1, near0, own))
    second1 = second_hop(last, across1)
    many, few = chunk_rows
    near0 = add_direct(near0)
    back0 = swap(near0[:many], "pool", 1), swap(near0[many:], "pool", 3)
    near1 = send_sub(project_out([beside1, across1], out_weight))
    second0, near1 = tie((second0, near1))
    near1 = send_heads(near1)
    far0 = send_heads(send_sub(project_out([second0], out_weight)))
    far1 = project_out([second1], out_weight)
    back0, near1, far0, far1, own = tie((back0, near1, far0, far1, own))
    near1 = add_shares(near1)
    back1 = swap(near1[:few], "pool", 1), swap(near1[few:], "pool", 3)
    back_second0 = swap(add_shares(far0), "pool", 2)
    far1 = send_heads(send_sub(far1))
    own = send_sub(own)
    own0, own1 = send_heads(own, 0, many), send_heads(own, many, many + few)
    back1, back_second0, far1 = tie((back1, back_second0, far1))
    back_second1 = swap(add_shares(far1), "pool", 2)
    own0, own1 = add_shares(own0), add_shares(own1, many)
    backs = [(0, 1, back0[0]), (0, 3, back0[1]), (many, 1, back1[0]), (many, 3, back1[1])]
    backs += [(0, 2, back_second0), (0, 0, own0), (many, 0, own1), (many, 2, back_second1)]
    output = jnp.zeros((part_rows, pool_size * columns), jnp.bfloat16)
    for row, flip, block in backs:
        output = lax.dynamic_update_slice(output, block, (row, (pool_index ^ flip) * columns))
    return output


def solution(mesh):
    in_specs = (
        P(("groups", "pool"), None, ("heads", "sub")),
        P(("groups", "pool"), None),
        P(None, ("heads", "sub"), None, None),
        P(),
        P(),
        P(("heads", "sub"), "pool"),
        P("groups", None),
        P("groups", None),
        P("groups"),
        P("groups"),
    )
    out_specs = P(("groups", "pool", "heads", "sub"), None)
    return jax.shard_map(
        per_device, mesh=mesh, in_specs=in_specs, out_specs=out_specs, check_vma=False
    )
```
